32 devices in a mesh: gx: 8 (over y, x, core), gy: 4 (over z).
Axes of the slice: x: 2, y: 2, z: 4, core: 2. Of those that a mesh axis runs over, the one named last changes fastest.
Arguments:
- pressure: float32 [128, 24576], P('gx', 'gy'), may hold values from -6 to 6
- previous: float32 [128, 24576], P('gx', 'gy'), may hold values from -6 to 6
- velocity: bfloat16 [128, 24576], P('gx', 'gy'), may hold values from 0.039794922 to 0.19921875
- tucker_core: bfloat16 [3, 384, 12288], P(None, 'gx', 'gy'), may hold values from -6 to 6
- first_factor: bfloat16 [128, 384], P('gx'), may hold values from -0.3125 to 0.3125
- second_factor: bfloat16 [384, 384], P('gy'), may hold values from -0.3125 to 0.3125
- depth_factor: bfloat16 [64, 32], replicated, may hold values from -1 to 1
Outputs:
- image: float32 [128, 24576], P('gx', 'gy')
The draws below stay inside these ranges and needn't reach their ends.
All inputs are finite; a program needn't handle non-finite values.
Results may differ from the reference program's by a relative error of at most 0.00035.
Values may be sent and summed in bfloat16 or wider, within the bound.
No kernel may reach another device: no remote copies, remote signals or barrier semaphores. Data moves between devices by JAX's collectives and lax.ppermute only.
A program may use at most 192 MiB of HBM per device.

```python
import math
import jax
import jax.numpy as jnp
from jax import lax

CX = 16
NZ = 64
R1 = 384
R2 = 384
R3 = 32
STEPS = 3
NX = 128
NY = 384
N_GX = 8


def levels(stream_key, shape, pieces, low, largest):
    gain, own = 1.0, jax.random.fold_in(stream_key, 6)
    for dim, parts in pieces:
        steps = jnp.exp(jax.random.uniform(jax.random.fold_in(own, dim), (parts,), jnp.float32, low / len(pieces), largest / len(pieces)))
        gain = gain * jnp.repeat(steps, shape[dim] // parts).reshape([-1 if axis == dim else 1 for axis in range(len(shape))])
    return gain


def centred(own_key, extent, spread, limit, shards=(), held_as=jnp.bfloat16):
    drawn = jax.random.normal(own_key, extent, jnp.float32) * spread
    if len(shards) > 0:
        drawn = levels(own_key, extent, shards, -0.22, 0.18) * drawn
    return jnp.clip(drawn, min=-limit, max=limit).astype(held_as)


def setup_inputs(seed: int = 0) -> dict:
    keys = jax.random.split(jax.random.key(seed), 8)
    return {
        "pressure": centred(keys[0], (NX, NY * NZ), 1.0, 6.0, ((0, 8), (1, 4)), jnp.float32),
        "previous": centred(keys[1], (NX, NY * NZ), 1.0, 6.0, ((0, 8), (1, 4)), jnp.float32),
        "velocity": jnp.clip(jnp.exp(math.log(0.19921875) - 1.61066415 * jax.random.uniform(keys[2], (NX, NY * NZ), jnp.float32) ** levels(keys[2], (NX, NY * NZ), ((0, 8), (1, 4)), -0.2, 0.2)), 0.039794922, 0.19921875).astype(jnp.bfloat16),
        "tucker_core": centred(keys[3], (STEPS, R1, R2 * R3), 1.0, 6.0, ((1, 8), (2, 4))),
        "first_factor": centred(keys[4], (NX, R1), R1 ** -0.5, 0.3125, ((0, 8),)),
        "second_factor": centred(keys[5], (NY, R2), R2 ** -0.5, 0.3125, ((0, 4),)),
        "depth_factor": centred(keys[6], (NZ, R3), R3 ** -0.5, 1.0),
    }


STENCIL = (-205.0 / 72.0, 8.0 / 5.0, -1.0 / 5.0, 8.0 / 315.0, -1.0 / 560.0)
HIGH = lax.Precision.HIGHEST


def laplace(field):
    padded = jnp.pad(field, 4)
    size_x, size_y, size_z = field.shape
    total = 3.0 * STENCIL[0] * field
    for reach in range(1, 5):
        near = padded[4 + reach:4 + reach + size_x, 4:4 + size_y, 4:4 + size_z] + padded[4 - reach:4 - reach + size_x, 4:4 + size_y, 4:4 + size_z]
        near = near + padded[4:4 + size_x, 4 + reach:4 + reach + size_y, 4:4 + size_z] + padded[4:4 + size_x, 4 - reach:4 - reach + size_y, 4:4 + size_z]
        near = near + padded[4:4 + size_x, 4:4 + size_y, 4 + reach:4 + reach + size_z] + padded[4:4 + size_x, 4:4 + size_y, 4 - reach:4 - reach + size_z]
        total = total + STENCIL[reach] * near
    return total


def source_field(core_step, first_factor, second_factor, depth_factor):
    core_block = core_step.astype(jnp.float32).reshape(R1, R2, R3)
    second = second_factor.astype(jnp.float32)
    depth = depth_factor.astype(jnp.float32)

    def one_block(rows):
        partial_value = jnp.einsum("xa,abc->xbc", rows.astype(jnp.float32), core_block, precision=HIGH)
        mixed = jnp.einsum("xbc,yb->xyc", partial_value, second, precision=HIGH)
        return jnp.einsum("xyc,zc->xyz", mixed, depth, precision=HIGH)

    blocks = lax.map(one_block, first_factor.reshape(N_GX, CX, R1))
    return blocks.reshape(NX, NY, NZ)


def reference(pressure, previous, velocity, tucker_core, first_factor, second_factor, depth_factor):
    current = pressure.reshape(NX, NY, NZ)
    before = previous.reshape(NX, NY, NZ)
    speed = velocity.astype(jnp.float32).reshape(NX, NY, NZ)
    image = jnp.zeros((NX, NY, NZ), jnp.float32)
    for section in range(STEPS):
        following = 2.0 * current - before + speed * laplace(current)
        image = image + source_field(tucker_core[section], first_factor, second_factor, depth_factor) * following
        before = current
        current = following
    return image.reshape(NX, NY * NZ)
```

```python
import functools

import jax
import jax.numpy as jnp
from jax import lax
from jax.experimental import pallas as pl
from jax.experimental.pallas import tpu as pltpu
from jax.sharding import PartitionSpec as P

STENCIL = (-205.0 / 72.0, 8.0 / 5.0, -1.0 / 5.0, 8.0 / 315.0, -1.0 / 560.0)
F32 = jnp.float32
BF16 = jnp.bfloat16
LANES = 128
TOP = 2.0**7.75
VMEM_BYTES = 48 * 1024 * 1024


def encode(values):
    peak = jnp.max(jnp.abs(values), axis=1, keepdims=True)
    scale = (jnp.maximum(peak, 1e-30) * (1.0 + 2.0**-7)).astype(BF16).astype(F32)
    ratio = values * (TOP / scale)
    power = ratio * ratio
    power = power * power
    power = power * power
    power = power * power
    return jnp.where(ratio < 0.0, -power, power).astype(BF16), scale


def decode(codes, unit):
    codes = codes.astype(F32)
    size = jnp.maximum(jnp.abs(codes), 2.0**-126)
    for _ in range(4):
        size = lax.rsqrt(size)
    size = size * unit
    return jnp.where(codes < 0.0, -size, jnp.where(codes > 0.0, size, 0.0))


def put_codes(ref, row, values, flat):
    rows = values.shape[0]
    codes, scale = encode(values)
    ref[row : row + rows, :flat] = codes
    ref[row : row + rows, flat : flat + LANES] = jnp.broadcast_to(scale, (rows, LANES)).astype(BF16)


def units(ref, row, rows, lane):
    return ref[row : row + rows, lane : lane + LANES].astype(F32) * (1.0 / TOP)


def split(values):
    upper = values.astype(BF16)
    return upper, (values - upper.astype(F32)).astype(BF16)


def dot(left, right):
    return jnp.dot(left, right, preferred_element_type=F32)


def swap_groups(tiles, depth):
    group = lax.broadcasted_iota(jnp.int32, (1, LANES), 1) // depth
    low_half, even = group < 2, group % 2 == 0

    def exchange(left, right, distance, keep):
        return (
            jnp.where(keep, left, pltpu.roll(right, distance, 1)),
            jnp.where(keep, pltpu.roll(left, LANES - distance, 1), right),
        )

    first, third = exchange(tiles[0], tiles[2], 2 * depth, low_half)
    second, fourth = exchange(tiles[1], tiles[3], 2 * depth, low_half)
    first, second = exchange(first, second, depth, even)
    third, fourth = exchange(third, fourth, depth, even)
    return first, second, third, fourth


def pieces(rows):
    return [(start, 16) for start in range(0, rows, 16)] if rows % 16 == 0 else [(0, rows)]


def project_kernel(chips, parts, core, other, *rest):
    factors, outs, (partial,) = rest[:chips], rest[chips:-1], rest[-1:]
    steps, rank, flat = core.shape
    lines = partial.shape[1]
    cells = lines // steps
    place = lax.axis_index("gx")
    factor = jnp.concatenate([ref[...] for ref in factors], axis=0)
    offset = lax.broadcasted_iota(jnp.int32, (factor.shape[1], rank), 0) - lax.broadcasted_iota(
        jnp.int32, (factor.shape[1], rank), 1
    )
    own_rows, other_rows = [
        dot(factor, jnp.where(offset == owner * rank, 1.0, 0.0).astype(BF16)).astype(BF16)
        for owner in (place, place + 1 - 2 * (place % 2))
    ]
    share = flat // parts
    width = 512 if share % 512 == 0 else 256
    for part in range(parts):
        mine, sends = outs[part * chips], outs[part * chips + 1 : (part + 1) * chips]
        for step in range(steps):
            for low in range(0, share, width):
                lanes = slice(part * share + low, part * share + low + width)
                value = dot(own_rows, core[step, :, lanes]) + dot(other_rows, other[step, :, lanes])
                mine[step * cells : (step + 1) * cells, low : low + width] = value[:cells]
                for distance in range(1, chips):
                    partial[distance - 1, step * cells : (step + 1) * cells, low : low + width] = value[
                        distance * cells : (distance + 1) * cells
                    ]
        for distance in range(1, chips):
            for start, count in pieces(lines):
                put_codes(sends[distance - 1], start, partial[distance - 1, start : start + count, :], share)


def gather_kernel(depth, steps, mine, *rest):
    received, (codes, spread, turned) = rest[:-3], rest[-3:]
    lines, flat = mine.shape
    cells = lines // steps
    quads = LANES // depth
    groups = flat // LANES
    pad = spread.shape[0] // lines
    for start, count in pieces(lines):
        scales = [units(ref, start, count, flat) for ref in received]
        for group in range(groups):
            lanes = slice(group * LANES, (group + 1) * LANES)
            value = mine[start : start + count, lanes]
            for ref, unit in zip(received, scales):
                value = value + decode(ref[start : start + count, lanes], unit)
            for row in range(0, count, 8):
                spread[pl.ds((start + row) * pad + group, 8, stride=pad), :] = value[row : row + 8]
    rest_x = cells // quads
    for line in range(steps * rest_x):
        base = line // rest_x * cells + line % rest_x
        for top in range(0, groups, 8):
            count = min(8, groups - top)
            tiles = [
                spread[(base + i * rest_x) * pad + top : (base + i * rest_x) * pad + top + 8, :] for i in range(quads)
            ]
            for j, tile in enumerate(swap_groups(tiles, depth)):
                turned[j * groups + top : j * groups + top + count, line * LANES : (line + 1) * LANES] = tile[:count]
    for start, count in pieces(turned.shape[0]):
        put_codes(codes, start, turned[start : start + count, :], turned.shape[1])


def contract_second(part, parts, depth, second, blocks, upper, lower, total, earlier):
    count_y, rows, flat = upper.shape
    quads = LANES // depth
    ranks = second.shape[1]
    place = lax.axis_index("gy")
    width = 512 if flat % 512 == 0 else 256
    for distance, block in enumerate(blocks):
        owner = jnp.bitwise_xor(place, distance)
        for start, count in pieces(rows):
            unit = units(block, start, count, flat)
            for low in range(0, flat, LANES):
                high, rest_of = split(decode(block[start : start + count, low : low + LANES], unit))
                upper[owner, start : start + count, low : low + LANES] = high
                lower[owner, start : start + count, low : low + LANES] = rest_of
    shape = (ranks, count_y * rows)
    column = lax.broadcasted_iota(jnp.int32, shape, 1)
    inside = column % rows
    groups = rows // quads
    rank = column // rows * (rows * parts) + part * rows + inside % groups * quads + inside // groups
    chosen = jnp.where(lax.broadcasted_iota(jnp.int32, shape, 0) == rank, 1.0, 0.0).astype(BF16)
    columns = dot(second[...], chosen).astype(BF16)
    together = count_y if rows % 16 == 0 else 1
    for low in range(0, flat, width):
        value = None if earlier is None else earlier[:, low : low + width]
        for first in range(0, count_y, together):
            left = columns[:, first * rows : (first + together) * rows]
            for ref in (upper, lower):
                right = ref[first : first + together, :, low : low + width].reshape(together * rows, width)
                value = dot(left, right) if value is None else value + dot(left, right)
        total[:, low : low + width] = value


def early_kernel(part, parts, depth, second, *rest):
    blocks, (total, upper, lower) = rest[:-3], rest[-3:]
    contract_second(part, parts, depth, second, blocks, upper, lower, total, None)


def image_kernel(part, parts, depth, steps, second, depth_factor, waves, *rest):
    rest, (image, upper, lower, mixed, spread) = rest[:-5], rest[-5:]
    earlier, blocks = (rest[0], rest[1:]) if part > 0 else (None, rest)
    contract_second(part, parts, depth, second, blocks, upper, lower, mixed, earlier)
    flat = mixed.shape[1]
    cells = image.shape[0]
    levels = depth_factor.shape[0]
    quads = LANES // depth
    groups = flat // LANES
    pad = spread.shape[0] // mixed.shape[0]
    for row in range(0, mixed.shape[0], 8):
        for group in range(groups):
            spread[pl.ds(row * pad + group, 8, stride=pad), :] = mixed[
                row : row + 8, group * LANES : (group + 1) * LANES
            ]
    square = jnp.concatenate([depth_factor[...].astype(F32)] * quads, axis=1)
    square = jnp.concatenate([square] * quads, axis=0)
    shape = square.shape
    same = lax.broadcasted_iota(jnp.int32, shape, 0) // levels == lax.broadcasted_iota(jnp.int32, shape, 1) // depth
    square = jnp.where(same, square, 0.0).astype(BF16)
    tiles = quads * levels // LANES
    contract = (((1,), (1,)), ((), ()))
    rest_x = cells // quads
    for quad in range(mixed.shape[0] // quads):
        turned = [
            swap_groups(
                [spread[(quad * quads + j) * pad + top : (quad * quads + j) * pad + top + 8, :] for j in range(quads)],
                depth,
            )
            for top in range(0, pad, 8)
        ]
        high, rest_of = split(jnp.concatenate([piece[i] for i in range(quads) for piece in turned], axis=0))
        source = lax.dot_general(high, square, contract, preferred_element_type=F32) + lax.dot_general(
            rest_of, square, contract, preferred_element_type=F32
        )
        for tile in range(tiles):
            at = quad * tiles + tile
            total = None
            for step in range(steps):
                value = jnp.concatenate(
                    [
                        source[i * pad + step * rest_x : i * pad + (step + 1) * rest_x, tile * LANES : (tile + 1) * LANES]
                        for i in range(quads)
                    ],
                    axis=0,
                )
                value = value * waves[at, step * cells : (step + 1) * cells, :]
                total = value if total is None else total + value
            image[:, at * LANES : (at + 1) * LANES] = total


def pack_kernel(pressure, previous, velocity, own, up, down):
    cells, flat = pressure.shape
    span = up.shape[1] - LANES
    put_codes(own, 0, pressure[...], flat)
    put_codes(own, cells, previous[...], flat)
    own[2 * cells :, :flat] = velocity[...]
    own[2 * cells :, flat:] = jnp.zeros((cells, LANES), BF16)
    up[:, :span] = own[:, flat - span : flat]
    down[:, :span] = own[:, :span]
    up[:, span:] = own[:, flat:]
    down[:, span:] = own[:, flat:]


def edge_kernel(own, low, high, ahead, behind):
    flat = own.shape[1] - LANES
    span = low.shape[1] - LANES
    near = span * 2 // 3
    cells = own.shape[0] // 3
    half = cells // 2
    scales = 2 * near + flat
    spans = [
        (low, slice(span - near, span), slice(0, near)),
        (own, slice(0, flat), slice(near, near + flat)),
        (high, slice(0, near), slice(near + flat, scales)),
        (low, slice(span, span + LANES), slice(scales, scales + LANES)),
        (own, slice(flat, flat + LANES), slice(scales + LANES, scales + 2 * LANES)),
        (high, slice(span, span + LANES), slice(scales + 2 * LANES, scales + 3 * LANES)),
    ]
    for ref, rows in ((ahead, slice(half, cells)), (behind, slice(0, half))):
        for part, lanes, into in spans:
            ref[:cells, into] = part[:cells, lanes]
            prior = part[cells : 2 * cells, lanes].astype(F32)[rows]
            speed = part[2 * cells :, lanes].astype(F32)[rows]
            ref[cells:, into] = jnp.concatenate([prior, speed], axis=0).astype(BF16)


def wave_kernel(levels, pressure, previous, velocity, left, right, low, high, waves, first, second, third, prior, speed):
    cells, flat = pressure.shape
    half = cells // 2
    span = low.shape[1] - LANES
    near = span * 2 // 3
    steps = waves.shape[1] // cells
    edge, inner, own_tiles = span // LANES, near // LANES, flat // LANES

    for tile in range(own_tiles):
        lane = tile * LANES
        first[edge + tile, cells : 2 * cells, :] = pressure[:, lane : lane + LANES]
        prior[inner + tile, half : half + cells, :] = previous[:, lane : lane + LANES]
        speed[inner + tile, half : half + cells, :] = velocity[:, lane : lane + LANES].astype(F32)
    wide = own_tiles + 2 * inner
    for part, top, side in ((left, 0, 0), (right, 2 * cells, half + cells)):
        scales = [units(part, 0, 2 * cells, (wide + k) * LANES) for k in range(3)]
        for tile in range(wide):
            lanes = slice(tile * LANES, (tile + 1) * LANES)
            unit = scales[0 if tile < inner else 1 if tile < inner + own_tiles else 2]
            first[edge - inner + tile, top : top + cells, :] = decode(part[:cells, lanes], unit[:cells])
            both = part[cells:, lanes].astype(F32)
            prior[tile, side : side + half, :] = decode(both[:half], unit[cells : cells + half])
            speed[tile, side : side + half, :] = both[half:]
        for tile in list(range(edge - inner)) + list(range(edge + own_tiles + inner, 2 * edge + own_tiles)):
            first[tile, top : top + cells, :] = jnp.zeros((cells, LANES), F32)
    for part, start, cut, begin in ((low, 0, edge - inner, 0), (high, edge + own_tiles, 0, inner + own_tiles)):
        unit = units(part, 0, 3 * cells, span)
        for tile in range(edge):
            lanes = slice(tile * LANES, (tile + 1) * LANES)
            first[start + tile, cells : 2 * cells, :] = decode(part[:cells, lanes], unit[:cells])
            if cut <= tile < cut + inner:
                prior[begin + tile - cut, half : half + cells, :] = decode(
                    part[cells : 2 * cells, lanes], unit[cells : 2 * cells]
                )
                speed[begin + tile - cut, half : half + cells, :] = part[2 * cells :, lanes].astype(F32)

    line = lax.broadcasted_iota(jnp.int32, (LANES, LANES), 0)
    column = lax.broadcasted_iota(jnp.int32, (LANES, LANES), 1)
    gap = jnp.abs(line - column)
    band = jnp.zeros((LANES, LANES), F32)
    for reach in range(5):
        band = jnp.where(gap == reach, STENCIL[reach] * (3.0 if reach == 0 else 1.0), band)
    band = jnp.where(line // levels == column // levels, band, 0.0)
    band_upper, band_lower = split(band)
    bands = jnp.concatenate([band_upper, band_upper, band_lower], axis=0)
    front = lax.broadcasted_iota(jnp.int32, (1, LANES), 1) < levels
    count = 4

    def advance(now, before, shift, tile_shift, later, out_row, top, rows, tile):
        tiles = [now[tile + step, top : top + rows, :] for step in range(-2, count + 2)]
        rolled = [pltpu.roll(value, levels, 1) for value in tiles]
        tall = jnp.concatenate(tiles[2 : 2 + count], axis=0)
        upper, lower = split(tall)
        deep = dot(jnp.concatenate([upper, lower, upper], axis=1), bands)
        for step in range(count):
            at = step + 2
            total = deep[step * rows : (step + 1) * rows]
            sides = [
                jnp.where(front, rolled[at] + rolled[at - 1], rolled[at + 1] + rolled[at]),
                tiles[at + 1] + tiles[at - 1],
                jnp.where(front, rolled[at + 1] + rolled[at - 2], rolled[at + 2] + rolled[at - 1]),
                tiles[at + 2] + tiles[at - 2],
            ]
            for reach in range(1, 5):
                value = sides[reach - 1] + now[tile + step, top + reach : top + reach + rows, :]
                value = value + now[tile + step, top - reach : top - reach + rows, :]
                total = total + STENCIL[reach] * value
            rate = speed[tile + step - (edge - inner), top - half : top - half + rows, :]
            past = before[tile + step - tile_shift, top - shift : top - shift + rows, :]
            following = 2.0 * tiles[at] - past + rate * total
            if later is None:
                waves[tile + step - edge, out_row : out_row + rows, :] = following
            else:
                later[tile + step, top : top + rows, :] = following

    chain = [(first, prior, half, edge - inner, second), (second, first, 0, 0, third), (third, second, 0, 0, None)]
    for step in range(steps):
        now, before, shift, tile_shift, later = chain[step]
        margin = (steps - 1 - step) * (edge // steps)
        tops = (cells - half, 2 * cells - half) if later is not None else (cells,)

        def loop(block, carry):
            for top in tops:
                advance(now, before, shift, tile_shift, later, step * cells, top, cells, edge - margin + count * block)
            return carry

        lax.fori_loop(0, (own_tiles + 2 * margin) // count, loop, 0)
        if later is not None:
            for tile in range(own_tiles):
                waves[tile, step * cells : (step + 1) * cells, :] = later[edge + tile, cells : 2 * cells, :]


def call(kernel, outs, scratch, flops, *args):
    moved = sum(arg.size * arg.dtype.itemsize for arg in args)
    moved += sum(out.size * jnp.dtype(out.dtype).itemsize for out in outs)
    return pl.pallas_call(
        kernel,
        out_shape=outs,
        scratch_shapes=scratch,
        cost_estimate=pl.CostEstimate(flops=flops, bytes_accessed=moved, transcendentals=0),
        compiler_params=pltpu.CompilerParams(vmem_limit_bytes=VMEM_BYTES),
    )(*args)


def shape_of(*shape, dtype=F32):
    return jax.ShapeDtypeStruct(shape, dtype)


def body(pressure, previous, velocity, tucker_core, first_factor, second_factor, depth_factor):
    cells, flat = pressure.shape
    levels, depth = depth_factor.shape
    steps, rank, core_flat = tucker_core.shape
    local_second = core_flat // depth
    lines = steps * cells
    count_x, count_y = lax.axis_size("gx"), lax.axis_size("gy")
    chips = count_x // 2
    span = 4 * steps * levels
    near = span * 2 // 3
    parts = 2 if local_second % 32 == 0 else 1
    rows = local_second // parts
    share = core_flat // parts
    groups_pad = (share // LANES + 7) // 8 * 8
    lines_pad = (lines * depth // LANES + 7) // 8 * 8

    across = [[(i, 2 * ((i // 2) ^ distance) + i % 2) for i in range(count_x)] for distance in range(1, chips)]
    factors = [first_factor] + [lax.ppermute(first_factor, "gx", route) for route in across]
    other = lax.ppermute(tucker_core, "gx", [(i, i + 1 - 2 * (i % 2)) for i in range(count_x)])

    outs = call(
        functools.partial(project_kernel, chips, parts),
        ([shape_of(lines, share)] + [shape_of(lines, share + LANES, dtype=BF16)] * (chips - 1)) * parts,
        [pltpu.VMEM((chips - 1, lines, share), F32)],
        4 * lines * chips * rank * core_flat,
        tucker_core,
        other,
        *factors,
    )
    outs = [outs[part * chips : (part + 1) * chips] for part in range(parts)]
    received = [[lax.ppermute(send, "gx", route) for send, route in zip(outs[0][1:], across)]]

    pressure_later, _ = lax.optimization_barrier((pressure, outs[0][0]))
    own, up, down = call(
        pack_kernel,
        [shape_of(3 * cells, flat + LANES, dtype=BF16)] + [shape_of(3 * cells, span + LANES, dtype=BF16)] * 2,
        [],
        10 * cells * flat,
        pressure_later,
        previous,
        velocity,
    )
    low = lax.ppermute(up, "gy", [(i, i + 1) for i in range(count_y - 1)])
    high = lax.ppermute(down, "gy", [(i + 1, i) for i in range(count_y - 1)])
    mixed, blocks = [], []
    for part in range(parts):
        if part + 1 < parts:
            received[part], sends = lax.optimization_barrier((received[part], outs[part + 1][1:]))
            received.append([lax.ppermute(send, "gx", route) for send, route in zip(sends, across)])
        if part > 0:
            received[part], blocks[1:3] = lax.optimization_barrier((received[part], blocks[1:3]))
            mixed = call(
                functools.partial(early_kernel, part - 1, parts, depth),
                [shape_of(second_factor.shape[0], lines * depth)],
                [pltpu.VMEM((count_y, rows, lines * depth), BF16)] * 2,
                4 * second_factor.shape[0] * count_y * rows * lines * depth,
                second_factor,
                *blocks,
            )
        (codes,) = call(
            functools.partial(gather_kernel, depth, steps),
            [shape_of(rows, lines * depth + LANES, dtype=BF16)],
            [pltpu.VMEM((lines * groups_pad, LANES), F32), pltpu.VMEM((rows, lines * depth), F32)],
            30 * chips * lines * share,
            outs[part][0],
            *received[part],
        )
        if part == 0:
            codes, low, high = lax.optimization_barrier((codes, low, high))
            ahead, behind = call(
                edge_kernel,
                [shape_of(2 * cells, flat + 2 * near + 3 * LANES, dtype=BF16)] * 2,
                [],
                1000,
                own,
                low,
                high,
            )
        if part == parts - 1:
            codes, ahead, behind = lax.optimization_barrier((codes, ahead, behind))
        blocks = [codes] + [
            lax.ppermute(codes, "gy", [(i, i ^ distance) for i in range(count_y)]) for distance in range(1, count_y)
        ]

    left = lax.ppermute(ahead, "gx", [(i, i + 1) for i in range(count_x - 1)])
    right = lax.ppermute(behind, "gx", [(i + 1, i) for i in range(count_x - 1)])
    (waves,) = call(
        functools.partial(wave_kernel, levels),
        [shape_of(flat // LANES, lines, LANES)],
        [pltpu.VMEM(((flat + 2 * span) // LANES, 3 * cells, LANES), F32)] * 3
        + [pltpu.VMEM(((flat + 2 * near) // LANES, 2 * cells, LANES), F32)] * 2,
        150 * lines * flat,
        pressure,
        previous,
        velocity,
        left,
        right,
        low,
        high,
    )
    cells_y = second_factor.shape[0]
    (image,) = call(
        functools.partial(image_kernel, parts - 1, parts, depth, steps),
        [shape_of(cells, flat)],
        [pltpu.VMEM((count_y, rows, lines * depth), BF16)] * 2
        + [pltpu.VMEM((cells_y, lines * depth), F32), pltpu.VMEM((cells_y * lines_pad, LANES), F32)],
        4 * cells_y * count_y * rows * lines * depth,
        second_factor,
        depth_factor,
        waves,
        *mixed,
        *blocks,
    )
    return image


def solution(mesh):
    placed = (
        P("gx", "gy"),
        P("gx", "gy"),
        P("gx", "gy"),
        P(None, "gx", "gy"),
        P("gx", None),
        P("gy", None),
        P(),
    )
    return jax.shard_map(body, mesh=mesh, in_specs=placed, out_specs=P("gx", "gy"), check_vma=False)
```

```python
import functools

import jax
import jax.numpy as jnp
from jax import lax
from jax.experimental import pallas as pl
from jax.experimental.pallas import tpu as pltpu
from jax.sharding import PartitionSpec as P

STENCIL = (-205.0 / 72.0, 8.0 / 5.0, -1.0 / 5.0, 8.0 / 315.0, -1.0 / 560.0)
F32 = jnp.float32
BF16 = jnp.bfloat16
LANES = 128
TOP = 2.0**7.75
VMEM_BYTES = 48 * 1024 * 1024


def encode(values):
    peak = jnp.max(jnp.abs(values), axis=1, keepdims=True)
    scale = (jnp.maximum(peak, 1e-30) * (1.0 + 2.0**-7)).astype(BF16).astype(F32)
    ratio = values * (TOP / scale)
    power = ratio * ratio
    power = power * power
    power = power * power
    power = power * power
    return jnp.where(ratio < 0.0, -power, power).astype(BF16), scale


def decode(codes, unit):
    codes = codes.astype(F32)
    size = jnp.maximum(jnp.abs(codes), 2.0**-126)
    for _ in range(4):
        size = lax.rsqrt(size)
    size = size * unit
    return jnp.where(codes < 0.0, -size, jnp.where(codes > 0.0, size, 0.0))


def put_codes(ref, row, values, flat):
    rows = values.shape[0]
    codes, scale = encode(values)
    ref[row : row + rows, :flat] = codes
    ref[row : row + rows, flat : flat + LANES] = jnp.broadcast_to(scale, (rows, LANES)).astype(BF16)


def units(ref, row, rows, lane):
    return ref[row : row + rows, lane : lane + LANES].astype(F32) * (1.0 / TOP)


def split(values):
    upper = values.astype(BF16)
    return upper, (values - upper.astype(F32)).astype(BF16)


def dot(left, right):
    return jnp.dot(left, right, preferred_element_type=F32)


def swap_groups(tiles, depth):
    group = lax.broadcasted_iota(jnp.int32, (1, LANES), 1) // depth
    low_half, even = group < 2, group % 2 == 0

    def exchange(left, right, distance, keep):
        return (
            jnp.where(keep, left, pltpu.roll(right, distance, 1)),
            jnp.where(keep, pltpu.roll(left, LANES - distance, 1), right),
        )

    first, third = exchange(tiles[0], tiles[2], 2 * depth, low_half)
    second, fourth = exchange(tiles[1], tiles[3], 2 * depth, low_half)
    first, second = exchange(first, second, depth, even)
    third, fourth = exchange(third, fourth, depth, even)
    return first, second, third, fourth


def pieces(rows):
    return [(start, 16) for start in range(0, rows, 16)] if rows % 16 == 0 else [(0, rows)]


def project_kernel(chips, core, other, *rest):
    factors, mine, sends, (partial,) = rest[:chips], rest[chips], rest[chips + 1 : -1], rest[-1:]
    steps, rank, flat = core.shape
    lines = mine.shape[0]
    cells = lines // steps
    place = lax.axis_index("gx")
    factor = jnp.concatenate([ref[...] for ref in factors], axis=0)
    offset = lax.broadcasted_iota(jnp.int32, (factor.shape[1], rank), 0) - lax.broadcasted_iota(
        jnp.int32, (factor.shape[1], rank), 1
    )
    own_rows, other_rows = [
        dot(factor, jnp.where(offset == owner * rank, 1.0, 0.0).astype(BF16)).astype(BF16)
        for owner in (place, place + 1 - 2 * (place % 2))
    ]
    width = 512 if flat % 512 == 0 else 256
    for step in range(steps):
        for low in range(0, flat, width):
            lanes = slice(low, low + width)
            value = dot(own_rows, core[step, :, lanes]) + dot(other_rows, other[step, :, lanes])
            mine[step * cells : (step + 1) * cells, lanes] = value[:cells]
            for distance in range(1, chips):
                partial[distance - 1, step * cells : (step + 1) * cells, lanes] = value[
                    distance * cells : (distance + 1) * cells
                ]
    for distance in range(1, chips):
        for start, count in pieces(lines):
            put_codes(sends[distance - 1], start, partial[distance - 1, start : start + count, :], flat)


def gather_kernel(depth, steps, mine, *rest):
    received, (codes, spread, turned) = rest[:-3], rest[-3:]
    lines, flat = mine.shape
    cells = lines // steps
    quads = LANES // depth
    groups = flat // LANES
    pad = spread.shape[0] // lines
    for start, count in pieces(lines):
        scales = [units(ref, start, count, flat) for ref in received]
        for group in range(groups):
            lanes = slice(group * LANES, (group + 1) * LANES)
            value = mine[start : start + count, lanes]
            for ref, unit in zip(received, scales):
                value = value + decode(ref[start : start + count, lanes], unit)
            for row in range(0, count, 8):
                spread[pl.ds((start + row) * pad + group, 8, stride=pad), :] = value[row : row + 8]
    rest_x = cells // quads
    for line in range(steps * rest_x):
        base = line // rest_x * cells + line % rest_x
        for top in range(0, groups, 8):
            count = min(8, groups - top)
            tiles = [
                spread[(base + i * rest_x) * pad + top : (base + i * rest_x) * pad + top + 8, :] for i in range(quads)
            ]
            for j, tile in enumerate(swap_groups(tiles, depth)):
                turned[j * groups + top : j * groups + top + count, line * LANES : (line + 1) * LANES] = tile[:count]
    for start, count in pieces(turned.shape[0]):
        put_codes(codes, start, turned[start : start + count, :], turned.shape[1])


def contract_second(depth, second, blocks, total, earlier, terms):
    rows, flat = blocks[0][1].shape[0], total.shape[1]
    quads = LANES // depth
    ranks = second.shape[1]
    place = lax.axis_index("gy")
    inner = (place == 1) | (place == 2)
    width = 512 if flat % 512 == 0 else 256
    columns = []
    inside = lax.broadcasted_iota(jnp.int32, (ranks, rows), 1)
    inside = inside % (rows // quads) * quads + inside // (rows // quads)
    offset = lax.broadcasted_iota(jnp.int32, (ranks, rows), 0) - inside
    for at, (distance, *options) in enumerate(blocks):
        owner = jnp.bitwise_xor(place, distance)
        chosen = jnp.where(offset == owner * rows, 1.0, 0.0).astype(BF16)
        columns.append(dot(second[...], chosen).astype(BF16))
        for start, count in pieces(rows):
            unit = units(options[0], start, count, flat)
            if len(options) > 1:
                unit = jnp.where(inner, unit, units(options[1], start, count, flat))
            for low in range(0, flat, LANES):
                codes = options[0][start : start + count, low : low + LANES].astype(F32)
                if len(options) > 1:
                    codes = jnp.where(
                        inner, codes, options[1][start : start + count, low : low + LANES].astype(F32)
                    )
                high, rest_of = split(decode(codes, unit))
                terms[2 * at, start : start + count, low : low + LANES] = high
                terms[2 * at + 1, start : start + count, low : low + LANES] = rest_of
    together = len(blocks) if rows % 16 == 0 else 1
    for low in range(0, flat, width):
        value = None if earlier is None else earlier[:, low : low + width]
        for at in range(0, len(blocks), together):
            left = jnp.concatenate([columns[k // 2] for k in range(2 * at, 2 * (at + together))], axis=1)
            right = [terms[k, :, low : low + width] for k in range(2 * at, 2 * (at + together))]
            if rows % 16 == 0:
                products = [dot(left, jnp.concatenate(right, axis=0))]
            else:
                products = [dot(columns[at], part) for part in right]
            for product in products:
                value = product if value is None else value + product
        total[:, low : low + width] = value


def early_kernel(depth, distances, second, *rest):
    blocks, (total, terms) = rest[:-2], rest[-2:]
    contract_second(depth, second, list(zip(distances, blocks)), total, None, terms)


def image_kernel(depth, steps, distance, second, depth_factor, waves, earlier, *rest):
    blocks, (image, terms, mixed, spread) = rest[:-4], rest[-4:]
    contract_second(depth, second, [(distance, *blocks)], mixed, earlier, terms)
    flat = mixed.shape[1]
    cells = image.shape[0]
    levels = depth_factor.shape[0]
    quads = LANES // depth
    groups = flat // LANES
    pad = spread.shape[0] // mixed.shape[0]
    for row in range(0, mixed.shape[0], 8):
        for group in range(groups):
            spread[pl.ds(row * pad + group, 8, stride=pad), :] = mixed[
                row : row + 8, group * LANES : (group + 1) * LANES
            ]
    square = jnp.concatenate([depth_factor[...].astype(F32)] * quads, axis=1)
    square = jnp.concatenate([square] * quads, axis=0)
    shape = square.shape
    same = lax.broadcasted_iota(jnp.int32, shape, 0) // levels == lax.broadcasted_iota(jnp.int32, shape, 1) // depth
    square = jnp.where(same, square, 0.0).astype(BF16)
    square = jnp.concatenate([square, square], axis=1)
    tiles = quads * levels // LANES
    contract = (((1,), (1,)), ((), ()))
    rest_x = cells // quads
    many = mixed.shape[0] // quads
    batch = 4 if many % 4 == 0 else 1
    for first in range(0, many, batch):
        stack = []
        for quad in range(first, first + batch):
            turned = [
                swap_groups(
                    [
                        spread[(quad * quads + j) * pad + top : (quad * quads + j) * pad + top + 8, :]
                        for j in range(quads)
                    ],
                    depth,
                )
                for top in range(0, pad, 8)
            ]
            stack += [piece[i] for i in range(quads) for piece in turned]
        high, rest_of = split(jnp.concatenate(stack, axis=0))
        source = lax.dot_general(
            jnp.concatenate([high, rest_of], axis=1), square, contract, preferred_element_type=F32
        )
        for quad in range(first, first + batch):
            base = (quad - first) * quads * pad
            for tile in range(tiles):
                at = quad * tiles + tile
                lanes = slice(tile * LANES, (tile + 1) * LANES)
                total = None
                for step in range(steps):
                    value = jnp.concatenate(
                        [
                            source[base + i * pad + step * rest_x : base + i * pad + (step + 1) * rest_x, lanes]
                            for i in range(quads)
                        ],
                        axis=0,
                    )
                    value = value * waves[at, step * cells : (step + 1) * cells, :]
                    total = value if total is None else total + value
                image[:, at * LANES : (at + 1) * LANES] = total


def lift_kernel(core, factor, core_near, factor_near):
    core_near[...] = core[...]
    factor_near[...] = factor[...]


def pack_kernel(pressure, previous, velocity, own, up, down):
    cells, flat = pressure.shape
    span = up.shape[1] - LANES
    put_codes(own, 0, pressure[...], flat)
    put_codes(own, cells, previous[...], flat)
    own[2 * cells :, :flat] = velocity[...]
    own[2 * cells :, flat:] = jnp.zeros((cells, LANES), BF16)
    up[:, :span] = own[:, flat - span : flat]
    down[:, :span] = own[:, :span]
    up[:, span:] = own[:, flat:]
    down[:, span:] = own[:, flat:]


def edge_kernel(own, low, high, ahead, behind):
    flat = own.shape[1] - LANES
    span = low.shape[1] - LANES
    near = span * 2 // 3
    cells = own.shape[0] // 3
    half = cells // 2
    scales = 2 * near + flat
    spans = [
        (low, slice(span - near, span), slice(0, near)),
        (own, slice(0, flat), slice(near, near + flat)),
        (high, slice(0, near), slice(near + flat, scales)),
        (low, slice(span, span + LANES), slice(scales, scales + LANES)),
        (own, slice(flat, flat + LANES), slice(scales + LANES, scales + 2 * LANES)),
        (high, slice(span, span + LANES), slice(scales + 2 * LANES, scales + 3 * LANES)),
    ]
    for ref, rows in ((ahead, slice(half, cells)), (behind, slice(0, half))):
        for part, lanes, into in spans:
            ref[:cells, into] = part[:cells, lanes]
            prior = part[cells : 2 * cells, lanes].astype(F32)[rows]
            speed = part[2 * cells :, lanes].astype(F32)[rows]
            ref[cells:, into] = jnp.concatenate([prior, speed], axis=0).astype(BF16)


def wave_kernel(levels, pressure, previous, velocity, left, right, low, high, waves, first, second, third, prior, speed):
    cells, flat = pressure.shape
    half = cells // 2
    span = low.shape[1] - LANES
    near = span * 2 // 3
    steps = waves.shape[1] // cells
    edge, inner, own_tiles = span // LANES, near // LANES, flat // LANES

    for tile in range(own_tiles):
        lane = tile * LANES
        first[edge + tile, cells : 2 * cells, :] = pressure[:, lane : lane + LANES]
        prior[inner + tile, half : half + cells, :] = previous[:, lane : lane + LANES]
        speed[inner + tile, half : half + cells, :] = velocity[:, lane : lane + LANES].astype(F32)
    wide = own_tiles + 2 * inner
    for part, top, side in ((left, 0, 0), (right, 2 * cells, half + cells)):
        scales = [units(part, 0, 2 * cells, (wide + k) * LANES) for k in range(3)]
        for tile in range(wide):
            lanes = slice(tile * LANES, (tile + 1) * LANES)
            unit = scales[0 if tile < inner else 1 if tile < inner + own_tiles else 2]
            first[edge - inner + tile, top : top + cells, :] = decode(part[:cells, lanes], unit[:cells])
            both = part[cells:, lanes].astype(F32)
            prior[tile, side : side + half, :] = decode(both[:half], unit[cells : cells + half])
            speed[tile, side : side + half, :] = both[half:]
        for tile in list(range(edge - inner)) + list(range(edge + own_tiles + inner, 2 * edge + own_tiles)):
            first[tile, top : top + cells, :] = jnp.zeros((cells, LANES), F32)
    for part, start, cut, begin in ((low, 0, edge - inner, 0), (high, edge + own_tiles, 0, inner + own_tiles)):
        unit = units(part, 0, 3 * cells, span)
        for tile in range(edge):
            lanes = slice(tile * LANES, (tile + 1) * LANES)
            first[start + tile, cells : 2 * cells, :] = decode(part[:cells, lanes], unit[:cells])
            if cut <= tile < cut + inner:
                prior[begin + tile - cut, half : half + cells, :] = decode(
                    part[cells : 2 * cells, lanes], unit[cells : 2 * cells]
                )
                speed[begin + tile - cut, half : half + cells, :] = part[2 * cells :, lanes].astype(F32)

    line = lax.broadcasted_iota(jnp.int32, (LANES, LANES), 0)
    column = lax.broadcasted_iota(jnp.int32, (LANES, LANES), 1)
    gap = jnp.abs(line - column)
    band = jnp.zeros((LANES, LANES), F32)
    for reach in range(5):
        band = jnp.where(gap == reach, STENCIL[reach] * (3.0 if reach == 0 else 1.0), band)
    band = jnp.where(line // levels == column // levels, band, 0.0)
    band_upper, band_lower = split(band)
    bands = jnp.concatenate([band_upper, band_upper, band_lower], axis=0)
    front = lax.broadcasted_iota(jnp.int32, (1, LANES), 1) < levels
    count = 4
    for tile in list(range(edge - inner)) + list(range(edge + own_tiles + inner, 2 * edge + own_tiles)):
        second[tile, :, :] = jnp.zeros((3 * cells, LANES), F32)

    def advance(now, before, shift, tile_shift, later, out_row, top, rows, tile):
        tiles = [now[tile + step, top : top + rows, :] for step in range(-2, count + 2)]
        rolled = [pltpu.roll(value, levels, 1) for value in tiles]
        tall = jnp.concatenate(tiles[2 : 2 + count], axis=0)
        upper, lower = split(tall)
        deep = dot(jnp.concatenate([upper, lower, upper], axis=1), bands)
        for step in range(count):
            at = step + 2
            total = deep[step * rows : (step + 1) * rows]
            sides = [
                jnp.where(front, rolled[at] + rolled[at - 1], rolled[at + 1] + rolled[at]),
                tiles[at + 1] + tiles[at - 1],
                jnp.where(front, rolled[at + 1] + rolled[at - 2], rolled[at + 2] + rolled[at - 1]),
                tiles[at + 2] + tiles[at - 2],
            ]
            for reach in range(1, 5):
                value = sides[reach - 1] + now[tile + step, top + reach : top + reach + rows, :]
                value = value + now[tile + step, top - reach : top - reach + rows, :]
                total = total + STENCIL[reach] * value
            rate = speed[tile + step - (edge - inner), top - half : top - half + rows, :]
            past = before[tile + step - tile_shift, top - shift : top - shift + rows, :]
            following = 2.0 * tiles[at] - past + rate * total
            if later is None:
                waves[tile + step - edge, out_row : out_row + rows, :] = following
            else:
                later[tile + step, top : top + rows, :] = following

    chain = [(first, prior, half, edge - inner, second), (second, first, 0, 0, third), (third, second, 0, 0, None)]
    for step in range(steps):
        now, before, shift, tile_shift, later = chain[step]
        top, rows = (cells - half, 2 * cells) if later is not None else (cells, cells)
        margin = inner if later is not None else 0

        def loop(block, carry):
            for group in range(2):
                tile = edge - margin + 2 * count * block + group * count
                advance(now, before, shift, tile_shift, later, step * cells, top, rows, tile)
            return carry

        lax.fori_loop(0, (own_tiles + 2 * margin) // (2 * count), loop, 0)
        if later is not None:
            for tile in range(own_tiles):
                waves[tile, step * cells : (step + 1) * cells, :] = later[edge + tile, cells : 2 * cells, :]


def call(kernel, outs, scratch, flops, *args):
    moved = sum(arg.size * arg.dtype.itemsize for arg in args)
    moved += sum(out.size * jnp.dtype(out.dtype).itemsize for out in outs)
    return pl.pallas_call(
        kernel,
        out_shape=outs,
        scratch_shapes=scratch,
        cost_estimate=pl.CostEstimate(flops=flops, bytes_accessed=moved, transcendentals=0),
        compiler_params=pltpu.CompilerParams(vmem_limit_bytes=VMEM_BYTES),
    )(*args)


def shape_of(*shape, dtype=F32):
    return jax.ShapeDtypeStruct(shape, dtype)


def body(pressure, previous, velocity, tucker_core, first_factor, second_factor, depth_factor):
    cells, flat = pressure.shape
    levels, depth = depth_factor.shape
    steps, rank, core_flat = tucker_core.shape
    local_second = core_flat // depth
    lines = steps * cells
    count_x, count_y = lax.axis_size("gx"), lax.axis_size("gy")
    chips = count_x // 2
    span = 4 * steps * levels
    near = span * 2 // 3
    groups_pad = (core_flat // LANES + 7) // 8 * 8
    lines_pad = (lines * depth // LANES + 7) // 8 * 8

    across = [[(i, 2 * ((i // 2) ^ distance) + i % 2) for i in range(count_x)] for distance in range(1, chips)]
    factors = [lax.ppermute(first_factor, "gx", route) for route in across]
    other = lax.ppermute(tucker_core, "gx", [(i, i + 1 - 2 * (i % 2)) for i in range(count_x)])
    core_near, factor_near = call(
        lift_kernel,
        [shape_of(*array.shape, dtype=BF16) for array in (tucker_core, first_factor)],
        [],
        1000,
        tucker_core,
        first_factor,
    )
    mine, *sends = call(
        functools.partial(project_kernel, chips),
        [shape_of(lines, core_flat)] + [shape_of(lines, core_flat + LANES, dtype=BF16)] * (chips - 1),
        [pltpu.VMEM((chips - 1, lines, core_flat), F32)],
        4 * lines * chips * rank * core_flat,
        core_near,
        other,
        factor_near,
        *factors,
    )
    received = [lax.ppermute(send, "gx", route) for send, route in zip(sends, across)]
    pressure_later, _ = lax.optimization_barrier((pressure, mine))
    own, up, down = call(
        pack_kernel,
        [shape_of(3 * cells, flat + LANES, dtype=BF16)] + [shape_of(3 * cells, span + LANES, dtype=BF16)] * 2,
        [],
        10 * cells * flat,
        pressure_later,
        previous,
        velocity,
    )
    low = lax.ppermute(up, "gy", [(i, i + 1) for i in range(count_y - 1)])
    high = lax.ppermute(down, "gy", [(i + 1, i) for i in range(count_y - 1)])

    (codes,) = call(
        functools.partial(gather_kernel, depth, steps),
        [shape_of(local_second, lines * depth + LANES, dtype=BF16)],
        [pltpu.VMEM((lines * groups_pad, LANES), F32), pltpu.VMEM((local_second, lines * depth), F32)],
        30 * chips * lines * core_flat,
        mine,
        *received,
    )
    codes, low, high = lax.optimization_barrier((codes, low, high))
    ahead, behind = call(
        edge_kernel,
        [shape_of(2 * cells, flat + 2 * near + 3 * LANES, dtype=BF16)] * 2,
        [],
        1000,
        own,
        low,
        high,
    )

    def far(distance):
        return lax.ppermute(codes, "gy", [(i, i ^ distance) for i in range(count_y)])

    if count_y == 4:
        blocks = [codes, far(1), far(2)]
        codes_later, blocks[2] = lax.optimization_barrier((codes, blocks[2]))
        last = [
            lax.ppermute(codes_later, "gy", [(1, 2), (2, 1)]),
            lax.ppermute(blocks[2], "gy", [(1, 0), (2, 3)]),
        ]
    else:
        blocks = [codes] + [far(distance) for distance in range(1, count_y - 1)]
        last = [far(count_y - 1)]

    left = lax.ppermute(ahead, "gx", [(i, i + 1) for i in range(count_x - 1)])
    right = lax.ppermute(behind, "gx", [(i + 1, i) for i in range(count_x - 1)])
    (waves,) = call(
        functools.partial(wave_kernel, levels),
        [shape_of(flat // LANES, lines, LANES)],
        [pltpu.VMEM(((flat + 2 * span) // LANES, 3 * cells, LANES), F32)] * 3
        + [pltpu.VMEM(((flat + 2 * near) // LANES, 2 * cells, LANES), F32)] * 2,
        150 * lines * flat,
        pressure,
        previous,
        velocity,
        left,
        right,
        low,
        high,
    )
    cells_y = second_factor.shape[0]
    (mixed,) = call(
        functools.partial(early_kernel, depth, tuple(range(count_y - 1))),
        [shape_of(cells_y, lines * depth)],
        [pltpu.VMEM((2 * (count_y - 1), local_second, lines * depth), BF16)],
        4 * cells_y * count_y * local_second * lines * depth,
        second_factor,
        *blocks,
    )
    (image,) = call(
        functools.partial(image_kernel, depth, steps, count_y - 1),
        [shape_of(cells, flat)],
        [
            pltpu.VMEM((2, local_second, lines * depth), BF16),
            pltpu.VMEM((cells_y, lines * depth), F32),
            pltpu.VMEM((cells_y * lines_pad, LANES), F32),
        ],
        4 * cells_y * local_second * lines * depth,
        second_factor,
        depth_factor,
        waves,
        mixed,
        *last,
    )
    return image


def solution(mesh):
    placed = (
        P("gx", "gy"),
        P("gx", "gy"),
        P("gx", "gy"),
        P(None, "gx", "gy"),
        P("gx", None),
        P("gy", None),
        P(),
    )
    return jax.shard_map(body, mesh=mesh, in_specs=placed, out_specs=P("gx", "gy"), check_vma=False)
```

```python
import functools

import jax
import jax.numpy as jnp
from jax import lax
from jax.experimental import pallas as pl
from jax.experimental.pallas import tpu as pltpu
from jax.sharding import PartitionSpec as P

STENCIL = (-205.0 / 72.0, 8.0 / 5.0, -1.0 / 5.0, 8.0 / 315.0, -1.0 / 560.0)
F32 = jnp.float32
BF16 = jnp.bfloat16
LANES = 128
TOP = 2.0**7.75
VMEM_BYTES = 48 * 1024 * 1024


def encode(values):
    peak = jnp.max(jnp.abs(values), axis=1, keepdims=True)
    scale = (jnp.maximum(peak, 1e-30) * (1.0 + 2.0**-7)).astype(BF16).astype(F32)
    ratio = values * (TOP / scale)
    power = ratio * ratio
    power = power * power
    power = power * power
    power = power * power
    return jnp.where(ratio < 0.0, -power, power).astype(BF16), scale


def decode(codes, unit):
    codes = codes.astype(F32)
    size = jnp.maximum(jnp.abs(codes), 2.0**-126)
    for _ in range(4):
        size = lax.rsqrt(size)
    size = size * unit
    return jnp.where(codes < 0.0, -size, jnp.where(codes > 0.0, size, 0.0))


def put_codes(ref, row, values, flat):
    rows = values.shape[0]
    codes, scale = encode(values)
    ref[row : row + rows, :flat] = codes
    ref[row : row + rows, flat : flat + LANES] = jnp.broadcast_to(scale, (rows, LANES)).astype(BF16)


def units(ref, row, rows, lane):
    return ref[row : row + rows, lane : lane + LANES].astype(F32) * (1.0 / TOP)


def split(values):
    upper = values.astype(BF16)
    return upper, (values - upper.astype(F32)).astype(BF16)


def dot(left, right):
    return jnp.dot(left, right, preferred_element_type=F32)


def swap_groups(tiles, depth):
    group = lax.broadcasted_iota(jnp.int32, (1, LANES), 1) // depth
    low_half, even = group < 2, group % 2 == 0

    def exchange(left, right, distance, keep):
        return (
            jnp.where(keep, left, pltpu.roll(right, distance, 1)),
            jnp.where(keep, pltpu.roll(left, LANES - distance, 1), right),
        )

    first, third = exchange(tiles[0], tiles[2], 2 * depth, low_half)
    second, fourth = exchange(tiles[1], tiles[3], 2 * depth, low_half)
    first, second = exchange(first, second, depth, even)
    third, fourth = exchange(third, fourth, depth, even)
    return first, second, third, fourth


def pieces(rows):
    return [(start, 16) for start in range(0, rows, 16)] if rows % 16 == 0 else [(0, rows)]


def project_kernel(chips, core, other, *rest):
    factors, mine, sends, (partial,) = rest[:chips], rest[chips], rest[chips + 1 : -1], rest[-1:]
    steps, rank, flat = core.shape
    lines = mine.shape[0]
    cells = lines // steps
    place = lax.axis_index("gx")
    factor = jnp.concatenate([ref[...] for ref in factors], axis=0)
    offset = lax.broadcasted_iota(jnp.int32, (factor.shape[1], rank), 0) - lax.broadcasted_iota(
        jnp.int32, (factor.shape[1], rank), 1
    )
    own_rows, other_rows = [
        dot(factor, jnp.where(offset == owner * rank, 1.0, 0.0).astype(BF16)).astype(BF16)
        for owner in (place, place + 1 - 2 * (place % 2))
    ]
    width = 512 if flat % 512 == 0 else 256
    for step in range(steps):
        for low in range(0, flat, width):
            lanes = slice(low, low + width)
            value = dot(own_rows, core[step, :, lanes]) + dot(other_rows, other[step, :, lanes])
            mine[step * cells : (step + 1) * cells, lanes] = value[:cells]
            for distance in range(1, chips):
                partial[distance - 1, step * cells : (step + 1) * cells, lanes] = value[
                    distance * cells : (distance + 1) * cells
                ]
    for distance in range(1, chips):
        for start, count in pieces(lines):
            put_codes(sends[distance - 1], start, partial[distance - 1, start : start + count, :], flat)


def gather_kernel(depth, steps, mine, *rest):
    received, (codes, spread, turned) = rest[:-3], rest[-3:]
    lines, flat = mine.shape
    cells = lines // steps
    quads = LANES // depth
    groups = flat // LANES
    pad = spread.shape[0] // lines
    for start, count in pieces(lines):
        scales = [units(ref, start, count, flat) for ref in received]
        for group in range(groups):
            lanes = slice(group * LANES, (group + 1) * LANES)
            value = mine[start : start + count, lanes]
            for ref, unit in zip(received, scales):
                value = value + decode(ref[start : start + count, lanes], unit)
            for row in range(0, count, 8):
                spread[pl.ds((start + row) * pad + group, 8, stride=pad), :] = value[row : row + 8]
    rest_x = cells // quads
    for line in range(steps * rest_x):
        base = line // rest_x * cells + line % rest_x
        for top in range(0, groups, 8):
            count = min(8, groups - top)
            tiles = [
                spread[(base + i * rest_x) * pad + top : (base + i * rest_x) * pad + top + 8, :] for i in range(quads)
            ]
            for j, tile in enumerate(swap_groups(tiles, depth)):
                turned[j * groups + top : j * groups + top + count, line * LANES : (line + 1) * LANES] = tile[:count]
    for start, count in pieces(turned.shape[0]):
        put_codes(codes, start, turned[start : start + count, :], turned.shape[1])


def contract_second(depth, second, blocks, total, earlier, terms):
    rows, flat = blocks[0][1].shape[0], total.shape[1]
    quads = LANES // depth
    ranks = second.shape[1]
    place = lax.axis_index("gy")
    inner = (place == 1) | (place == 2)
    width = 512 if flat % 512 == 0 else 256
    columns = []
    inside = lax.broadcasted_iota(jnp.int32, (ranks, rows), 1)
    inside = inside % (rows // quads) * quads + inside // (rows // quads)
    offset = lax.broadcasted_iota(jnp.int32, (ranks, rows), 0) - inside
    for at, (distance, *options) in enumerate(blocks):
        owner = jnp.bitwise_xor(place, distance)
        chosen = jnp.where(offset == owner * rows, 1.0, 0.0).astype(BF16)
        columns.append(dot(second[...], chosen).astype(BF16))
        for start, count in pieces(rows):
            unit = units(options[0], start, count, flat)
            if len(options) > 1:
                unit = jnp.where(inner, unit, units(options[1], start, count, flat))
            for low in range(0, flat, LANES):
                codes = options[0][start : start + count, low : low + LANES].astype(F32)
                if len(options) > 1:
                    codes = jnp.where(
                        inner, codes, options[1][start : start + count, low : low + LANES].astype(F32)
                    )
                high, rest_of = split(decode(codes, unit))
                terms[2 * at, start : start + count, low : low + LANES] = high
                terms[2 * at + 1, start : start + count, low : low + LANES] = rest_of
    together = len(blocks) if rows % 16 == 0 else 1
    for low in range(0, flat, width):
        value = None if earlier is None else earlier[:, low : low + width]
        for at in range(0, len(blocks), together):
            left = jnp.concatenate([columns[k // 2] for k in range(2 * at, 2 * (at + together))], axis=1)
            right = [terms[k, :, low : low + width] for k in range(2 * at, 2 * (at + together))]
            if rows % 16 == 0:
                products = [dot(left, jnp.concatenate(right, axis=0))]
            else:
                products = [dot(columns[at], part) for part in right]
            for product in products:
                value = product if value is None else value + product
        total[:, low : low + width] = value


def early_kernel(depth, distances, second, *rest):
    blocks, (total, terms) = rest[:-2], rest[-2:]
    contract_second(depth, second, list(zip(distances, blocks)), total, None, terms)


def image_kernel(depth, steps, distance, second, depth_factor, waves, earlier, *rest):
    blocks, (image, terms, mixed, spread) = rest[:-4], rest[-4:]
    contract_second(depth, second, [(distance, *blocks)], mixed, earlier, terms)
    flat = mixed.shape[1]
    cells = image.shape[0]
    levels = depth_factor.shape[0]
    quads = LANES // depth
    groups = flat // LANES
    pad = spread.shape[0] // mixed.shape[0]
    for row in range(0, mixed.shape[0], 8):
        for group in range(groups):
            spread[pl.ds(row * pad + group, 8, stride=pad), :] = mixed[
                row : row + 8, group * LANES : (group + 1) * LANES
            ]
    square = jnp.concatenate([depth_factor[...].astype(F32)] * quads, axis=1)
    square = jnp.concatenate([square] * quads, axis=0)
    shape = square.shape
    same = lax.broadcasted_iota(jnp.int32, shape, 0) // levels == lax.broadcasted_iota(jnp.int32, shape, 1) // depth
    square = jnp.where(same, square, 0.0).astype(BF16)
    square = jnp.concatenate([square, square], axis=1)
    tiles = quads * levels // LANES
    contract = (((1,), (1,)), ((), ()))
    rest_x = cells // quads
    many = mixed.shape[0] // quads
    batch = 4 if many % 4 == 0 else 1
    for first in range(0, many, batch):
        stack = []
        for quad in range(first, first + batch):
            turned = [
                swap_groups(
                    [
                        spread[(quad * quads + j) * pad + top : (quad * quads + j) * pad + top + 8, :]
                        for j in range(quads)
                    ],
                    depth,
                )
                for top in range(0, pad, 8)
            ]
            stack += [piece[i] for i in range(quads) for piece in turned]
        high, rest_of = split(jnp.concatenate(stack, axis=0))
        source = lax.dot_general(
            jnp.concatenate([high, rest_of], axis=1), square, contract, preferred_element_type=F32
        )
        for quad in range(first, first + batch):
            base = (quad - first) * quads * pad
            for tile in range(tiles):
                at = quad * tiles + tile
                lanes = slice(tile * LANES, (tile + 1) * LANES)
                total = None
                for step in range(steps):
                    value = jnp.concatenate(
                        [
                            source[base + i * pad + step * rest_x : base + i * pad + (step + 1) * rest_x, lanes]
                            for i in range(quads)
                        ],
                        axis=0,
                    )
                    value = value * waves[at, step * cells : (step + 1) * cells, :]
                    total = value if total is None else total + value
                image[:, at * LANES : (at + 1) * LANES] = total


def lift_kernel(core, factor, core_near, factor_near):
    core_near[...] = core[...]
    factor_near[...] = factor[...]


def pack_kernel(pressure, previous, velocity, own, up, down):
    cells, flat = pressure.shape
    span = up.shape[1] - LANES
    put_codes(own, 0, pressure[...], flat)
    put_codes(own, cells, previous[...], flat)
    own[2 * cells :, :flat] = velocity[...]
    own[2 * cells :, flat:] = jnp.zeros((cells, LANES), BF16)
    up[:, :span] = own[:, flat - span : flat]
    down[:, :span] = own[:, :span]
    up[:, span:] = own[:, flat:]
    down[:, span:] = own[:, flat:]


def edge_kernel(own, low, high, ahead, behind):
    flat = own.shape[1] - LANES
    span = low.shape[1] - LANES
    near = span * 2 // 3
    cells = own.shape[0] // 3
    half = cells // 2
    scales = 2 * near + flat
    spans = [
        (low, slice(span - near, span), slice(0, near)),
        (own, slice(0, flat), slice(near, near + flat)),
        (high, slice(0, near), slice(near + flat, scales)),
        (low, slice(span, span + LANES), slice(scales, scales + LANES)),
        (own, slice(flat, flat + LANES), slice(scales + LANES, scales + 2 * LANES)),
        (high, slice(span, span + LANES), slice(scales + 2 * LANES, scales + 3 * LANES)),
    ]
    for ref, rows in ((ahead, slice(half, cells)), (behind, slice(0, half))):
        for part, lanes, into in spans:
            ref[:cells, into] = part[:cells, lanes]
            prior = part[cells : 2 * cells, lanes].astype(F32)[rows]
            speed = part[2 * cells :, lanes].astype(F32)[rows]
            ref[cells:, into] = jnp.concatenate([prior, speed], axis=0).astype(BF16)


def wave_kernel(levels, pressure, previous, velocity, left, right, low, high, waves, first, second, third, prior, speed):
    cells, flat = pressure.shape
    half = cells // 2
    span = low.shape[1] - LANES
    near = span * 2 // 3
    steps = waves.shape[1] // cells
    edge, inner, own_tiles = span // LANES, near // LANES, flat // LANES

    for tile in range(own_tiles):
        lane = tile * LANES
        first[edge + tile, cells : 2 * cells, :] = pressure[:, lane : lane + LANES]
        prior[inner + tile, half : half + cells, :] = previous[:, lane : lane + LANES]
        speed[inner + tile, half : half + cells, :] = velocity[:, lane : lane + LANES].astype(F32)
    wide = own_tiles + 2 * inner
    for part, top, side in ((left, 0, 0), (right, 2 * cells, half + cells)):
        scales = [units(part, 0, 2 * cells, (wide + k) * LANES) for k in range(3)]
        for tile in range(wide):
            lanes = slice(tile * LANES, (tile + 1) * LANES)
            unit = scales[0 if tile < inner else 1 if tile < inner + own_tiles else 2]
            first[edge - inner + tile, top : top + cells, :] = decode(part[:cells, lanes], unit[:cells])
            both = part[cells:, lanes].astype(F32)
            prior[tile, side : side + half, :] = decode(both[:half], unit[cells : cells + half])
            speed[tile, side : side + half, :] = both[half:]
        for tile in list(range(edge - inner)) + list(range(edge + own_tiles + inner, 2 * edge + own_tiles)):
            first[tile, top : top + cells, :] = jnp.zeros((cells, LANES), F32)
    for part, start, cut, begin in ((low, 0, edge - inner, 0), (high, edge + own_tiles, 0, inner + own_tiles)):
        unit = units(part, 0, 3 * cells, span)
        for tile in range(edge):
            lanes = slice(tile * LANES, (tile + 1) * LANES)
            first[start + tile, cells : 2 * cells, :] = decode(part[:cells, lanes], unit[:cells])
            if cut <= tile < cut + inner:
                prior[begin + tile - cut, half : half + cells, :] = decode(
                    part[cells : 2 * cells, lanes], unit[cells : 2 * cells]
                )
                speed[begin + tile - cut, half : half + cells, :] = part[2 * cells :, lanes].astype(F32)

    line = lax.broadcasted_iota(jnp.int32, (LANES, LANES), 0)
    column = lax.broadcasted_iota(jnp.int32, (LANES, LANES), 1)
    gap = jnp.abs(line - column)
    band = jnp.zeros((LANES, LANES), F32)
    for reach in range(5):
        band = jnp.where(gap == reach, STENCIL[reach] * (3.0 if reach == 0 else 1.0), band)
    band = jnp.where(line // levels == column // levels, band, 0.0)
    band_upper, band_lower = split(band)
    bands = jnp.concatenate([band_upper, band_upper, band_lower], axis=0)
    front = lax.broadcasted_iota(jnp.int32, (1, LANES), 1) < levels
    count = 4
    for tile in list(range(edge - inner)) + list(range(edge + own_tiles + inner, 2 * edge + own_tiles)):
        second[tile, :, :] = jnp.zeros((3 * cells, LANES), F32)

    def advance(now, before, shift, tile_shift, later, out_row, top, rows, tile):
        tiles = [now[tile + step, top : top + rows, :] for step in range(-2, count + 2)]
        rolled = [pltpu.roll(value, levels, 1) for value in tiles]
        tall = jnp.concatenate(tiles[2 : 2 + count], axis=0)
        upper, lower = split(tall)
        deep = dot(jnp.concatenate([upper, lower, upper], axis=1), bands)
        for step in range(count):
            at = step + 2
            total = deep[step * rows : (step + 1) * rows]
            sides = [
                jnp.where(front, rolled[at] + rolled[at - 1], rolled[at + 1] + rolled[at]),
                tiles[at + 1] + tiles[at - 1],
                jnp.where(front, rolled[at + 1] + rolled[at - 2], rolled[at + 2] + rolled[at - 1]),
                tiles[at + 2] + tiles[at - 2],
            ]
            for reach in range(1, 5):
                value = sides[reach - 1] + now[tile + step, top + reach : top + reach + rows, :]
                value = value + now[tile + step, top - reach : top - reach + rows, :]
                total = total + STENCIL[reach] * value
            rate = speed[tile + step - (edge - inner), top - half : top - half + rows, :]
            past = before[tile + step - tile_shift, top - shift : top - shift + rows, :]
            following = 2.0 * tiles[at] - past + rate * total
            if later is None:
                waves[tile + step - edge, out_row : out_row + rows, :] = following
            else:
                later[tile + step, top : top + rows, :] = following

    chain = [(first, prior, half, edge - inner, second), (second, first, 0, 0, third), (third, second, 0, 0, None)]
    for step in range(steps):
        now, before, shift, tile_shift, later = chain[step]
        top, rows = (cells - half, 2 * cells) if later is not None else (cells, cells)
        margin = inner if later is not None else 0

        def loop(block, carry):
            for group in range(2):
                tile = edge - margin + 2 * count * block + group * count
                advance(now, before, shift, tile_shift, later, step * cells, top, rows, tile)
            return carry

        lax.fori_loop(0, (own_tiles + 2 * margin) // (2 * count), loop, 0)
        if later is not None:
            for tile in range(own_tiles):
                waves[tile, step * cells : (step + 1) * cells, :] = later[edge + tile, cells : 2 * cells, :]


def call(kernel, outs, scratch, flops, *args):
    moved = sum(arg.size * arg.dtype.itemsize for arg in args)
    moved += sum(out.size * jnp.dtype(out.dtype).itemsize for out in outs)
    return pl.pallas_call(
        kernel,
        out_shape=outs,
        scratch_shapes=scratch,
        cost_estimate=pl.CostEstimate(flops=flops, bytes_accessed=moved, transcendentals=0),
        compiler_params=pltpu.CompilerParams(vmem_limit_bytes=VMEM_BYTES),
    )(*args)


def shape_of(*shape, dtype=F32):
    return jax.ShapeDtypeStruct(shape, dtype)


def body(pressure, previous, velocity, tucker_core, first_factor, second_factor, depth_factor):
    cells, flat = pressure.shape
    levels, depth = depth_factor.shape
    steps, rank, core_flat = tucker_core.shape
    local_second = core_flat // depth
    lines = steps * cells
    count_x, count_y = lax.axis_size("gx"), lax.axis_size("gy")
    chips = count_x // 2
    span = 4 * steps * levels
    near = span * 2 // 3
    groups_pad = (core_flat // LANES + 7) // 8 * 8
    lines_pad = (lines * depth // LANES + 7) // 8 * 8

    across = [[(i, 2 * ((i // 2) ^ distance) + i % 2) for i in range(count_x)] for distance in range(1, chips)]
    factors = [lax.ppermute(first_factor, "gx", route) for route in across[::-1]][::-1]
    other = lax.ppermute(tucker_core, "gx", [(i, i + 1 - 2 * (i % 2)) for i in range(count_x)])
    core_near, factor_near = call(
        lift_kernel,
        [shape_of(*array.shape, dtype=BF16) for array in (tucker_core, first_factor)],
        [],
        1000,
        tucker_core,
        first_factor,
    )
    mine, *sends = call(
        functools.partial(project_kernel, chips),
        [shape_of(lines, core_flat)] + [shape_of(lines, core_flat + LANES, dtype=BF16)] * (chips - 1),
        [pltpu.VMEM((chips - 1, lines, core_flat), F32)],
        4 * lines * chips * rank * core_flat,
        core_near,
        other,
        factor_near,
        *factors,
    )
    received = [lax.ppermute(send, "gx", route) for send, route in zip(sends, across)]
    pressure_later, _ = lax.optimization_barrier((pressure, mine))
    own, up, down = call(
        pack_kernel,
        [shape_of(3 * cells, flat + LANES, dtype=BF16)] + [shape_of(3 * cells, span + LANES, dtype=BF16)] * 2,
        [],
        10 * cells * flat,
        pressure_later,
        previous,
        velocity,
    )
    low = lax.ppermute(up, "gy", [(i, i + 1) for i in range(count_y - 1)])
    high = lax.ppermute(down, "gy", [(i + 1, i) for i in range(count_y - 1)])

    ahead, behind = call(
        edge_kernel,
        [shape_of(2 * cells, flat + 2 * near + 3 * LANES, dtype=BF16)] * 2,
        [],
        1000,
        own,
        low,
        high,
    )

    mine, ahead, behind = lax.optimization_barrier((mine, ahead, behind))
    (codes,) = call(
        functools.partial(gather_kernel, depth, steps),
        [shape_of(local_second, lines * depth + LANES, dtype=BF16)],
        [pltpu.VMEM((lines * groups_pad, LANES), F32), pltpu.VMEM((local_second, lines * depth), F32)],
        30 * chips * lines * core_flat,
        mine,
        *received,
    )
    codes, ahead, behind = lax.optimization_barrier((codes, ahead, behind))

    def far(distance):
        return lax.ppermute(codes, "gy", [(i, i ^ distance) for i in range(count_y)])

    if count_y == 4:
        distances = (0, 2, 1)
        blocks = [codes, far(2), far(1)]
        codes_later, blocks = lax.optimization_barrier((codes, blocks))
        last = [
            lax.ppermute(codes_later, "gy", [(1, 2), (2, 1)]),
            lax.ppermute(blocks[1], "gy", [(1, 0), (2, 3)]),
        ]
    else:
        distances = tuple(range(count_y - 1))
        blocks = [codes] + [far(distance) for distance in distances[1:]]
        last = [far(count_y - 1)]

    left = lax.ppermute(ahead, "gx", [(i, i + 1) for i in range(count_x - 1)])
    right = lax.ppermute(behind, "gx", [(i + 1, i) for i in range(count_x - 1)])
    (waves,) = call(
        functools.partial(wave_kernel, levels),
        [shape_of(flat // LANES, lines, LANES)],
        [pltpu.VMEM(((flat + 2 * span) // LANES, 3 * cells, LANES), F32)] * 3
        + [pltpu.VMEM(((flat + 2 * near) // LANES, 2 * cells, LANES), F32)] * 2,
        150 * lines * flat,
        pressure,
        previous,
        velocity,
        left,
        right,
        low,
        high,
    )
    cells_y = second_factor.shape[0]
    (mixed,) = call(
        functools.partial(early_kernel, depth, distances),
        [shape_of(cells_y, lines * depth)],
        [pltpu.VMEM((2 * (count_y - 1), local_second, lines * depth), BF16)],
        4 * cells_y * count_y * local_second * lines * depth,
        second_factor,
        *blocks,
    )
    (image,) = call(
        functools.partial(image_kernel, depth, steps, count_y - 1),
        [shape_of(cells, flat)],
        [
            pltpu.VMEM((2, local_second, lines * depth), BF16),
            pltpu.VMEM((cells_y, lines * depth), F32),
            pltpu.VMEM((cells_y * lines_pad, LANES), F32),
        ],
        4 * cells_y * local_second * lines * depth,
        second_factor,
        depth_factor,
        waves,
        mixed,
        *last,
    )
    return image


def solution(mesh):
    placed = (
        P("gx", "gy"),
        P("gx", "gy"),
        P("gx", "gy"),
        P(None, "gx", "gy"),
        P("gx", None),
        P("gy", None),
        P(),
    )
    return jax.shard_map(body, mesh=mesh, in_specs=placed, out_specs=P("gx", "gy"), check_vma=False)
```

```python
import functools

import jax
import jax.numpy as jnp
from jax import lax
from jax.experimental import pallas as pl
from jax.experimental.pallas import tpu as pltpu
from jax.sharding import PartitionSpec as P

STENCIL = (-205.0 / 72.0, 8.0 / 5.0, -1.0 / 5.0, 8.0 / 315.0, -1.0 / 560.0)
F32 = jnp.float32
BF16 = jnp.bfloat16
LANES = 128
TOP = 2.0**7.75
VMEM_BYTES = 48 * 1024 * 1024


def encode(values):
    peak = jnp.max(jnp.abs(values), axis=1, keepdims=True)
    scale = (jnp.maximum(peak, 1e-30) * (1.0 + 2.0**-7)).astype(BF16).astype(F32)
    ratio = values * (TOP / scale)
    power = ratio * ratio
    power = power * power
    power = power * power
    power = power * power
    return jnp.where(ratio < 0.0, -power, power).astype(BF16), scale


def decode(codes, unit):
    codes = codes.astype(F32)
    size = jnp.maximum(jnp.abs(codes), 2.0**-126)
    for _ in range(4):
        size = lax.rsqrt(size)
    size = size * unit
    return jnp.where(codes < 0.0, -size, jnp.where(codes > 0.0, size, 0.0))


def put_codes(ref, row, values, flat):
    rows = values.shape[0]
    codes, scale = encode(values)
    ref[row : row + rows, :flat] = codes
    ref[row : row + rows, flat : flat + LANES] = jnp.broadcast_to(scale, (rows, LANES)).astype(BF16)


def units(ref, row, rows, lane):
    return ref[row : row + rows, lane : lane + LANES].astype(F32) * (1.0 / TOP)


def split(values):
    upper = values.astype(BF16)
    return upper, (values - upper.astype(F32)).astype(BF16)


def dot(left, right):
    return jnp.dot(left, right, preferred_element_type=F32)


def swap_groups(tiles, depth):
    group = lax.broadcasted_iota(jnp.int32, (1, LANES), 1) // depth
    low_half, even = group < 2, group % 2 == 0

    def exchange(left, right, distance, keep):
        return (
            jnp.where(keep, left, pltpu.roll(right, distance, 1)),
            jnp.where(keep, pltpu.roll(left, LANES - distance, 1), right),
        )

    first, third = exchange(tiles[0], tiles[2], 2 * depth, low_half)
    second, fourth = exchange(tiles[1], tiles[3], 2 * depth, low_half)
    first, second = exchange(first, second, depth, even)
    third, fourth = exchange(third, fourth, depth, even)
    return first, second, third, fourth


def pieces(rows):
    return [(start, 16) for start in range(0, rows, 16)] if rows % 16 == 0 else [(0, rows)]


def project_kernel(core, other, factors, mine, *rest):
    sends, (partial,) = rest[:-1], rest[-1:]
    chips = factors.shape[0]
    steps, rank, flat = core.shape
    lines = mine.shape[0]
    cells = lines // steps
    place = lax.axis_index("gx")
    factor = jnp.concatenate([factors[jnp.bitwise_xor(place // 2, distance)] for distance in range(chips)], axis=0)
    offset = lax.broadcasted_iota(jnp.int32, (factor.shape[1], rank), 0) - lax.broadcasted_iota(
        jnp.int32, (factor.shape[1], rank), 1
    )
    own_rows, other_rows = [
        dot(factor, jnp.where(offset == owner * rank, 1.0, 0.0).astype(BF16)).astype(BF16)
        for owner in (place, place + 1 - 2 * (place % 2))
    ]
    width = 512 if flat % 512 == 0 else 256
    for step in range(steps):
        for low in range(0, flat, width):
            lanes = slice(low, low + width)
            value = dot(own_rows, core[step, :, lanes]) + dot(other_rows, other[step, :, lanes])
            mine[step * cells : (step + 1) * cells, lanes] = value[:cells]
            for distance in range(1, chips):
                partial[distance - 1, step * cells : (step + 1) * cells, lanes] = value[
                    distance * cells : (distance + 1) * cells
                ]
    for distance in range(1, chips):
        for start, count in pieces(lines):
            put_codes(sends[distance - 1], start, partial[distance - 1, start : start + count, :], flat)


def gather_kernel(depth, steps, mine, *rest):
    received, (codes, spread, turned) = rest[:-3], rest[-3:]
    lines, flat = mine.shape
    cells = lines // steps
    quads = LANES // depth
    groups = flat // LANES
    pad = spread.shape[0] // lines
    for start, count in pieces(lines):
        scales = [units(ref, start, count, flat) for ref in received]
        for group in range(groups):
            lanes = slice(group * LANES, (group + 1) * LANES)
            value = mine[start : start + count, lanes]
            for ref, unit in zip(received, scales):
                value = value + decode(ref[start : start + count, lanes], unit)
            for row in range(0, count, 8):
                spread[pl.ds((start + row) * pad + group, 8, stride=pad), :] = value[row : row + 8]
    rest_x = cells // quads
    for line in range(steps * rest_x):
        base = line // rest_x * cells + line % rest_x
        for top in range(0, groups, 8):
            count = min(8, groups - top)
            tiles = [
                spread[(base + i * rest_x) * pad + top : (base + i * rest_x) * pad + top + 8, :] for i in range(quads)
            ]
            for j, tile in enumerate(swap_groups(tiles, depth)):
                turned[j * groups + top : j * groups + top + count, line * LANES : (line + 1) * LANES] = tile[:count]
    for start, count in pieces(turned.shape[0]):
        put_codes(codes, start, turned[start : start + count, :], turned.shape[1])


def contract_second(depth, second, blocks, total, earlier, terms):
    rows, flat = blocks[0][1].shape[0], total.shape[1]
    quads = LANES // depth
    ranks = second.shape[1]
    place = lax.axis_index("gy")
    inner = (place == 1) | (place == 2)
    width = 512 if flat % 512 == 0 else 256
    columns = []
    inside = lax.broadcasted_iota(jnp.int32, (ranks, rows), 1)
    inside = inside % (rows // quads) * quads + inside // (rows // quads)
    offset = lax.broadcasted_iota(jnp.int32, (ranks, rows), 0) - inside
    for at, (distance, *options) in enumerate(blocks):
        owner = jnp.bitwise_xor(place, distance)
        chosen = jnp.where(offset == owner * rows, 1.0, 0.0).astype(BF16)
        columns.append(dot(second[...], chosen).astype(BF16))
        for start, count in pieces(rows):
            unit = units(options[0], start, count, flat)
            if len(options) > 1:
                unit = jnp.where(inner, unit, units(options[1], start, count, flat))
            for low in range(0, flat, LANES):
                codes = options[0][start : start + count, low : low + LANES].astype(F32)
                if len(options) > 1:
                    codes = jnp.where(
                        inner, codes, options[1][start : start + count, low : low + LANES].astype(F32)
                    )
                high, rest_of = split(decode(codes, unit))
                terms[2 * at, start : start + count, low : low + LANES] = high
                terms[2 * at + 1, start : start + count, low : low + LANES] = rest_of
    together = len(blocks) if rows % 16 == 0 else 1
    for low in range(0, flat, width):
        value = None if earlier is None else earlier[:, low : low + width]
        for at in range(0, len(blocks), together):
            left = jnp.concatenate([columns[k // 2] for k in range(2 * at, 2 * (at + together))], axis=1)
            right = [terms[k, :, low : low + width] for k in range(2 * at, 2 * (at + together))]
            if rows % 16 == 0:
                products = [dot(left, jnp.concatenate(right, axis=0))]
            else:
                products = [dot(columns[at], part) for part in right]
            for product in products:
                value = product if value is None else value + product
        total[:, low : low + width] = value


def early_kernel(depth, distances, second, *rest):
    blocks, (total, terms) = rest[:-2], rest[-2:]
    contract_second(depth, second, list(zip(distances, blocks)), total, None, terms)


def image_kernel(depth, steps, distance, second, depth_factor, waves, earlier, *rest):
    blocks, (image, terms, mixed, spread) = rest[:-4], rest[-4:]
    contract_second(depth, second, [(distance, *blocks)], mixed, earlier, terms)
    flat = mixed.shape[1]
    cells = image.shape[0]
    levels = depth_factor.shape[0]
    quads = LANES // depth
    groups = flat // LANES
    pad = spread.shape[0] // mixed.shape[0]
    for row in range(0, mixed.shape[0], 8):
        for group in range(groups):
            spread[pl.ds(row * pad + group, 8, stride=pad), :] = mixed[
                row : row + 8, group * LANES : (group + 1) * LANES
            ]
    square = jnp.concatenate([depth_factor[...].astype(F32)] * quads, axis=1)
    square = jnp.concatenate([square] * quads, axis=0)
    shape = square.shape
    same = lax.broadcasted_iota(jnp.int32, shape, 0) // levels == lax.broadcasted_iota(jnp.int32, shape, 1) // depth
    square = jnp.where(same, square, 0.0).astype(BF16)
    square = jnp.concatenate([square, square], axis=1)
    tiles = quads * levels // LANES
    contract = (((1,), (1,)), ((), ()))
    rest_x = cells // quads
    many = mixed.shape[0] // quads
    batch = 4 if many % 4 == 0 else 1
    for first in range(0, many, batch):
        stack = []
        for quad in range(first, first + batch):
            turned = [
                swap_groups(
                    [
                        spread[(quad * quads + j) * pad + top : (quad * quads + j) * pad + top + 8, :]
                        for j in range(quads)
                    ],
                    depth,
                )
                for top in range(0, pad, 8)
            ]
            stack += [piece[i] for i in range(quads) for piece in turned]
        high, rest_of = split(jnp.concatenate(stack, axis=0))
        source = lax.dot_general(
            jnp.concatenate([high, rest_of], axis=1), square, contract, preferred_element_type=F32
        )
        for quad in range(first, first + batch):
            base = (quad - first) * quads * pad
            for tile in range(tiles):
                at = quad * tiles + tile
                lanes = slice(tile * LANES, (tile + 1) * LANES)
                total = None
                for step in range(steps):
                    value = jnp.concatenate(
                        [
                            source[base + i * pad + step * rest_x : base + i * pad + (step + 1) * rest_x, lanes]
                            for i in range(quads)
                        ],
                        axis=0,
                    )
                    value = value * waves[at, step * cells : (step + 1) * cells, :]
                    total = value if total is None else total + value
                image[:, at * LANES : (at + 1) * LANES] = total


def lift_kernel(core, core_near):
    core_near[...] = core[...]


def pack_kernel(pressure, previous, velocity, own, up, down):
    cells, flat = pressure.shape
    span = up.shape[1] - LANES
    put_codes(own, 0, pressure[...], flat)
    put_codes(own, cells, previous[...], flat)
    own[2 * cells :, :flat] = velocity[...]
    own[2 * cells :, flat:] = jnp.zeros((cells, LANES), BF16)
    up[:, :span] = own[:, flat - span : flat]
    down[:, :span] = own[:, :span]
    up[:, span:] = own[:, flat:]
    down[:, span:] = own[:, flat:]


def edge_kernel(own, low, high, ahead, behind):
    flat = own.shape[1] - LANES
    span = low.shape[1] - LANES
    near = span * 2 // 3
    cells = own.shape[0] // 3
    half = cells // 2
    scales = 2 * near + flat
    spans = [
        (low, slice(span - near, span), slice(0, near)),
        (own, slice(0, flat), slice(near, near + flat)),
        (high, slice(0, near), slice(near + flat, scales)),
        (low, slice(span, span + LANES), slice(scales, scales + LANES)),
        (own, slice(flat, flat + LANES), slice(scales + LANES, scales + 2 * LANES)),
        (high, slice(span, span + LANES), slice(scales + 2 * LANES, scales + 3 * LANES)),
    ]
    for ref, rows in ((ahead, slice(half, cells)), (behind, slice(0, half))):
        for part, lanes, into in spans:
            ref[:cells, into] = part[:cells, lanes]
            prior = part[cells : 2 * cells, lanes].astype(F32)[rows]
            speed = part[2 * cells :, lanes].astype(F32)[rows]
            ref[cells:, into] = jnp.concatenate([prior, speed], axis=0).astype(BF16)


def wave_kernel(levels, pressure, previous, velocity, left, right, low, high, waves, first, second, third, prior, speed):
    cells, flat = pressure.shape
    half = cells // 2
    span = low.shape[1] - LANES
    near = span * 2 // 3
    steps = waves.shape[1] // cells
    edge, inner, own_tiles = span // LANES, near // LANES, flat // LANES

    for tile in range(own_tiles):
        lane = tile * LANES
        first[edge + tile, cells : 2 * cells, :] = pressure[:, lane : lane + LANES]
        prior[inner + tile, half : half + cells, :] = previous[:, lane : lane + LANES]
        speed[inner + tile, half : half + cells, :] = velocity[:, lane : lane + LANES].astype(F32)
    wide = own_tiles + 2 * inner
    for part, top, side in ((left, 0, 0), (right, 2 * cells, half + cells)):
        scales = [units(part, 0, 2 * cells, (wide + k) * LANES) for k in range(3)]
        for tile in range(wide):
            lanes = slice(tile * LANES, (tile + 1) * LANES)
            unit = scales[0 if tile < inner else 1 if tile < inner + own_tiles else 2]
            first[edge - inner + tile, top : top + cells, :] = decode(part[:cells, lanes], unit[:cells])
            both = part[cells:, lanes].astype(F32)
            prior[tile, side : side + half, :] = decode(both[:half], unit[cells : cells + half])
            speed[tile, side : side + half, :] = both[half:]
        for tile in list(range(edge - inner)) + list(range(edge + own_tiles + inner, 2 * edge + own_tiles)):
            first[tile, top : top + cells, :] = jnp.zeros((cells, LANES), F32)
    for part, start, cut, begin in ((low, 0, edge - inner, 0), (high, edge + own_tiles, 0, inner + own_tiles)):
        unit = units(part, 0, 3 * cells, span)
        for tile in range(edge):
            lanes = slice(tile * LANES, (tile + 1) * LANES)
            first[start + tile, cells : 2 * cells, :] = decode(part[:cells, lanes], unit[:cells])
            if cut <= tile < cut + inner:
                prior[begin + tile - cut, half : half + cells, :] = decode(
                    part[cells : 2 * cells, lanes], unit[cells : 2 * cells]
                )
                speed[begin + tile - cut, half : half + cells, :] = part[2 * cells :, lanes].astype(F32)

    line = lax.broadcasted_iota(jnp.int32, (LANES, LANES), 0)
    column = lax.broadcasted_iota(jnp.int32, (LANES, LANES), 1)
    gap = jnp.abs(line - column)
    band = jnp.zeros((LANES, LANES), F32)
    for reach in range(5):
        band = jnp.where(gap == reach, STENCIL[reach] * (3.0 if reach == 0 else 1.0), band)
    band = jnp.where(line // levels == column // levels, band, 0.0)
    band_upper, band_lower = split(band)
    bands = jnp.concatenate([band_upper, band_upper, band_lower], axis=0)
    front = lax.broadcasted_iota(jnp.int32, (1, LANES), 1) < levels
    count = 4
    for tile in list(range(edge - inner)) + list(range(edge + own_tiles + inner, 2 * edge + own_tiles)):
        second[tile, :, :] = jnp.zeros((3 * cells, LANES), F32)

    def advance(now, before, shift, tile_shift, later, out_row, top, rows, tile):
        tiles = [now[tile + step, top : top + rows, :] for step in range(-2, count + 2)]
        rolled = [pltpu.roll(value, levels, 1) for value in tiles]
        tall = jnp.concatenate(tiles[2 : 2 + count], axis=0)
        upper, lower = split(tall)
        deep = dot(jnp.concatenate([upper, lower, upper], axis=1), bands)
        for step in range(count):
            at = step + 2
            total = deep[step * rows : (step + 1) * rows]
            sides = [
                jnp.where(front, rolled[at] + rolled[at - 1], rolled[at + 1] + rolled[at]),
                tiles[at + 1] + tiles[at - 1],
                jnp.where(front, rolled[at + 1] + rolled[at - 2], rolled[at + 2] + rolled[at - 1]),
                tiles[at + 2] + tiles[at - 2],
            ]
            for reach in range(1, 5):
                value = sides[reach - 1] + now[tile + step, top + reach : top + reach + rows, :]
                value = value + now[tile + step, top - reach : top - reach + rows, :]
                total = total + STENCIL[reach] * value
            rate = speed[tile + step - (edge - inner), top - half : top - half + rows, :]
            past = before[tile + step - tile_shift, top - shift : top - shift + rows, :]
            following = 2.0 * tiles[at] - past + rate * total
            if later is None:
                waves[tile + step - edge, out_row : out_row + rows, :] = following
            else:
                later[tile + step, top : top + rows, :] = following

    chain = [(first, prior, half, edge - inner, second), (second, first, 0, 0, third), (third, second, 0, 0, None)]
    for step in range(steps):
        now, before, shift, tile_shift, later = chain[step]
        top, rows = (cells - half, 2 * cells) if later is not None else (cells, cells)
        margin = inner if later is not None else 0

        def loop(block, carry):
            for group in range(2):
                tile = edge - margin + 2 * count * block + group * count
                advance(now, before, shift, tile_shift, later, step * cells, top, rows, tile)
            return carry

        lax.fori_loop(0, (own_tiles + 2 * margin) // (2 * count), loop, 0)
        if later is not None:
            for tile in range(own_tiles):
                waves[tile, step * cells : (step + 1) * cells, :] = later[edge + tile, cells : 2 * cells, :]


def call(kernel, outs, scratch, flops, *args):
    moved = sum(arg.size * arg.dtype.itemsize for arg in args)
    moved += sum(out.size * jnp.dtype(out.dtype).itemsize for out in outs)
    return pl.pallas_call(
        kernel,
        out_shape=outs,
        scratch_shapes=scratch,
        cost_estimate=pl.CostEstimate(flops=flops, bytes_accessed=moved, transcendentals=0),
        compiler_params=pltpu.CompilerParams(vmem_limit_bytes=VMEM_BYTES),
    )(*args)


def shape_of(*shape, dtype=F32):
    return jax.ShapeDtypeStruct(shape, dtype)


def body(pressure, previous, velocity, tucker_core, first_factor, second_factor, depth_factor):
    cells, flat = pressure.shape
    levels, depth = depth_factor.shape
    steps, rank, core_flat = tucker_core.shape
    local_second = core_flat // depth
    lines = steps * cells
    count_x, count_y = lax.axis_size("gx"), lax.axis_size("gy")
    chips = count_x // 2
    span = 4 * steps * levels
    near = span * 2 // 3
    groups_pad = (core_flat // LANES + 7) // 8 * 8
    lines_pad = (lines * depth // LANES + 7) // 8 * 8

    across = [[(i, 2 * ((i // 2) ^ distance) + i % 2) for i in range(count_x)] for distance in range(1, chips)]
    other = lax.ppermute(tucker_core, "gx", [(i, i + 1 - 2 * (i % 2)) for i in range(count_x)])
    factors = lax.all_to_all(
        jnp.broadcast_to(first_factor, (chips, *first_factor.shape)),
        "gx",
        0,
        0,
        axis_index_groups=[list(range(side, count_x, 2)) for side in range(2)],
    )
    (core_near,) = call(lift_kernel, [shape_of(*tucker_core.shape, dtype=BF16)], [], 1000, tucker_core)
    mine, *sends = call(
        project_kernel,
        [shape_of(lines, core_flat)] + [shape_of(lines, core_flat + LANES, dtype=BF16)] * (chips - 1),
        [pltpu.VMEM((chips - 1, lines, core_flat), F32)],
        4 * lines * chips * rank * core_flat,
        core_near,
        other,
        factors,
    )
    received = [lax.ppermute(send, "gx", route) for send, route in zip(sends, across)]
    pressure_later, _ = lax.optimization_barrier((pressure, mine))
    own, up, down = call(
        pack_kernel,
        [shape_of(3 * cells, flat + LANES, dtype=BF16)] + [shape_of(3 * cells, span + LANES, dtype=BF16)] * 2,
        [],
        10 * cells * flat,
        pressure_later,
        previous,
        velocity,
    )
    low = lax.ppermute(up, "gy", [(i, i + 1) for i in range(count_y - 1)])
    high = lax.ppermute(down, "gy", [(i + 1, i) for i in range(count_y - 1)])

    ahead, behind = call(
        edge_kernel,
        [shape_of(2 * cells, flat + 2 * near + 3 * LANES, dtype=BF16)] * 2,
        [],
        1000,
        own,
        low,
        high,
    )

    mine, ahead, behind = lax.optimization_barrier((mine, ahead, behind))
    (codes,) = call(
        functools.partial(gather_kernel, depth, steps),
        [shape_of(local_second, lines * depth + LANES, dtype=BF16)],
        [pltpu.VMEM((lines * groups_pad, LANES), F32), pltpu.VMEM((local_second, lines * depth), F32)],
        30 * chips * lines * core_flat,
        mine,
        *received,
    )
    codes, ahead, behind = lax.optimization_barrier((codes, ahead, behind))

    def far(distance):
        return lax.ppermute(codes, "gy", [(i, i ^ distance) for i in range(count_y)])

    if count_y == 4:
        distances = (0, 2, 1)
        blocks = [codes, far(2), far(1)]
        codes_later, blocks = lax.optimization_barrier((codes, blocks))
        last = [
            lax.ppermute(codes_later, "gy", [(1, 2), (2, 1)]),
            lax.ppermute(blocks[1], "gy", [(1, 0), (2, 3)]),
        ]
    else:
        distances = tuple(range(count_y - 1))
        blocks = [codes] + [far(distance) for distance in distances[1:]]
        last = [far(count_y - 1)]

    left = lax.ppermute(ahead, "gx", [(i, i + 1) for i in range(count_x - 1)])
    right = lax.ppermute(behind, "gx", [(i + 1, i) for i in range(count_x - 1)])
    (waves,) = call(
        functools.partial(wave_kernel, levels),
        [shape_of(flat // LANES, lines, LANES)],
        [pltpu.VMEM(((flat + 2 * span) // LANES, 3 * cells, LANES), F32)] * 3
        + [pltpu.VMEM(((flat + 2 * near) // LANES, 2 * cells, LANES), F32)] * 2,
        150 * lines * flat,
        pressure,
        previous,
        velocity,
        left,
        right,
        low,
        high,
    )
    cells_y = second_factor.shape[0]
    (mixed,) = call(
        functools.partial(early_kernel, depth, distances),
        [shape_of(cells_y, lines * depth)],
        [pltpu.VMEM((2 * (count_y - 1), local_second, lines * depth), BF16)],
        4 * cells_y * count_y * local_second * lines * depth,
        second_factor,
        *blocks,
    )
    (image,) = call(
        functools.partial(image_kernel, depth, steps, count_y - 1),
        [shape_of(cells, flat)],
        [
            pltpu.VMEM((2, local_second, lines * depth), BF16),
            pltpu.VMEM((cells_y, lines * depth), F32),
            pltpu.VMEM((cells_y * lines_pad, LANES), F32),
        ],
        4 * cells_y * local_second * lines * depth,
        second_factor,
        depth_factor,
        waves,
        mixed,
        *last,
    )
    return image


def solution(mesh):
    placed = (
        P("gx", "gy"),
        P("gx", "gy"),
        P("gx", "gy"),
        P(None, "gx", "gy"),
        P("gx", None),
        P("gy", None),
        P(),
    )
    return jax.shard_map(body, mesh=mesh, in_specs=placed, out_specs=P("gx", "gy"), check_vma=False)
```

```python
import functools

import jax
import jax.numpy as jnp
from jax import lax
from jax.experimental import pallas as pl
from jax.experimental.pallas import tpu as pltpu
from jax.sharding import PartitionSpec as P

STENCIL = (-205.0 / 72.0, 8.0 / 5.0, -1.0 / 5.0, 8.0 / 315.0, -1.0 / 560.0)
F32 = jnp.float32
BF16 = jnp.bfloat16
LANES = 128
TOP = 2.0**7.75
VMEM_BYTES = 48 * 1024 * 1024


def encode(values, axis=1):
    peak = jnp.max(jnp.abs(values), axis=axis, keepdims=True)
    scale = (jnp.maximum(peak, 1e-30) * (1.0 + 2.0**-7)).astype(BF16).astype(F32)
    ratio = values * (TOP / scale)
    power = ratio * ratio
    power = power * power
    power = power * power
    power = power * power
    return jnp.where(ratio < 0.0, -power, power).astype(BF16), scale


def decode(codes, unit):
    codes = codes.astype(F32)
    size = jnp.maximum(jnp.abs(codes), 2.0**-126)
    for _ in range(4):
        size = lax.rsqrt(size)
    size = size * unit
    return jnp.where(codes < 0.0, -size, jnp.where(codes > 0.0, size, 0.0))


def put_codes(ref, row, values, flat):
    rows = values.shape[0]
    codes, scale = encode(values)
    ref[row : row + rows, :flat] = codes
    ref[row : row + rows, flat : flat + LANES] = jnp.broadcast_to(scale, (rows, LANES)).astype(BF16)


def units(ref, row, rows, lane):
    return ref[row : row + rows, lane : lane + LANES].astype(F32) * (1.0 / TOP)


def split(values):
    upper = values.astype(BF16)
    return upper, (values - upper.astype(F32)).astype(BF16)


def dot(left, right):
    return jnp.dot(left, right, preferred_element_type=F32)


def swap_groups(tiles, depth):
    group = lax.broadcasted_iota(jnp.int32, (1, LANES), 1) // depth
    low_half, even = group < 2, group % 2 == 0

    def exchange(left, right, distance, keep):
        return (
            jnp.where(keep, left, pltpu.roll(right, distance, 1)),
            jnp.where(keep, pltpu.roll(left, LANES - distance, 1), right),
        )

    first, third = exchange(tiles[0], tiles[2], 2 * depth, low_half)
    second, fourth = exchange(tiles[1], tiles[3], 2 * depth, low_half)
    first, second = exchange(first, second, depth, even)
    third, fourth = exchange(third, fourth, depth, even)
    return first, second, third, fourth


def pieces(rows):
    return [(start, 16) for start in range(0, rows, 16)] if rows % 16 == 0 else [(0, rows)]


def project_kernel(chips, core, other, *rest):
    factors, mine, sends, (partial,) = rest[:chips], rest[chips], rest[chips + 1 : -1], rest[-1:]
    steps, rank, flat = core.shape
    lines = mine.shape[0]
    cells = lines // steps
    place = lax.axis_index("gx")
    factor = jnp.concatenate([ref[...] for ref in factors[::-1]], axis=0)
    offset = lax.broadcasted_iota(jnp.int32, (factor.shape[1], rank), 0) - lax.broadcasted_iota(
        jnp.int32, (factor.shape[1], rank), 1
    )
    own_rows, other_rows = [
        dot(factor, jnp.where(offset == owner * rank, 1.0, 0.0).astype(BF16)).astype(BF16)
        for owner in (place, place + 1 - 2 * (place % 2))
    ]
    width = 512 if flat % 512 == 0 else 256
    for step in range(steps):
        for low in range(0, flat, width):
            lanes = slice(low, low + width)
            value = dot(own_rows, core[step, :, lanes]) + dot(other_rows, other[step, :, lanes])
            mine[step * cells : (step + 1) * cells, lanes] = value[:cells]
            for distance in range(1, chips):
                partial[distance - 1, step * cells : (step + 1) * cells, lanes] = value[
                    distance * cells : (distance + 1) * cells
                ]
    for distance in range(1, chips):
        for start, count in pieces(lines):
            put_codes(sends[distance - 1], start, partial[distance - 1, start : start + count, :], flat)


def gather_kernel(depth, steps, mine, *rest):
    received, (codes, spread, turned) = rest[:-3], rest[-3:]
    lines, flat = mine.shape
    cells = lines // steps
    quads = LANES // depth
    groups = flat // LANES
    pad = spread.shape[0] // lines
    for start, count in pieces(lines):
        scales = [units(ref, start, count, flat) for ref in received]
        for group in range(groups):
            lanes = slice(group * LANES, (group + 1) * LANES)
            value = mine[start : start + count, lanes]
            for ref, unit in zip(received, scales):
                value = value + decode(ref[start : start + count, lanes], unit)
            for row in range(0, count, 8):
                spread[pl.ds((start + row) * pad + group, 8, stride=pad), :] = value[row : row + 8]
    rest_x = cells // quads
    for line in range(steps * rest_x):
        base = line // rest_x * cells + line % rest_x
        for top in range(0, groups, 8):
            count = min(8, groups - top)
            tiles = [
                spread[(base + i * rest_x) * pad + top : (base + i * rest_x) * pad + top + 8, :] for i in range(quads)
            ]
            for j, tile in enumerate(swap_groups(tiles, depth)):
                turned[j * groups + top : j * groups + top + count, line * LANES : (line + 1) * LANES] = tile[:count]
    for start, count in pieces(turned.shape[0]):
        put_codes(codes, start, turned[start : start + count, :], turned.shape[1])


def contract_second(depth, second, blocks, total, earlier, terms):
    rows, flat = blocks[0][1].shape[0], total.shape[1]
    quads = LANES // depth
    ranks = second.shape[1]
    place = lax.axis_index("gy")
    inner = (place == 1) | (place == 2)
    width = 512 if flat % 512 == 0 else 256
    columns = []
    inside = lax.broadcasted_iota(jnp.int32, (ranks, rows), 1)
    inside = inside % (rows // quads) * quads + inside // (rows // quads)
    offset = lax.broadcasted_iota(jnp.int32, (ranks, rows), 0) - inside
    for at, (distance, *options) in enumerate(blocks):
        owner = jnp.bitwise_xor(place, distance)
        chosen = jnp.where(offset == owner * rows, 1.0, 0.0).astype(BF16)
        columns.append(dot(second[...], chosen).astype(BF16))
        for start, count in pieces(rows):
            unit = units(options[0], start, count, flat)
            if len(options) > 1:
                unit = jnp.where(inner, unit, units(options[1], start, count, flat))
            for low in range(0, flat, LANES):
                codes = options[0][start : start + count, low : low + LANES].astype(F32)
                if len(options) > 1:
                    codes = jnp.where(
                        inner, codes, options[1][start : start + count, low : low + LANES].astype(F32)
                    )
                high, rest_of = split(decode(codes, unit))
                terms[2 * at, start : start + count, low : low + LANES] = high
                terms[2 * at + 1, start : start + count, low : low + LANES] = rest_of
    together = len(blocks) if rows % 16 == 0 else 1
    for low in range(0, flat, width):
        value = None if earlier is None else earlier[:, low : low + width]
        for at in range(0, len(blocks), together):
            left = jnp.concatenate([columns[k // 2] for k in range(2 * at, 2 * (at + together))], axis=1)
            right = [terms[k, :, low : low + width] for k in range(2 * at, 2 * (at + together))]
            if rows % 16 == 0:
                products = [dot(left, jnp.concatenate(right, axis=0))]
            else:
                products = [dot(columns[at], part) for part in right]
            for product in products:
                value = product if value is None else value + product
        total[:, low : low + width] = value


def early_kernel(depth, distances, second, *rest):
    blocks, (total, terms) = rest[:-2], rest[-2:]
    contract_second(depth, second, list(zip(distances, blocks)), total, None, terms)


def image_kernel(depth, steps, distance, second, depth_factor, waves, earlier, *rest):
    blocks, (image, terms, mixed, spread) = rest[:-4], rest[-4:]
    contract_second(depth, second, [(distance, *blocks)], mixed, earlier, terms)
    flat = mixed.shape[1]
    cells = image.shape[0]
    levels = depth_factor.shape[0]
    quads = LANES // depth
    groups = flat // LANES
    pad = spread.shape[0] // mixed.shape[0]
    for row in range(0, mixed.shape[0], 8):
        for group in range(groups):
            spread[pl.ds(row * pad + group, 8, stride=pad), :] = mixed[
                row : row + 8, group * LANES : (group + 1) * LANES
            ]
    square = jnp.concatenate([depth_factor[...].astype(F32)] * quads, axis=1)
    square = jnp.concatenate([square] * quads, axis=0)
    shape = square.shape
    same = lax.broadcasted_iota(jnp.int32, shape, 0) // levels == lax.broadcasted_iota(jnp.int32, shape, 1) // depth
    square = jnp.where(same, square, 0.0).astype(BF16)
    square = jnp.concatenate([square, square], axis=1)
    tiles = quads * levels // LANES
    contract = (((1,), (1,)), ((), ()))
    rest_x = cells // quads
    many = mixed.shape[0] // quads
    batch = 4 if many % 4 == 0 else 1
    for first in range(0, many, batch):
        stack = []
        for quad in range(first, first + batch):
            turned = [
                swap_groups(
                    [
                        spread[(quad * quads + j) * pad + top : (quad * quads + j) * pad + top + 8, :]
                        for j in range(quads)
                    ],
                    depth,
                )
                for top in range(0, pad, 8)
            ]
            stack += [piece[i] for i in range(quads) for piece in turned]
        high, rest_of = split(jnp.concatenate(stack, axis=0))
        source = lax.dot_general(
            jnp.concatenate([high, rest_of], axis=1), square, contract, preferred_element_type=F32
        )
        for quad in range(first, first + batch):
            base = (quad - first) * quads * pad
            for tile in range(tiles):
                at = quad * tiles + tile
                lanes = slice(tile * LANES, (tile + 1) * LANES)
                total = None
                for step in range(steps):
                    value = jnp.concatenate(
                        [
                            source[base + i * pad + step * rest_x : base + i * pad + (step + 1) * rest_x, lanes]
                            for i in range(quads)
                        ],
                        axis=0,
                    )
                    value = value * waves[at, step * cells : (step + 1) * cells, :]
                    total = value if total is None else total + value
                image[:, at * LANES : (at + 1) * LANES] = total


def lift_kernel(core, factor, core_near, factor_near):
    core_near[...] = core[...]
    factor_near[...] = factor[...]


def pack_kernel(pressure, previous, velocity, own, up, down):
    cells, flat = pressure.shape
    span = up.shape[1] - LANES
    for row, part in ((0, pressure), (cells, previous)):
        codes, scale = encode(part[...], (0, 1))
        own[row : row + cells, :flat] = codes
        own[row : row + cells, flat:] = jnp.broadcast_to(scale, (cells, LANES)).astype(BF16)
    own[2 * cells :, :flat] = velocity[...]
    own[2 * cells :, flat:] = jnp.zeros((cells, LANES), BF16)
    up[:, :span] = own[:, flat - span : flat]
    down[:, :span] = own[:, :span]
    up[:, span:] = own[:, flat:]
    down[:, span:] = own[:, flat:]


def layout(cells, flat, near):
    widths = (flat, flat // 2, flat // 4, near, near // 2, LANES)
    starts = [sum(widths[:k]) for k in range(len(widths))]
    return [slice(start, start + width) for start, width in zip(starts, widths)]


def edge_kernel(own, low, high, ahead, behind):
    flat = own.shape[1] - LANES
    span = low.shape[1] - LANES
    near = span * 2 // 3
    cells = own.shape[0] // 3
    half, quarter = cells // 2, cells // 4
    places = layout(cells, flat, near)
    lane = lax.broadcasted_iota(jnp.int32, (cells, LANES), 1) // 16
    scales = jnp.zeros((cells, LANES), F32)
    for k, (part, row) in enumerate(((own, 0), (own, cells), (low, 0), (high, 0), (low, cells), (high, cells))):
        width = part.shape[1]
        scales = jnp.where(lane == k, part[row : row + cells, width - LANES :].astype(F32), scales)
    pressure = own[:cells, :flat].astype(F32)
    previous = own[cells : 2 * cells, :flat].astype(F32)
    speed = own[2 * cells :, :flat].astype(F32)
    below, above = low[:, span - near : span].astype(F32), high[:, :near].astype(F32)
    for ref, first, next_first in ((ahead, half, half - quarter), (behind, 0, half)):
        rows = slice(first, first + half)
        close = half if first > 0 else 0
        tight = slice(cells - quarter, cells) if first > 0 else slice(0, quarter)
        blocks = [
            [previous[rows], speed[rows]],
            [pressure[rows, : flat // 2], pressure[rows, flat // 2 :]],
            [pressure[next_first : next_first + quarter, k * (flat // 4) : (k + 1) * (flat // 4)] for k in range(4)],
            [below[close : close + half], above[close : close + half]],
            [
                below[cells + tight.start : cells + tight.stop, near // 2 :],
                above[cells + tight.start : cells + tight.stop, : near // 2],
                below[2 * cells + tight.start : 2 * cells + tight.stop, near // 2 :],
                above[2 * cells + tight.start : 2 * cells + tight.stop, : near // 2],
            ],
            [scales],
        ]
        for place, block in zip(places, blocks):
            ref[:, place] = jnp.concatenate(block, axis=0).astype(BF16)


def wave_kernel(levels, pressure, previous, velocity, left, right, low, high, waves, first, second, third, prior, speed):
    cells, flat = pressure.shape
    half = cells // 2
    span = low.shape[1] - LANES
    near = span * 2 // 3
    steps = waves.shape[1] // cells
    edge, inner, own_tiles = span // LANES, near // LANES, flat // LANES

    for tile in range(own_tiles):
        lane = tile * LANES
        first[edge + tile, cells : 2 * cells, :] = pressure[:, lane : lane + LANES]
        prior[inner + tile, half : half + cells, :] = previous[:, lane : lane + LANES]
        speed[inner + tile, half : half + cells, :] = velocity[:, lane : lane + LANES].astype(F32)
    for tile in range(2 * edge + own_tiles):
        if tile < edge or tile >= edge + own_tiles:
            first[tile, :cells, :] = jnp.zeros((cells, LANES), F32)
            first[tile, 2 * cells :, :] = jnp.zeros((cells, LANES), F32)
    for tile in range(2 * inner + own_tiles):
        if tile < inner or tile >= inner + own_tiles:
            for ref in (prior, speed):
                ref[tile, :half, :] = jnp.zeros((half, LANES), F32)
                ref[tile, half + cells :, :] = jnp.zeros((half, LANES), F32)
    quarter = cells // 4
    places = layout(cells, flat, near)
    for part, top, far, side, tight in (
        (left, cells - half, half - quarter, 0, half - quarter),
        (right, 2 * cells, 2 * cells + half, half + cells, half + cells),
    ):
        scales = part[:half, places[5]].astype(F32) * (1.0 / TOP)
        unit = [jnp.broadcast_to(scales[:, 16 * k : 16 * k + 1], (half, LANES)) for k in range(6)]

        def tile_of(place, tile):
            start = places[place].start + tile * LANES
            return part[:, start : start + LANES].astype(F32)

        for tile in range(own_tiles):
            both = tile_of(0, tile)
            prior[inner + tile, side : side + half, :] = decode(both[:half], unit[1])
            speed[inner + tile, side : side + half, :] = both[half:]
        for tile in range(own_tiles // 2):
            both = tile_of(1, tile)
            first[edge + tile, top : top + half, :] = decode(both[:half], unit[0])
            first[edge + own_tiles // 2 + tile, top : top + half, :] = decode(both[half:], unit[0])
        for tile in range(own_tiles // 4):
            both = decode(tile_of(2, tile), jnp.concatenate([unit[0]] * 2, axis=0))
            for k in range(4):
                into = edge + k * (own_tiles // 4) + tile
                first[into, far : far + quarter, :] = both[k * quarter : (k + 1) * quarter]
        for tile in range(inner):
            both = tile_of(3, tile)
            first[edge - inner + tile, top : top + half, :] = decode(both[:half], unit[2])
            first[edge + own_tiles + tile, top : top + half, :] = decode(both[half:], unit[3])
        for tile in range(inner // 2):
            both = tile_of(4, tile)
            ends = (inner // 2 + tile, inner + own_tiles + tile)
            values = decode(both[:half], jnp.concatenate([unit[4][:quarter], unit[5][:quarter]], axis=0))
            for k, end in enumerate(ends):
                rows = slice(k * quarter, (k + 1) * quarter)
                prior[end, tight : tight + quarter, :] = values[rows]
                speed[end, tight : tight + quarter, :] = both[half:][rows]
    for part, start, cut, begin in ((low, 0, edge - inner, 0), (high, edge + own_tiles, 0, inner + own_tiles)):
        unit = units(part, 0, 3 * cells, span)
        for tile in range(edge):
            lanes = slice(tile * LANES, (tile + 1) * LANES)
            first[start + tile, cells : 2 * cells, :] = decode(part[:cells, lanes], unit[:cells])
            if cut <= tile < cut + inner:
                prior[begin + tile - cut, half : half + cells, :] = decode(
                    part[cells : 2 * cells, lanes], unit[cells : 2 * cells]
                )
                speed[begin + tile - cut, half : half + cells, :] = part[2 * cells :, lanes].astype(F32)

    line = lax.broadcasted_iota(jnp.int32, (LANES, LANES), 0)
    column = lax.broadcasted_iota(jnp.int32, (LANES, LANES), 1)
    gap = jnp.abs(line - column)
    band = jnp.zeros((LANES, LANES), F32)
    for reach in range(5):
        band = jnp.where(gap == reach, STENCIL[reach] * (3.0 if reach == 0 else 1.0), band)
    band = jnp.where(line // levels == column // levels, band, 0.0)
    band_upper, band_lower = split(band)
    bands = jnp.concatenate([band_upper, band_upper, band_lower], axis=0)
    front = lax.broadcasted_iota(jnp.int32, (1, LANES), 1) < levels
    count = 4
    for tile in list(range(edge - inner)) + list(range(edge + own_tiles + inner, 2 * edge + own_tiles)):
        second[tile, :, :] = jnp.zeros((3 * cells, LANES), F32)

    def advance(now, before, shift, tile_shift, later, out_row, top, rows, tile):
        tiles = [now[tile + step, top : top + rows, :] for step in range(-2, count + 2)]
        rolled = [pltpu.roll(value, levels, 1) for value in tiles]
        tall = jnp.concatenate(tiles[2 : 2 + count], axis=0)
        upper, lower = split(tall)
        deep = dot(jnp.concatenate([upper, lower, upper], axis=1), bands)
        for step in range(count):
            at = step + 2
            total = deep[step * rows : (step + 1) * rows]
            sides = [
                jnp.where(front, rolled[at] + rolled[at - 1], rolled[at + 1] + rolled[at]),
                tiles[at + 1] + tiles[at - 1],
                jnp.where(front, rolled[at + 1] + rolled[at - 2], rolled[at + 2] + rolled[at - 1]),
                tiles[at + 2] + tiles[at - 2],
            ]
            for reach in range(1, 5):
                value = sides[reach - 1] + now[tile + step, top + reach : top + reach + rows, :]
                value = value + now[tile + step, top - reach : top - reach + rows, :]
                total = total + STENCIL[reach] * value
            rate = speed[tile + step - (edge - inner), top - half : top - half + rows, :]
            past = before[tile + step - tile_shift, top - shift : top - shift + rows, :]
            following = 2.0 * tiles[at] - past + rate * total
            if later is None:
                waves[tile + step - edge, out_row : out_row + rows, :] = following
            else:
                later[tile + step, top : top + rows, :] = following

    chain = [(first, prior, half, edge - inner, second), (second, first, 0, 0, third), (third, second, 0, 0, None)]
    for step in range(steps):
        now, before, shift, tile_shift, later = chain[step]
        top, rows = (cells - half, 2 * cells) if later is not None else (cells, cells)
        margin = inner if later is not None else 0

        def loop(block, carry):
            for group in range(2):
                tile = edge - margin + 2 * count * block + group * count
                advance(now, before, shift, tile_shift, later, step * cells, top, rows, tile)
            return carry

        lax.fori_loop(0, (own_tiles + 2 * margin) // (2 * count), loop, 0)
        if later is not None:
            for tile in range(own_tiles):
                waves[tile, step * cells : (step + 1) * cells, :] = later[edge + tile, cells : 2 * cells, :]


def call(kernel, outs, scratch, flops, *args):
    moved = sum(arg.size * arg.dtype.itemsize for arg in args)
    moved += sum(out.size * jnp.dtype(out.dtype).itemsize for out in outs)
    return pl.pallas_call(
        kernel,
        out_shape=outs,
        scratch_shapes=scratch,
        cost_estimate=pl.CostEstimate(flops=flops, bytes_accessed=moved, transcendentals=0),
        compiler_params=pltpu.CompilerParams(vmem_limit_bytes=VMEM_BYTES),
    )(*args)


def shape_of(*shape, dtype=F32):
    return jax.ShapeDtypeStruct(shape, dtype)


def body(pressure, previous, velocity, tucker_core, first_factor, second_factor, depth_factor):
    cells, flat = pressure.shape
    levels, depth = depth_factor.shape
    steps, rank, core_flat = tucker_core.shape
    local_second = core_flat // depth
    lines = steps * cells
    count_x, count_y = lax.axis_size("gx"), lax.axis_size("gy")
    chips = count_x // 2
    span = 4 * steps * levels
    near = span * 2 // 3
    groups_pad = (core_flat // LANES + 7) // 8 * 8
    lines_pad = (lines * depth // LANES + 7) // 8 * 8

    across = [[(i, 2 * ((i // 2) ^ distance) + i % 2) for i in range(count_x)] for distance in range(1, chips)]
    factors = [lax.ppermute(first_factor, "gx", route) for route in across[::-1]]
    other = lax.ppermute(tucker_core, "gx", [(i, i + 1 - 2 * (i % 2)) for i in range(count_x)])
    core_near, factor_near = call(
        lift_kernel,
        [shape_of(*array.shape, dtype=BF16) for array in (tucker_core, first_factor)],
        [],
        1000,
        tucker_core,
        first_factor,
    )
    mine, *sends = call(
        functools.partial(project_kernel, chips),
        [shape_of(lines, core_flat)] + [shape_of(lines, core_flat + LANES, dtype=BF16)] * (chips - 1),
        [pltpu.VMEM((chips - 1, lines, core_flat), F32)],
        4 * lines * chips * rank * core_flat,
        core_near,
        other,
        *factors,
        factor_near,
    )
    received = [lax.ppermute(send, "gx", route) for send, route in zip(sends, across)]
    pressure_later, _ = lax.optimization_barrier((pressure, mine))
    own, up, down = call(
        pack_kernel,
        [shape_of(3 * cells, flat + LANES, dtype=BF16)] + [shape_of(3 * cells, span + LANES, dtype=BF16)] * 2,
        [],
        10 * cells * flat,
        pressure_later,
        previous,
        velocity,
    )
    low = lax.ppermute(up, "gy", [(i, i + 1) for i in range(count_y - 1)])
    high = lax.ppermute(down, "gy", [(i + 1, i) for i in range(count_y - 1)])

    ahead, behind = call(
        edge_kernel,
        [shape_of(cells, layout(cells, flat, near)[-1].stop, dtype=BF16)] * 2,
        [],
        1000,
        own,
        low,
        high,
    )

    mine, ahead, behind = lax.optimization_barrier((mine, ahead, behind))
    (codes,) = call(
        functools.partial(gather_kernel, depth, steps),
        [shape_of(local_second, lines * depth + LANES, dtype=BF16)],
        [pltpu.VMEM((lines * groups_pad, LANES), F32), pltpu.VMEM((local_second, lines * depth), F32)],
        30 * chips * lines * core_flat,
        mine,
        *received,
    )
    codes, ahead, behind = lax.optimization_barrier((codes, ahead, behind))

    def far(distance):
        return lax.ppermute(codes, "gy", [(i, i ^ distance) for i in range(count_y)])

    if count_y == 4:
        distances = (0, 2, 1)
        blocks = [codes, far(2), far(1)]
        codes_later, blocks = lax.optimization_barrier((codes, blocks))
        last = [
            lax.ppermute(codes_later, "gy", [(1, 2), (2, 1)]),
            lax.ppermute(blocks[1], "gy", [(1, 0), (2, 3)]),
        ]
    else:
        distances = tuple(range(count_y - 1))
        blocks = [codes] + [far(distance) for distance in distances[1:]]
        last = [far(count_y - 1)]

    left = lax.ppermute(ahead, "gx", [(i, i + 1) for i in range(count_x - 1)])
    right = lax.ppermute(behind, "gx", [(i + 1, i) for i in range(count_x - 1)])
    (waves,) = call(
        functools.partial(wave_kernel, levels),
        [shape_of(flat // LANES, lines, LANES)],
        [pltpu.VMEM(((flat + 2 * span) // LANES, 3 * cells, LANES), F32)] * 3
        + [pltpu.VMEM(((flat + 2 * near) // LANES, 2 * cells, LANES), F32)] * 2,
        150 * lines * flat,
        pressure,
        previous,
        velocity,
        left,
        right,
        low,
        high,
    )
    cells_y = second_factor.shape[0]
    (mixed,) = call(
        functools.partial(early_kernel, depth, distances),
        [shape_of(cells_y, lines * depth)],
        [pltpu.VMEM((2 * (count_y - 1), local_second, lines * depth), BF16)],
        4 * cells_y * count_y * local_second * lines * depth,
        second_factor,
        *blocks,
    )
    (image,) = call(
        functools.partial(image_kernel, depth, steps, count_y - 1),
        [shape_of(cells, flat)],
        [
            pltpu.VMEM((2, local_second, lines * depth), BF16),
            pltpu.VMEM((cells_y, lines * depth), F32),
            pltpu.VMEM((cells_y * lines_pad, LANES), F32),
        ],
        4 * cells_y * local_second * lines * depth,
        second_factor,
        depth_factor,
        waves,
        mixed,
        *last,
    )
    return image


def solution(mesh):
    placed = (
        P("gx", "gy"),
        P("gx", "gy"),
        P("gx", "gy"),
        P(None, "gx", "gy"),
        P("gx", None),
        P("gy", None),
        P(),
    )
    return jax.shard_map(body, mesh=mesh, in_specs=placed, out_specs=P("gx", "gy"), check_vma=False)
```

```python
import functools

import jax
import jax.numpy as jnp
from jax import lax
from jax.experimental import pallas as pl
from jax.experimental.pallas import tpu as pltpu
from jax.sharding import PartitionSpec as P

STENCIL = (-205.0 / 72.0, 8.0 / 5.0, -1.0 / 5.0, 8.0 / 315.0, -1.0 / 560.0)
F32 = jnp.float32
BF16 = jnp.bfloat16
LANES = 128
TOP = 2.0**7.75
VMEM_BYTES = 48 * 1024 * 1024


def encode(values, axis=1):
    peak = jnp.max(jnp.abs(values), axis=axis, keepdims=True)
    scale = (jnp.maximum(peak, 1e-30) * (1.0 + 2.0**-7)).astype(BF16).astype(F32)
    ratio = values * (TOP / scale)
    power = ratio * ratio
    power = power * power
    power = power * power
    power = power * power
    return jnp.where(ratio < 0.0, -power, power).astype(BF16), scale


def decode(codes, unit):
    codes = codes.astype(F32)
    size = jnp.maximum(jnp.abs(codes), 2.0**-126)
    for _ in range(4):
        size = lax.rsqrt(size)
    size = size * unit
    return jnp.where(codes < 0.0, -size, jnp.where(codes > 0.0, size, 0.0))


def put_codes(ref, row, values, flat):
    rows = values.shape[0]
    codes, scale = encode(values)
    ref[row : row + rows, :flat] = codes
    ref[row : row + rows, flat : flat + LANES] = jnp.broadcast_to(scale, (rows, LANES)).astype(BF16)


def units(ref, row, rows, lane):
    return ref[row : row + rows, lane : lane + LANES].astype(F32) * (1.0 / TOP)


def split(values):
    upper = values.astype(BF16)
    return upper, (values - upper.astype(F32)).astype(BF16)


def dot(left, right):
    return jnp.dot(left, right, preferred_element_type=F32)


def swap_groups(tiles, depth):
    group = lax.broadcasted_iota(jnp.int32, (1, LANES), 1) // depth
    low_half, even = group < 2, group % 2 == 0

    def exchange(left, right, distance, keep):
        return (
            jnp.where(keep, left, pltpu.roll(right, distance, 1)),
            jnp.where(keep, pltpu.roll(left, LANES - distance, 1), right),
        )

    first, third = exchange(tiles[0], tiles[2], 2 * depth, low_half)
    second, fourth = exchange(tiles[1], tiles[3], 2 * depth, low_half)
    first, second = exchange(first, second, depth, even)
    third, fourth = exchange(third, fourth, depth, even)
    return first, second, third, fourth


def pieces(rows):
    return [(start, 16) for start in range(0, rows, 16)] if rows % 16 == 0 else [(0, rows)]


def project_kernel(chips, core, other, *rest):
    factors, mine, sends, (partial,) = rest[:chips], rest[chips], rest[chips + 1 : -1], rest[-1:]
    steps, rank, flat = core.shape
    lines = mine.shape[0]
    cells = lines // steps
    place = lax.axis_index("gx")
    factor = jnp.concatenate([ref[...] for ref in factors[::-1]], axis=0)
    offset = lax.broadcasted_iota(jnp.int32, (factor.shape[1], rank), 0) - lax.broadcasted_iota(
        jnp.int32, (factor.shape[1], rank), 1
    )
    own_rows, other_rows = [
        dot(factor, jnp.where(offset == owner * rank, 1.0, 0.0).astype(BF16)).astype(BF16)
        for owner in (place, place + 1 - 2 * (place % 2))
    ]
    width = 512 if flat % 512 == 0 else 256
    for step in range(steps):
        for low in range(0, flat, width):
            lanes = slice(low, low + width)
            value = dot(own_rows, core[step, :, lanes]) + dot(other_rows, other[step, :, lanes])
            mine[step * cells : (step + 1) * cells, lanes] = value[:cells]
            for distance in range(1, chips):
                partial[distance - 1, step * cells : (step + 1) * cells, lanes] = value[
                    distance * cells : (distance + 1) * cells
                ]
    for distance in range(1, chips):
        for start, count in pieces(lines):
            put_codes(sends[distance - 1], start, partial[distance - 1, start : start + count, :], flat)


def gather_kernel(depth, steps, mine, *rest):
    received, (codes, spread, turned) = rest[:-3], rest[-3:]
    lines, flat = mine.shape
    cells = lines // steps
    quads = LANES // depth
    groups = flat // LANES
    pad = spread.shape[0] // lines
    for start, count in pieces(lines):
        scales = [units(ref, start, count, flat) for ref in received]
        for group in range(groups):
            lanes = slice(group * LANES, (group + 1) * LANES)
            value = mine[start : start + count, lanes]
            for ref, unit in zip(received, scales):
                value = value + decode(ref[start : start + count, lanes], unit)
            for row in range(0, count, 8):
                spread[pl.ds((start + row) * pad + group, 8, stride=pad), :] = value[row : row + 8]
    rest_x = cells // quads
    for line in range(steps * rest_x):
        base = line // rest_x * cells + line % rest_x
        for top in range(0, groups, 8):
            count = min(8, groups - top)
            tiles = [
                spread[(base + i * rest_x) * pad + top : (base + i * rest_x) * pad + top + 8, :] for i in range(quads)
            ]
            for j, tile in enumerate(swap_groups(tiles, depth)):
                turned[j * groups + top : j * groups + top + count, line * LANES : (line + 1) * LANES] = tile[:count]
    for start, count in pieces(turned.shape[0]):
        put_codes(codes, start, turned[start : start + count, :], turned.shape[1])


def contract_second(depth, second, blocks, total, earlier, terms):
    rows, flat = blocks[0][1].shape[0], total.shape[1]
    quads = LANES // depth
    ranks = second.shape[1]
    place = lax.axis_index("gy")
    inner = (place == 1) | (place == 2)
    width = 512 if flat % 512 == 0 else 256
    columns = []
    inside = lax.broadcasted_iota(jnp.int32, (ranks, rows), 1)
    inside = inside % (rows // quads) * quads + inside // (rows // quads)
    offset = lax.broadcasted_iota(jnp.int32, (ranks, rows), 0) - inside
    for at, (distance, *options) in enumerate(blocks):
        owner = jnp.bitwise_xor(place, distance)
        chosen = jnp.where(offset == owner * rows, 1.0, 0.0).astype(BF16)
        columns.append(dot(second[...], chosen).astype(BF16))
        for start, count in pieces(rows):
            unit = units(options[0], start, count, flat)
            if len(options) > 1:
                unit = jnp.where(inner, unit, units(options[1], start, count, flat))
            for low in range(0, flat, LANES):
                codes = options[0][start : start + count, low : low + LANES].astype(F32)
                if len(options) > 1:
                    codes = jnp.where(
                        inner, codes, options[1][start : start + count, low : low + LANES].astype(F32)
                    )
                high, rest_of = split(decode(codes, unit))
                terms[2 * at, start : start + count, low : low + LANES] = high
                terms[2 * at + 1, start : start + count, low : low + LANES] = rest_of
    together = len(blocks) if rows % 16 == 0 else 1
    for low in range(0, flat, width):
        value = None if earlier is None else earlier[:, low : low + width]
        for at in range(0, len(blocks), together):
            left = jnp.concatenate([columns[k // 2] for k in range(2 * at, 2 * (at + together))], axis=1)
            right = [terms[k, :, low : low + width] for k in range(2 * at, 2 * (at + together))]
            if rows % 16 == 0:
                products = [dot(left, jnp.concatenate(right, axis=0))]
            else:
                products = [dot(columns[at], part) for part in right]
            for product in products:
                value = product if value is None else value + product
        total[:, low : low + width] = value


def early_kernel(depth, distances, second, *rest):
    blocks, (total, terms) = rest[:-2], rest[-2:]
    contract_second(depth, second, list(zip(distances, blocks)), total, None, terms)


def image_kernel(depth, steps, distance, second, depth_factor, waves, earlier, *rest):
    blocks, (image, terms, mixed, spread) = rest[:-4], rest[-4:]
    contract_second(depth, second, [(distance, *blocks)], mixed, earlier, terms)
    flat = mixed.shape[1]
    cells = image.shape[0]
    levels = depth_factor.shape[0]
    quads = LANES // depth
    groups = flat // LANES
    pad = spread.shape[0] // mixed.shape[0]
    for row in range(0, mixed.shape[0], 8):
        for group in range(groups):
            spread[pl.ds(row * pad + group, 8, stride=pad), :] = mixed[
                row : row + 8, group * LANES : (group + 1) * LANES
            ]
    square = jnp.concatenate([depth_factor[...].astype(F32)] * quads, axis=1)
    square = jnp.concatenate([square] * quads, axis=0)
    shape = square.shape
    same = lax.broadcasted_iota(jnp.int32, shape, 0) // levels == lax.broadcasted_iota(jnp.int32, shape, 1) // depth
    square = jnp.where(same, square, 0.0).astype(BF16)
    square = jnp.concatenate([square, square], axis=1)
    tiles = quads * levels // LANES
    contract = (((1,), (1,)), ((), ()))
    rest_x = cells // quads
    many = mixed.shape[0] // quads
    batch = 4 if many % 4 == 0 else 1
    for first in range(0, many, batch):
        stack = []
        for quad in range(first, first + batch):
            turned = [
                swap_groups(
                    [
                        spread[(quad * quads + j) * pad + top : (quad * quads + j) * pad + top + 8, :]
                        for j in range(quads)
                    ],
                    depth,
                )
                for top in range(0, pad, 8)
            ]
            stack += [piece[i] for i in range(quads) for piece in turned]
        high, rest_of = split(jnp.concatenate(stack, axis=0))
        source = lax.dot_general(
            jnp.concatenate([high, rest_of], axis=1), square, contract, preferred_element_type=F32
        )
        for quad in range(first, first + batch):
            base = (quad - first) * quads * pad
            for tile in range(tiles):
                at = quad * tiles + tile
                lanes = slice(tile * LANES, (tile + 1) * LANES)
                total = None
                for step in range(steps):
                    value = jnp.concatenate(
                        [
                            source[base + i * pad + step * rest_x : base + i * pad + (step + 1) * rest_x, lanes]
                            for i in range(quads)
                        ],
                        axis=0,
                    )
                    value = value * waves[at, step * cells : (step + 1) * cells, :]
                    total = value if total is None else total + value
                image[:, at * LANES : (at + 1) * LANES] = total


def lift_kernel(core, factor, core_near, factor_near):
    core_near[...] = core[...]
    factor_near[...] = factor[...]


def pack_kernel(pressure, previous, velocity, second, own, up, down, second_near):
    second_near[...] = second[...]
    cells, flat = pressure.shape
    span = up.shape[1] - LANES
    for row, part in ((0, pressure), (cells, previous)):
        codes, scale = encode(part[...], (0, 1))
        own[row : row + cells, :flat] = codes
        own[row : row + cells, flat:] = jnp.broadcast_to(scale, (cells, LANES)).astype(BF16)
    own[2 * cells :, :flat] = velocity[...]
    own[2 * cells :, flat:] = jnp.zeros((cells, LANES), BF16)
    up[:, :span] = own[:, flat - span : flat]
    down[:, :span] = own[:, :span]
    up[:, span:] = own[:, flat:]
    down[:, span:] = own[:, flat:]


def layout(cells, flat, near):
    widths = (flat, flat // 2, flat // 4, near, near // 2, LANES)
    starts = [sum(widths[:k]) for k in range(len(widths))]
    return [slice(start, start + width) for start, width in zip(starts, widths)]


def edge_kernel(own, low, high, ahead, behind):
    flat = own.shape[1] - LANES
    span = low.shape[1] - LANES
    near = span * 2 // 3
    cells = own.shape[0] // 3
    half, quarter = cells // 2, cells // 4
    places = layout(cells, flat, near)
    lane = lax.broadcasted_iota(jnp.int32, (cells, LANES), 1) // 16
    scales = jnp.zeros((cells, LANES), F32)
    for k, (part, row) in enumerate(((own, 0), (own, cells), (low, 0), (high, 0), (low, cells), (high, cells))):
        width = part.shape[1]
        scales = jnp.where(lane == k, part[row : row + cells, width - LANES :].astype(F32), scales)
    pressure = own[:cells, :flat].astype(F32)
    previous = own[cells : 2 * cells, :flat].astype(F32)
    speed = own[2 * cells :, :flat].astype(F32)
    below, above = low[:, span - near : span].astype(F32), high[:, :near].astype(F32)
    for ref, first, next_first in ((ahead, half, half - quarter), (behind, 0, half)):
        rows = slice(first, first + half)
        close = half if first > 0 else 0
        tight = slice(cells - quarter, cells) if first > 0 else slice(0, quarter)
        blocks = [
            [previous[rows], speed[rows]],
            [pressure[rows, : flat // 2], pressure[rows, flat // 2 :]],
            [pressure[next_first : next_first + quarter, k * (flat // 4) : (k + 1) * (flat // 4)] for k in range(4)],
            [below[close : close + half], above[close : close + half]],
            [
                below[cells + tight.start : cells + tight.stop, near // 2 :],
                above[cells + tight.start : cells + tight.stop, : near // 2],
                below[2 * cells + tight.start : 2 * cells + tight.stop, near // 2 :],
                above[2 * cells + tight.start : 2 * cells + tight.stop, : near // 2],
            ],
            [scales],
        ]
        for place, block in zip(places, blocks):
            ref[:, place] = jnp.concatenate(block, axis=0).astype(BF16)


def wave_kernel(levels, pressure, previous, velocity, left, right, low, high, waves, first, second, third, prior, speed):
    cells, flat = pressure.shape
    half = cells // 2
    span = low.shape[1] - LANES
    near = span * 2 // 3
    steps = waves.shape[1] // cells
    edge, inner, own_tiles = span // LANES, near // LANES, flat // LANES

    for tile in range(own_tiles):
        lane = tile * LANES
        first[edge + tile, cells : 2 * cells, :] = pressure[:, lane : lane + LANES]
        prior[inner + tile, half : half + cells, :] = previous[:, lane : lane + LANES]
        speed[inner + tile, half : half + cells, :] = velocity[:, lane : lane + LANES].astype(F32)
    for tile in range(2 * edge + own_tiles):
        if tile < edge or tile >= edge + own_tiles:
            first[tile, :cells, :] = jnp.zeros((cells, LANES), F32)
            first[tile, 2 * cells :, :] = jnp.zeros((cells, LANES), F32)
    for tile in range(2 * inner + own_tiles):
        if tile < inner or tile >= inner + own_tiles:
            for ref in (prior, speed):
                ref[tile, :half, :] = jnp.zeros((half, LANES), F32)
                ref[tile, half + cells :, :] = jnp.zeros((half, LANES), F32)
    quarter = cells // 4
    places = layout(cells, flat, near)
    for part, top, far, side, tight in (
        (left, cells - half, half - quarter, 0, half - quarter),
        (right, 2 * cells, 2 * cells + half, half + cells, half + cells),
    ):
        scales = part[:half, places[5]].astype(F32) * (1.0 / TOP)
        unit = [jnp.broadcast_to(scales[:, 16 * k : 16 * k + 1], (half, LANES)) for k in range(6)]

        def tile_of(place, tile):
            start = places[place].start + tile * LANES
            return part[:, start : start + LANES].astype(F32)

        for tile in range(own_tiles):
            both = tile_of(0, tile)
            prior[inner + tile, side : side + half, :] = decode(both[:half], unit[1])
            speed[inner + tile, side : side + half, :] = both[half:]
        for tile in range(own_tiles // 2):
            both = tile_of(1, tile)
            first[edge + tile, top : top + half, :] = decode(both[:half], unit[0])
            first[edge + own_tiles // 2 + tile, top : top + half, :] = decode(both[half:], unit[0])
        for tile in range(own_tiles // 4):
            both = decode(tile_of(2, tile), jnp.concatenate([unit[0]] * 2, axis=0))
            for k in range(4):
                into = edge + k * (own_tiles // 4) + tile
                first[into, far : far + quarter, :] = both[k * quarter : (k + 1) * quarter]
        for tile in range(inner):
            both = tile_of(3, tile)
            first[edge - inner + tile, top : top + half, :] = decode(both[:half], unit[2])
            first[edge + own_tiles + tile, top : top + half, :] = decode(both[half:], unit[3])
        for tile in range(inner // 2):
            both = tile_of(4, tile)
            ends = (inner // 2 + tile, inner + own_tiles + tile)
            values = decode(both[:half], jnp.concatenate([unit[4][:quarter], unit[5][:quarter]], axis=0))
            for k, end in enumerate(ends):
                rows = slice(k * quarter, (k + 1) * quarter)
                prior[end, tight : tight + quarter, :] = values[rows]
                speed[end, tight : tight + quarter, :] = both[half:][rows]
    for part, start, cut, begin in ((low, 0, edge - inner, 0), (high, edge + own_tiles, 0, inner + own_tiles)):
        unit = units(part, 0, 3 * cells, span)
        for tile in range(edge):
            lanes = slice(tile * LANES, (tile + 1) * LANES)
            first[start + tile, cells : 2 * cells, :] = decode(part[:cells, lanes], unit[:cells])
            if cut <= tile < cut + inner:
                prior[begin + tile - cut, half : half + cells, :] = decode(
                    part[cells : 2 * cells, lanes], unit[cells : 2 * cells]
                )
                speed[begin + tile - cut, half : half + cells, :] = part[2 * cells :, lanes].astype(F32)

    line = lax.broadcasted_iota(jnp.int32, (LANES, LANES), 0)
    column = lax.broadcasted_iota(jnp.int32, (LANES, LANES), 1)
    gap = jnp.abs(line - column)
    band = jnp.zeros((LANES, LANES), F32)
    for reach in range(5):
        band = jnp.where(gap == reach, STENCIL[reach] * (3.0 if reach == 0 else 1.0), band)
    band = jnp.where(line // levels == column // levels, band, 0.0)
    band_upper, band_lower = split(band)
    bands = jnp.concatenate([band_upper, band_upper, band_lower], axis=0)
    front = lax.broadcasted_iota(jnp.int32, (1, LANES), 1) < levels
    count = 4
    for tile in list(range(edge - inner)) + list(range(edge + own_tiles + inner, 2 * edge + own_tiles)):
        second[tile, :, :] = jnp.zeros((3 * cells, LANES), F32)

    def advance(now, before, shift, tile_shift, later, out_row, top, rows, tile):
        tiles = [now[tile + step, top : top + rows, :] for step in range(-2, count + 2)]
        rolled = [pltpu.roll(value, levels, 1) for value in tiles]
        tall = jnp.concatenate(tiles[2 : 2 + count], axis=0)
        upper, lower = split(tall)
        deep = dot(jnp.concatenate([upper, lower, upper], axis=1), bands)
        for step in range(count):
            at = step + 2
            total = deep[step * rows : (step + 1) * rows]
            sides = [
                jnp.where(front, rolled[at] + rolled[at - 1], rolled[at + 1] + rolled[at]),
                tiles[at + 1] + tiles[at - 1],
                jnp.where(front, rolled[at + 1] + rolled[at - 2], rolled[at + 2] + rolled[at - 1]),
                tiles[at + 2] + tiles[at - 2],
            ]
            for reach in range(1, 5):
                value = sides[reach - 1] + now[tile + step, top + reach : top + reach + rows, :]
                value = value + now[tile + step, top - reach : top - reach + rows, :]
                total = total + STENCIL[reach] * value
            rate = speed[tile + step - (edge - inner), top - half : top - half + rows, :]
            past = before[tile + step - tile_shift, top - shift : top - shift + rows, :]
            following = 2.0 * tiles[at] - past + rate * total
            if later is None:
                waves[tile + step - edge, out_row : out_row + rows, :] = following
            else:
                later[tile + step, top : top + rows, :] = following

    chain = [(first, prior, half, edge - inner, second), (second, first, 0, 0, third), (third, second, 0, 0, None)]
    for step in range(steps):
        now, before, shift, tile_shift, later = chain[step]
        top, rows = (cells - half, 2 * cells) if later is not None else (cells, cells)
        margin = (steps - 1 - step) * (edge // steps)

        for tile in range(edge - margin, edge + own_tiles + margin, count):
            advance(now, before, shift, tile_shift, later, step * cells, top, rows, tile)
        if later is not None:
            for tile in range(own_tiles):
                waves[tile, step * cells : (step + 1) * cells, :] = later[edge + tile, cells : 2 * cells, :]


def call(kernel, outs, scratch, flops, *args):
    moved = sum(arg.size * arg.dtype.itemsize for arg in args)
    moved += sum(out.size * jnp.dtype(out.dtype).itemsize for out in outs)
    return pl.pallas_call(
        kernel,
        out_shape=outs,
        scratch_shapes=scratch,
        cost_estimate=pl.CostEstimate(flops=flops, bytes_accessed=moved, transcendentals=0),
        compiler_params=pltpu.CompilerParams(vmem_limit_bytes=VMEM_BYTES),
    )(*args)


def shape_of(*shape, dtype=F32):
    return jax.ShapeDtypeStruct(shape, dtype)


def body(pressure, previous, velocity, tucker_core, first_factor, second_factor, depth_factor):
    cells, flat = pressure.shape
    levels, depth = depth_factor.shape
    steps, rank, core_flat = tucker_core.shape
    local_second = core_flat // depth
    lines = steps * cells
    count_x, count_y = lax.axis_size("gx"), lax.axis_size("gy")
    chips = count_x // 2
    span = 4 * steps * levels
    near = span * 2 // 3
    groups_pad = (core_flat // LANES + 7) // 8 * 8
    lines_pad = (lines * depth // LANES + 7) // 8 * 8

    across = [[(i, 2 * ((i // 2) ^ distance) + i % 2) for i in range(count_x)] for distance in range(1, chips)]
    factors = [lax.ppermute(first_factor, "gx", route) for route in across[::-1]]
    other = lax.ppermute(tucker_core, "gx", [(i, i + 1 - 2 * (i % 2)) for i in range(count_x)])
    core_near, factor_near = call(
        lift_kernel,
        [shape_of(*array.shape, dtype=BF16) for array in (tucker_core, first_factor)],
        [],
        1000,
        tucker_core,
        first_factor,
    )
    mine, *sends = call(
        functools.partial(project_kernel, chips),
        [shape_of(lines, core_flat)] + [shape_of(lines, core_flat + LANES, dtype=BF16)] * (chips - 1),
        [pltpu.VMEM((chips - 1, lines, core_flat), F32)],
        4 * lines * chips * rank * core_flat,
        core_near,
        other,
        *factors,
        factor_near,
    )
    received = [lax.ppermute(send, "gx", route) for send, route in zip(sends, across)]
    pressure_later, _ = lax.optimization_barrier((pressure, mine))
    own, up, down, second_near = call(
        pack_kernel,
        [shape_of(3 * cells, flat + LANES, dtype=BF16)]
        + [shape_of(3 * cells, span + LANES, dtype=BF16)] * 2
        + [shape_of(*second_factor.shape, dtype=BF16)],
        [],
        10 * cells * flat,
        pressure_later,
        previous,
        velocity,
        second_factor,
    )
    low = lax.ppermute(up, "gy", [(i, i + 1) for i in range(count_y - 1)])
    high = lax.ppermute(down, "gy", [(i + 1, i) for i in range(count_y - 1)])

    ahead, behind = call(
        edge_kernel,
        [shape_of(cells, layout(cells, flat, near)[-1].stop, dtype=BF16)] * 2,
        [],
        1000,
        own,
        low,
        high,
    )

    mine, ahead, behind = lax.optimization_barrier((mine, ahead, behind))
    (codes,) = call(
        functools.partial(gather_kernel, depth, steps),
        [shape_of(local_second, lines * depth + LANES, dtype=BF16)],
        [pltpu.VMEM((lines * groups_pad, LANES), F32), pltpu.VMEM((local_second, lines * depth), F32)],
        30 * chips * lines * core_flat,
        mine,
        *received,
    )
    codes, ahead, behind = lax.optimization_barrier((codes, ahead, behind))

    def far(distance):
        return lax.ppermute(codes, "gy", [(i, i ^ distance) for i in range(count_y)])

    if count_y == 4:
        distances = (0, 2, 1)
        blocks = [codes, far(2), far(1)]
        codes_later, blocks = lax.optimization_barrier((codes, blocks))
        last = [
            lax.ppermute(codes_later, "gy", [(1, 2), (2, 1)]),
            lax.ppermute(blocks[1], "gy", [(1, 0), (2, 3)]),
        ]
    else:
        distances = tuple(range(count_y - 1))
        blocks = [codes] + [far(distance) for distance in distances[1:]]
        last = [far(count_y - 1)]

    left = lax.ppermute(ahead, "gx", [(i, i + 1) for i in range(count_x - 1)])
    right = lax.ppermute(behind, "gx", [(i + 1, i) for i in range(count_x - 1)])
    (waves,) = call(
        functools.partial(wave_kernel, levels),
        [shape_of(flat // LANES, lines, LANES)],
        [pltpu.VMEM(((flat + 2 * span) // LANES, 3 * cells, LANES), F32)] * 3
        + [pltpu.VMEM(((flat + 2 * near) // LANES, 2 * cells, LANES), F32)] * 2,
        150 * lines * flat,
        pressure,
        previous,
        velocity,
        left,
        right,
        low,
        high,
    )
    cells_y = second_factor.shape[0]
    (mixed,) = call(
        functools.partial(early_kernel, depth, distances),
        [shape_of(cells_y, lines * depth)],
        [pltpu.VMEM((2 * (count_y - 1), local_second, lines * depth), BF16)],
        4 * cells_y * count_y * local_second * lines * depth,
        second_near,
        *blocks,
    )
    (image,) = call(
        functools.partial(image_kernel, depth, steps, count_y - 1),
        [shape_of(cells, flat)],
        [
            pltpu.VMEM((2, local_second, lines * depth), BF16),
            pltpu.VMEM((cells_y, lines * depth), F32),
            pltpu.VMEM((cells_y * lines_pad, LANES), F32),
        ],
        4 * cells_y * local_second * lines * depth,
        second_near,
        depth_factor,
        waves,
        mixed,
        *last,
    )
    return image


def solution(mesh):
    placed = (
        P("gx", "gy"),
        P("gx", "gy"),
        P("gx", "gy"),
        P(None, "gx", "gy"),
        P("gx", None),
        P("gy", None),
        P(),
    )
    return jax.shard_map(body, mesh=mesh, in_specs=placed, out_specs=P("gx", "gy"), check_vma=False)
```

```python
import functools

import jax
import jax.numpy as jnp
from jax import lax
from jax.experimental import pallas as pl
from jax.experimental.pallas import tpu as pltpu
from jax.sharding import PartitionSpec as P

STENCIL = (-205.0 / 72.0, 8.0 / 5.0, -1.0 / 5.0, 8.0 / 315.0, -1.0 / 560.0)
F32 = jnp.float32
BF16 = jnp.bfloat16
LANES = 128
TOP = 2.0**7.75
VMEM_BYTES = 48 * 1024 * 1024


def scale_of(peak):
    return (jnp.maximum(peak, 1e-30) * (1.0 + 2.0**-7)).astype(BF16).astype(F32)


def raise_power(ratio):
    power = ratio * ratio
    power = power * power
    power = power * power
    power = power * power
    return jnp.where(ratio < 0.0, -power, power).astype(BF16)


def encode(values):
    scale = scale_of(jnp.max(jnp.abs(values), axis=(0, 1), keepdims=True))
    return raise_power(values * (TOP / scale)), scale


def decode(codes, unit):
    codes = codes.astype(F32)
    size = jnp.maximum(jnp.abs(codes), 2.0**-126)
    for _ in range(4):
        size = lax.rsqrt(size)
    size = size * unit
    return jnp.where(codes < 0.0, -size, jnp.where(codes > 0.0, size, 0.0))


def stride_of(rows):
    return (rows + 15) // 16 * 16


def message(rows, flat):
    return shape_of(flat // LANES * stride_of(rows) + 16, LANES, dtype=BF16)


def put_message(ref, source):
    rows, flat = source.shape
    stride = stride_of(rows)
    peak = jnp.max(jnp.abs(source[...]), axis=0, keepdims=True)
    scale = scale_of(jnp.max(peak, axis=1, keepdims=True))
    factor = TOP / scale
    for tile in range(flat // LANES):
        for start, count in pieces(rows):
            into = tile * stride + start
            ref[into : into + count, :] = raise_power(
                source[start : start + count, tile * LANES : (tile + 1) * LANES] * factor
            )
    ref[flat // LANES * stride :, :] = jnp.broadcast_to(scale, (16, LANES)).astype(BF16)


def unit_of(ref):
    return ref[ref.shape[0] - 16 :, :].astype(F32)[:8] * (1.0 / TOP)


def units(ref, row, rows, lane):
    return ref[row : row + rows, lane : lane + LANES].astype(F32) * (1.0 / TOP)


def pieces(rows):
    return [(start, 16) for start in range(0, rows, 16)] if rows % 16 == 0 else [(0, rows)]


def split(values):
    upper = values.astype(BF16)
    return upper, (values - upper.astype(F32)).astype(BF16)


def dot(left, right):
    return jnp.dot(left, right, preferred_element_type=F32)


def swap_groups(tiles, depth):
    group = lax.broadcasted_iota(jnp.int32, (1, LANES), 1) // depth
    low_half, even = group < 2, group % 2 == 0

    def exchange(left, right, distance, keep):
        return (
            jnp.where(keep, left, pltpu.roll(right, distance, 1)),
            jnp.where(keep, pltpu.roll(left, LANES - distance, 1), right),
        )

    first, third = exchange(tiles[0], tiles[2], 2 * depth, low_half)
    second, fourth = exchange(tiles[1], tiles[3], 2 * depth, low_half)
    first, second = exchange(first, second, depth, even)
    third, fourth = exchange(third, fourth, depth, even)
    return first, second, third, fourth


def project_kernel(chips, core, other, *rest):
    factors, mine, sends, (partial,) = rest[:chips], rest[chips], rest[chips + 1 : -1], rest[-1:]
    steps, rank, flat = core.shape
    lines = mine.shape[0]
    cells = lines // steps
    place = lax.axis_index("gx")
    factor = jnp.concatenate([ref[...] for ref in factors[::-1]], axis=0)
    offset = lax.broadcasted_iota(jnp.int32, (factor.shape[1], rank), 0) - lax.broadcasted_iota(
        jnp.int32, (factor.shape[1], rank), 1
    )
    own_rows, other_rows = [
        dot(factor, jnp.where(offset == owner * rank, 1.0, 0.0).astype(BF16)).astype(BF16)
        for owner in (place, place + 1 - 2 * (place % 2))
    ]
    width = 512 if flat % 512 == 0 else 256
    for step in range(steps):
        for low in range(0, flat, width):
            lanes = slice(low, low + width)
            value = dot(own_rows, core[step, :, lanes]) + dot(other_rows, other[step, :, lanes])
            mine[step * cells : (step + 1) * cells, lanes] = value[:cells]
            for distance in range(1, chips):
                partial[distance - 1, step * cells : (step + 1) * cells, lanes] = value[
                    distance * cells : (distance + 1) * cells
                ]
    for distance in range(1, chips):
        put_message(sends[distance - 1], partial.at[distance - 1])


def gather_kernel(depth, steps, mine, *rest):
    received, (codes, spread, turned) = rest[:-3], rest[-3:]
    lines, flat = mine.shape
    cells = lines // steps
    quads = LANES // depth
    groups = flat // LANES
    pad = spread.shape[0] // lines
    scales = [unit_of(ref) for ref in received]
    for start, count in pieces(lines):
        for group in range(groups):
            lanes = slice(group * LANES, (group + 1) * LANES)
            value = mine[start : start + count, lanes]
            for ref, unit in zip(received, scales):
                into = group * stride_of(lines) + start
                value = value + decode(ref[into : into + count, :], unit[:1])
            for row in range(0, count, 8):
                spread[pl.ds((start + row) * pad + group, 8, stride=pad), :] = value[row : row + 8]
    rest_x = cells // quads
    for line in range(steps * rest_x):
        base = line // rest_x * cells + line % rest_x
        for top in range(0, groups, 8):
            count = min(8, groups - top)
            tiles = [
                spread[(base + i * rest_x) * pad + top : (base + i * rest_x) * pad + top + 8, :] for i in range(quads)
            ]
            for j, tile in enumerate(swap_groups(tiles, depth)):
                turned[j * groups + top : j * groups + top + count, line * LANES : (line + 1) * LANES] = tile[:count]
    put_message(codes, turned)


def contract_second(depth, second, blocks, total, earlier, terms):
    rows, flat = terms.shape[1], total.shape[1]
    quads = LANES // depth
    ranks = second.shape[1]
    place = lax.axis_index("gy")
    inner = (place == 1) | (place == 2)
    width = 512 if flat % 512 == 0 else 256
    columns = []
    inside = lax.broadcasted_iota(jnp.int32, (ranks, rows), 1)
    inside = inside % (rows // quads) * quads + inside // (rows // quads)
    offset = lax.broadcasted_iota(jnp.int32, (ranks, rows), 0) - inside
    for at, (distance, *options) in enumerate(blocks):
        owner = jnp.bitwise_xor(place, distance)
        chosen = jnp.where(offset == owner * rows, 1.0, 0.0).astype(BF16)
        columns.append(dot(second[...], chosen).astype(BF16))
        unit = unit_of(options[0])[:1]
        if len(options) > 1:
            unit = jnp.where(inner, unit, unit_of(options[1])[:1])
        for low in range(0, flat, LANES):
            for start, count in pieces(rows):
                into = low // LANES * stride_of(rows) + start
                codes = options[0][into : into + count, :].astype(F32)
                if len(options) > 1:
                    codes = jnp.where(inner, codes, options[1][into : into + count, :].astype(F32))
                high, rest_of = split(decode(codes, unit))
                terms[2 * at, start : start + count, low : low + LANES] = high
                terms[2 * at + 1, start : start + count, low : low + LANES] = rest_of
    together = len(blocks) if rows % 16 == 0 else 1
    for low in range(0, flat, width):
        value = None if earlier is None else earlier[:, low : low + width]
        for at in range(0, len(blocks), together):
            left = jnp.concatenate([columns[k // 2] for k in range(2 * at, 2 * (at + together))], axis=1)
            right = [terms[k, :, low : low + width] for k in range(2 * at, 2 * (at + together))]
            if rows % 16 == 0:
                products = [dot(left, jnp.concatenate(right, axis=0))]
            else:
                products = [dot(columns[at], part) for part in right]
            for product in products:
                value = product if value is None else value + product
        total[:, low : low + width] = value


def early_kernel(depth, distances, second, *rest):
    blocks, (total, terms) = rest[:-2], rest[-2:]
    contract_second(depth, second, list(zip(distances, blocks)), total, None, terms)


def image_kernel(depth, steps, distance, second, depth_factor, waves, earlier, *rest):
    blocks, (image, terms, mixed, spread) = rest[:-4], rest[-4:]
    contract_second(depth, second, [(distance, *blocks)], mixed, earlier, terms)
    flat = mixed.shape[1]
    cells = image.shape[0]
    levels = depth_factor.shape[0]
    quads = LANES // depth
    groups = flat // LANES
    pad = spread.shape[0] // mixed.shape[0]
    for row in range(0, mixed.shape[0], 8):
        for group in range(groups):
            spread[pl.ds(row * pad + group, 8, stride=pad), :] = mixed[
                row : row + 8, group * LANES : (group + 1) * LANES
            ]
    square = jnp.concatenate([depth_factor[...].astype(F32)] * quads, axis=1)
    square = jnp.concatenate([square] * quads, axis=0)
    shape = square.shape
    same = lax.broadcasted_iota(jnp.int32, shape, 0) // levels == lax.broadcasted_iota(jnp.int32, shape, 1) // depth
    square = jnp.where(same, square, 0.0).astype(BF16)
    square = jnp.concatenate([square, square], axis=1)
    tiles = quads * levels // LANES
    contract = (((1,), (1,)), ((), ()))
    rest_x = cells // quads
    many = mixed.shape[0] // quads
    batch = 4 if many % 4 == 0 else 1
    for first in range(0, many, batch):
        stack = []
        for quad in range(first, first + batch):
            turned = [
                swap_groups(
                    [
                        spread[(quad * quads + j) * pad + top : (quad * quads + j) * pad + top + 8, :]
                        for j in range(quads)
                    ],
                    depth,
                )
                for top in range(0, pad, 8)
            ]
            stack += [piece[i] for i in range(quads) for piece in turned]
        high, rest_of = split(jnp.concatenate(stack, axis=0))
        source = lax.dot_general(
            jnp.concatenate([high, rest_of], axis=1), square, contract, preferred_element_type=F32
        )
        for quad in range(first, first + batch):
            base = (quad - first) * quads * pad
            for tile in range(tiles):
                at = quad * tiles + tile
                lanes = slice(tile * LANES, (tile + 1) * LANES)
                total = None
                for step in range(steps):
                    value = jnp.concatenate(
                        [
                            source[base + i * pad + step * rest_x : base + i * pad + (step + 1) * rest_x, lanes]
                            for i in range(quads)
                        ],
                        axis=0,
                    )
                    value = value * waves[at, step * cells : (step + 1) * cells, :]
                    total = value if total is None else total + value
                image[:, at * LANES : (at + 1) * LANES] = total


def lift_kernel(core, factor, core_near, factor_near):
    core_near[...] = core[...]
    factor_near[...] = factor[...]


def pack_kernel(pressure, previous, velocity, second, own, up, down, second_near):
    second_near[...] = second[...]
    cells, flat = pressure.shape
    span = up.shape[1] - LANES
    for row, part in ((0, pressure), (cells, previous)):
        codes, scale = encode(part[...])
        own[row : row + cells, :flat] = codes
        own[row : row + cells, flat:] = jnp.broadcast_to(scale, (cells, LANES)).astype(BF16)
    own[2 * cells :, :flat] = velocity[...]
    own[2 * cells :, flat:] = jnp.zeros((cells, LANES), BF16)
    up[:, :span] = own[:, flat - span : flat]
    down[:, :span] = own[:, :span]
    up[:, span:] = own[:, flat:]
    down[:, span:] = own[:, flat:]


def layout(cells, flat, near):
    widths = (flat, flat // 2, flat // 4, near, near // 2, LANES)
    starts = [sum(widths[:k]) for k in range(len(widths))]
    return [slice(start, start + width) for start, width in zip(starts, widths)]


def edge_kernel(own, low, high, ahead, behind):
    flat = own.shape[1] - LANES
    span = low.shape[1] - LANES
    near = span * 2 // 3
    cells = own.shape[0] // 3
    half, quarter = cells // 2, cells // 4
    places = layout(cells, flat, near)
    lane = lax.broadcasted_iota(jnp.int32, (cells, LANES), 1) // 16
    scales = jnp.zeros((cells, LANES), F32)
    for k, (part, row) in enumerate(((own, 0), (own, cells), (low, 0), (high, 0), (low, cells), (high, cells))):
        width = part.shape[1]
        scales = jnp.where(lane == k, part[row : row + cells, width - LANES :].astype(F32), scales)
    pressure = own[:cells, :flat].astype(F32)
    previous = own[cells : 2 * cells, :flat].astype(F32)
    speed = own[2 * cells :, :flat].astype(F32)
    below, above = low[:, span - near : span].astype(F32), high[:, :near].astype(F32)
    for ref, first, next_first in ((ahead, half, half - quarter), (behind, 0, half)):
        rows = slice(first, first + half)
        close = half if first > 0 else 0
        tight = slice(cells - quarter, cells) if first > 0 else slice(0, quarter)
        blocks = [
            [previous[rows], speed[rows]],
            [pressure[rows, : flat // 2], pressure[rows, flat // 2 :]],
            [pressure[next_first : next_first + quarter, k * (flat // 4) : (k + 1) * (flat // 4)] for k in range(4)],
            [below[close : close + half], above[close : close + half]],
            [
                below[cells + tight.start : cells + tight.stop, near // 2 :],
                above[cells + tight.start : cells + tight.stop, : near // 2],
                below[2 * cells + tight.start : 2 * cells + tight.stop, near // 2 :],
                above[2 * cells + tight.start : 2 * cells + tight.stop, : near // 2],
            ],
            [scales],
        ]
        for place, block in zip(places, blocks):
            ref[:, place] = jnp.concatenate(block, axis=0).astype(BF16)


def wave_kernel(levels, pressure, previous, velocity, left, right, low, high, waves, first, second, third, prior, speed):
    cells, flat = pressure.shape
    half = cells // 2
    span = low.shape[1] - LANES
    near = span * 2 // 3
    steps = waves.shape[1] // cells
    edge, inner, own_tiles = span // LANES, near // LANES, flat // LANES

    for tile in range(own_tiles):
        lane = tile * LANES
        first[edge + tile, cells : 2 * cells, :] = pressure[:, lane : lane + LANES]
        prior[inner + tile, half : half + cells, :] = previous[:, lane : lane + LANES]
        speed[inner + tile, half : half + cells, :] = velocity[:, lane : lane + LANES].astype(F32)
    for tile in range(2 * edge + own_tiles):
        if tile < edge or tile >= edge + own_tiles:
            first[tile, :cells, :] = jnp.zeros((cells, LANES), F32)
            first[tile, 2 * cells :, :] = jnp.zeros((cells, LANES), F32)
    for tile in range(2 * inner + own_tiles):
        if tile < inner or tile >= inner + own_tiles:
            for ref in (prior, speed):
                ref[tile, :half, :] = jnp.zeros((half, LANES), F32)
                ref[tile, half + cells :, :] = jnp.zeros((half, LANES), F32)
    quarter = cells // 4
    places = layout(cells, flat, near)
    for part, top, far, side, tight in (
        (left, cells - half, half - quarter, 0, half - quarter),
        (right, 2 * cells, 2 * cells + half, half + cells, half + cells),
    ):
        scales = part[:half, places[5]].astype(F32) * (1.0 / TOP)
        unit = [jnp.broadcast_to(scales[:, 16 * k : 16 * k + 1], (half, LANES)) for k in range(6)]

        def tile_of(place, tile):
            start = places[place].start + tile * LANES
            return part[:, start : start + LANES].astype(F32)

        for tile in range(own_tiles):
            both = tile_of(0, tile)
            prior[inner + tile, side : side + half, :] = decode(both[:half], unit[1])
            speed[inner + tile, side : side + half, :] = both[half:]
        for tile in range(own_tiles // 2):
            both = tile_of(1, tile)
            first[edge + tile, top : top + half, :] = decode(both[:half], unit[0])
            first[edge + own_tiles // 2 + tile, top : top + half, :] = decode(both[half:], unit[0])
        for tile in range(own_tiles // 4):
            both = decode(tile_of(2, tile), jnp.concatenate([unit[0]] * 2, axis=0))
            for k in range(4):
                into = edge + k * (own_tiles // 4) + tile
                first[into, far : far + quarter, :] = both[k * quarter : (k + 1) * quarter]
        for tile in range(inner):
            both = tile_of(3, tile)
            first[edge - inner + tile, top : top + half, :] = decode(both[:half], unit[2])
            first[edge + own_tiles + tile, top : top + half, :] = decode(both[half:], unit[3])
        for tile in range(inner // 2):
            both = tile_of(4, tile)
            ends = (inner // 2 + tile, inner + own_tiles + tile)
            values = decode(both[:half], jnp.concatenate([unit[4][:quarter], unit[5][:quarter]], axis=0))
            for k, end in enumerate(ends):
                rows = slice(k * quarter, (k + 1) * quarter)
                prior[end, tight : tight + quarter, :] = values[rows]
                speed[end, tight : tight + quarter, :] = both[half:][rows]
    for part, start, cut, begin in ((low, 0, edge - inner, 0), (high, edge + own_tiles, 0, inner + own_tiles)):
        unit = units(part, 0, 3 * cells, span)
        for tile in range(edge):
            lanes = slice(tile * LANES, (tile + 1) * LANES)
            first[start + tile, cells : 2 * cells, :] = decode(part[:cells, lanes], unit[:cells])
            if cut <= tile < cut + inner:
                prior[begin + tile - cut, half : half + cells, :] = decode(
                    part[cells : 2 * cells, lanes], unit[cells : 2 * cells]
                )
                speed[begin + tile - cut, half : half + cells, :] = part[2 * cells :, lanes].astype(F32)

    line = lax.broadcasted_iota(jnp.int32, (LANES, LANES), 0)
    column = lax.broadcasted_iota(jnp.int32, (LANES, LANES), 1)
    gap = jnp.abs(line - column)
    band = jnp.zeros((LANES, LANES), F32)
    for reach in range(5):
        band = jnp.where(gap == reach, STENCIL[reach] * (3.0 if reach == 0 else 1.0), band)
    band = jnp.where(line // levels == column // levels, band, 0.0)
    band_upper, band_lower = split(band)
    bands = jnp.concatenate([band_upper, band_upper, band_lower], axis=0)
    front = lax.broadcasted_iota(jnp.int32, (1, LANES), 1) < levels
    count = 4
    for tile in list(range(edge - inner)) + list(range(edge + own_tiles + inner, 2 * edge + own_tiles)):
        second[tile, :, :] = jnp.zeros((3 * cells, LANES), F32)

    def advance(now, before, shift, tile_shift, later, out_row, top, rows, tile):
        tiles = [now[tile + step, top : top + rows, :] for step in range(-2, count + 2)]
        rolled = [pltpu.roll(value, levels, 1) for value in tiles]
        tall = jnp.concatenate(tiles[2 : 2 + count], axis=0)
        upper, lower = split(tall)
        deep = dot(jnp.concatenate([upper, lower, upper], axis=1), bands)
        for step in range(count):
            at = step + 2
            total = deep[step * rows : (step + 1) * rows]
            sides = [
                jnp.where(front, rolled[at] + rolled[at - 1], rolled[at + 1] + rolled[at]),
                tiles[at + 1] + tiles[at - 1],
                jnp.where(front, rolled[at + 1] + rolled[at - 2], rolled[at + 2] + rolled[at - 1]),
                tiles[at + 2] + tiles[at - 2],
            ]
            for reach in range(1, 5):
                value = sides[reach - 1] + now[tile + step, top + reach : top + reach + rows, :]
                value = value + now[tile + step, top - reach : top - reach + rows, :]
                total = total + STENCIL[reach] * value
            rate = speed[tile + step - (edge - inner), top - half : top - half + rows, :]
            past = before[tile + step - tile_shift, top - shift : top - shift + rows, :]
            following = 2.0 * tiles[at] - past + rate * total
            if later is None:
                waves[tile + step - edge, out_row : out_row + rows, :] = following
            else:
                later[tile + step, top : top + rows, :] = following

    chain = [(first, prior, half, edge - inner, second), (second, first, 0, 0, third), (third, second, 0, 0, None)]
    for step in range(steps):
        now, before, shift, tile_shift, later = chain[step]
        top, rows = (cells - half, 2 * cells) if later is not None else (cells, cells)
        margin = (steps - 1 - step) * (edge // steps)

        for tile in range(edge - margin, edge + own_tiles + margin, count):
            advance(now, before, shift, tile_shift, later, step * cells, top, rows, tile)
        if later is not None:
            for tile in range(own_tiles):
                waves[tile, step * cells : (step + 1) * cells, :] = later[edge + tile, cells : 2 * cells, :]


def call(kernel, outs, scratch, flops, *args):
    moved = sum(arg.size * arg.dtype.itemsize for arg in args)
    moved += sum(out.size * jnp.dtype(out.dtype).itemsize for out in outs)
    return pl.pallas_call(
        kernel,
        out_shape=outs,
        scratch_shapes=scratch,
        cost_estimate=pl.CostEstimate(flops=flops, bytes_accessed=moved, transcendentals=0),
        compiler_params=pltpu.CompilerParams(vmem_limit_bytes=VMEM_BYTES),
    )(*args)


def shape_of(*shape, dtype=F32):
    return jax.ShapeDtypeStruct(shape, dtype)


def body(pressure, previous, velocity, tucker_core, first_factor, second_factor, depth_factor):
    cells, flat = pressure.shape
    levels, depth = depth_factor.shape
    steps, rank, core_flat = tucker_core.shape
    local_second = core_flat // depth
    lines = steps * cells
    count_x, count_y = lax.axis_size("gx"), lax.axis_size("gy")
    chips = count_x // 2
    span = 4 * steps * levels
    near = span * 2 // 3
    groups_pad = (core_flat // LANES + 7) // 8 * 8
    lines_pad = (lines * depth // LANES + 7) // 8 * 8

    across = [[(i, 2 * ((i // 2) ^ distance) + i % 2) for i in range(count_x)] for distance in range(1, chips)]
    factors = [lax.ppermute(first_factor, "gx", route) for route in across[::-1]]
    other = lax.ppermute(tucker_core, "gx", [(i, i + 1 - 2 * (i % 2)) for i in range(count_x)])
    core_near, factor_near = call(
        lift_kernel,
        [shape_of(*array.shape, dtype=BF16) for array in (tucker_core, first_factor)],
        [],
        1000,
        tucker_core,
        first_factor,
    )
    mine, *sends = call(
        functools.partial(project_kernel, chips),
        [shape_of(lines, core_flat)] + [message(lines, core_flat)] * (chips - 1),
        [pltpu.VMEM((chips - 1, lines, core_flat), F32)],
        4 * lines * chips * rank * core_flat,
        core_near,
        other,
        *factors,
        factor_near,
    )
    received = [lax.ppermute(send, "gx", route) for send, route in zip(sends, across)]
    pressure_later, _ = lax.optimization_barrier((pressure, mine))
    own, up, down, second_near = call(
        pack_kernel,
        [shape_of(3 * cells, flat + LANES, dtype=BF16)]
        + [shape_of(3 * cells, span + LANES, dtype=BF16)] * 2
        + [shape_of(*second_factor.shape, dtype=BF16)],
        [],
        10 * cells * flat,
        pressure_later,
        previous,
        velocity,
        second_factor,
    )
    low = lax.ppermute(up, "gy", [(i, i + 1) for i in range(count_y - 1)])
    high = lax.ppermute(down, "gy", [(i + 1, i) for i in range(count_y - 1)])

    ahead, behind = call(
        edge_kernel,
        [shape_of(cells, layout(cells, flat, near)[-1].stop, dtype=BF16)] * 2,
        [],
        1000,
        own,
        low,
        high,
    )

    mine, ahead, behind = lax.optimization_barrier((mine, ahead, behind))
    (codes,) = call(
        functools.partial(gather_kernel, depth, steps),
        [message(local_second, lines * depth)],
        [pltpu.VMEM((lines * groups_pad, LANES), F32), pltpu.VMEM((local_second, lines * depth), F32)],
        30 * chips * lines * core_flat,
        mine,
        *received,
    )
    codes, ahead, behind = lax.optimization_barrier((codes, ahead, behind))

    def far(distance):
        return lax.ppermute(codes, "gy", [(i, i ^ distance) for i in range(count_y)])

    if count_y == 4:
        distances = (0, 2, 1)
        blocks = [codes, far(2), far(1)]
        codes_later, blocks = lax.optimization_barrier((codes, blocks))
        last = [
            lax.ppermute(codes_later, "gy", [(1, 2), (2, 1)]),
            lax.ppermute(blocks[1], "gy", [(1, 0), (2, 3)]),
        ]
    else:
        distances = tuple(range(count_y - 1))
        blocks = [codes] + [far(distance) for distance in distances[1:]]
        last = [far(count_y - 1)]

    left = lax.ppermute(ahead, "gx", [(i, i + 1) for i in range(count_x - 1)])
    right = lax.ppermute(behind, "gx", [(i + 1, i) for i in range(count_x - 1)])
    (waves,) = call(
        functools.partial(wave_kernel, levels),
        [shape_of(flat // LANES, lines, LANES)],
        [pltpu.VMEM(((flat + 2 * span) // LANES, 3 * cells, LANES), F32)] * 3
        + [pltpu.VMEM(((flat + 2 * near) // LANES, 2 * cells, LANES), F32)] * 2,
        150 * lines * flat,
        pressure,
        previous,
        velocity,
        left,
        right,
        low,
        high,
    )
    cells_y = second_factor.shape[0]
    (mixed,) = call(
        functools.partial(early_kernel, depth, distances),
        [shape_of(cells_y, lines * depth)],
        [pltpu.VMEM((2 * (count_y - 1), local_second, lines * depth), BF16)],
        4 * cells_y * count_y * local_second * lines * depth,
        second_near,
        *blocks,
    )
    (image,) = call(
        functools.partial(image_kernel, depth, steps, count_y - 1),
        [shape_of(cells, flat)],
        [
            pltpu.VMEM((2, local_second, lines * depth), BF16),
            pltpu.VMEM((cells_y, lines * depth), F32),
            pltpu.VMEM((cells_y * lines_pad, LANES), F32),
        ],
        4 * cells_y * local_second * lines * depth,
        second_near,
        depth_factor,
        waves,
        mixed,
        *last,
    )
    return image


def solution(mesh):
    placed = (
        P("gx", "gy"),
        P("gx", "gy"),
        P("gx", "gy"),
        P(None, "gx", "gy"),
        P("gx", None),
        P("gy", None),
        P(),
    )
    return jax.shard_map(body, mesh=mesh, in_specs=placed, out_specs=P("gx", "gy"), check_vma=False)
```

```python
import functools

import jax
import jax.numpy as jnp
from jax import lax
from jax.experimental import pallas as pl
from jax.experimental.pallas import tpu as pltpu
from jax.sharding import PartitionSpec as P

STENCIL = (-205.0 / 72.0, 8.0 / 5.0, -1.0 / 5.0, 8.0 / 315.0, -1.0 / 560.0)
F32 = jnp.float32
BF16 = jnp.bfloat16
LANES = 128
TOP = 2.0**7.75
VMEM_BYTES = 48 * 1024 * 1024


def scale_of(peak):
    return (jnp.maximum(peak, 1e-30) * (1.0 + 2.0**-7)).astype(BF16).astype(F32)


def raise_power(ratio):
    power = ratio * ratio
    power = power * power
    power = power * power
    power = power * power
    return jnp.where(ratio < 0.0, -power, power).astype(BF16)


def encode(values):
    scale = scale_of(jnp.max(jnp.abs(values), axis=(0, 1), keepdims=True))
    return raise_power(values * (TOP / scale)), scale


def decode(codes, unit):
    codes = codes.astype(F32)
    size = jnp.maximum(jnp.abs(codes), 2.0**-126)
    for _ in range(4):
        size = lax.rsqrt(size)
    size = size * unit
    return jnp.where(codes < 0.0, -size, jnp.where(codes > 0.0, size, 0.0))


def stride_of(rows):
    return (rows + 15) // 16 * 16


def message(rows, flat):
    return shape_of(flat // LANES * stride_of(rows) + 16, LANES, dtype=BF16)


def put_message(ref, source):
    rows, flat = source.shape
    stride = stride_of(rows)
    peak = jnp.max(jnp.abs(source[...]), axis=0, keepdims=True)
    scale = scale_of(jnp.max(peak, axis=1, keepdims=True))
    factor = TOP / scale
    for tile in range(flat // LANES):
        for start, count in pieces(rows):
            into = tile * stride + start
            ref[into : into + count, :] = raise_power(
                source[start : start + count, tile * LANES : (tile + 1) * LANES] * factor
            )
    ref[flat // LANES * stride :, :] = jnp.broadcast_to(scale, (16, LANES)).astype(BF16)


def unit_of(ref):
    return ref[ref.shape[0] - 16 :, :].astype(F32)[:8] * (1.0 / TOP)


def units(ref, row, rows, lane):
    return ref[row : row + rows, lane : lane + LANES].astype(F32) * (1.0 / TOP)


def pieces(rows):
    return [(start, 16) for start in range(0, rows, 16)] if rows % 16 == 0 else [(0, rows)]


def split(values):
    upper = values.astype(BF16)
    return upper, (values - upper.astype(F32)).astype(BF16)


def dot(left, right):
    return jnp.dot(left, right, preferred_element_type=F32)


def swap_groups(tiles, depth):
    group = lax.broadcasted_iota(jnp.int32, (1, LANES), 1) // depth
    low_half, even = group < 2, group % 2 == 0

    def exchange(left, right, distance, keep):
        return (
            jnp.where(keep, left, pltpu.roll(right, distance, 1)),
            jnp.where(keep, pltpu.roll(left, LANES - distance, 1), right),
        )

    first, third = exchange(tiles[0], tiles[2], 2 * depth, low_half)
    second, fourth = exchange(tiles[1], tiles[3], 2 * depth, low_half)
    first, second = exchange(first, second, depth, even)
    third, fourth = exchange(third, fourth, depth, even)
    return first, second, third, fourth


def project_kernel(chips, core, other, *rest):
    factors, mine, sends, (partial,) = rest[:chips], rest[chips], rest[chips + 1 : -1], rest[-1:]
    steps, rank, flat = core.shape
    lines = mine.shape[0]
    cells = lines // steps
    place = lax.axis_index("gx")
    factor = jnp.concatenate([ref[...] for ref in factors[::-1]], axis=0)
    offset = lax.broadcasted_iota(jnp.int32, (factor.shape[1], rank), 0) - lax.broadcasted_iota(
        jnp.int32, (factor.shape[1], rank), 1
    )
    own_rows, other_rows = [
        dot(factor, jnp.where(offset == owner * rank, 1.0, 0.0).astype(BF16)).astype(BF16)
        for owner in (place, place + 1 - 2 * (place % 2))
    ]
    width = 512 if flat % 512 == 0 else 256
    for step in range(steps):
        for low in range(0, flat, width):
            lanes = slice(low, low + width)
            value = dot(own_rows, core[step, :, lanes]) + dot(other_rows, other[step, :, lanes])
            mine[step * cells : (step + 1) * cells, lanes] = value[:cells]
            for distance in range(1, chips):
                partial[distance - 1, step * cells : (step + 1) * cells, lanes] = value[
                    distance * cells : (distance + 1) * cells
                ]
    for distance in range(1, chips):
        put_message(sends[distance - 1], partial.at[distance - 1])


def gather_kernel(depth, steps, mine, *rest):
    received, (codes, spread, turned) = rest[:-3], rest[-3:]
    lines, flat = mine.shape
    cells = lines // steps
    quads = LANES // depth
    groups = flat // LANES
    pad = spread.shape[0] // lines
    scales = [unit_of(ref) for ref in received]
    for start, count in pieces(lines):
        for group in range(groups):
            lanes = slice(group * LANES, (group + 1) * LANES)
            value = mine[start : start + count, lanes]
            for ref, unit in zip(received, scales):
                into = group * stride_of(lines) + start
                value = value + decode(ref[into : into + count, :], unit[:1])
            for row in range(0, count, 8):
                spread[pl.ds((start + row) * pad + group, 8, stride=pad), :] = value[row : row + 8]
    rest_x = cells // quads
    for line in range(steps * rest_x):
        base = line // rest_x * cells + line % rest_x
        for top in range(0, groups, 8):
            count = min(8, groups - top)
            tiles = [
                spread[(base + i * rest_x) * pad + top : (base + i * rest_x) * pad + top + 8, :] for i in range(quads)
            ]
            for j, tile in enumerate(swap_groups(tiles, depth)):
                turned[j * groups + top : j * groups + top + count, line * LANES : (line + 1) * LANES] = tile[:count]
    put_message(codes, turned)


def contract_second(depth, second, blocks, total, earlier, terms):
    rows, flat = terms.shape[1], total.shape[1]
    quads = LANES // depth
    ranks = second.shape[1]
    place = lax.axis_index("gy")
    inner = (place == 1) | (place == 2)
    width = 512 if flat % 512 == 0 else 256
    columns = []
    inside = lax.broadcasted_iota(jnp.int32, (ranks, rows), 1)
    inside = inside % (rows // quads) * quads + inside // (rows // quads)
    offset = lax.broadcasted_iota(jnp.int32, (ranks, rows), 0) - inside
    for at, (distance, *options) in enumerate(blocks):
        owner = jnp.bitwise_xor(place, distance)
        chosen = jnp.where(offset == owner * rows, 1.0, 0.0).astype(BF16)
        columns.append(dot(second[...], chosen).astype(BF16))
        unit = unit_of(options[0])[:1]
        if len(options) > 1:
            unit = jnp.where(inner, unit, unit_of(options[1])[:1])
        for low in range(0, flat, LANES):
            for start, count in pieces(rows):
                into = low // LANES * stride_of(rows) + start
                codes = options[0][into : into + count, :].astype(F32)
                if len(options) > 1:
                    codes = jnp.where(inner, codes, options[1][into : into + count, :].astype(F32))
                high, rest_of = split(decode(codes, unit))
                terms[2 * at, start : start + count, low : low + LANES] = high
                terms[2 * at + 1, start : start + count, low : low + LANES] = rest_of
    together = len(blocks) if rows % 16 == 0 else 1
    for low in range(0, flat, width):
        value = None if earlier is None else earlier[:, low : low + width]
        for at in range(0, len(blocks), together):
            left = jnp.concatenate([columns[k // 2] for k in range(2 * at, 2 * (at + together))], axis=1)
            right = [terms[k, :, low : low + width] for k in range(2 * at, 2 * (at + together))]
            if rows % 16 == 0:
                products = [dot(left, jnp.concatenate(right, axis=0))]
            else:
                products = [dot(columns[at], part) for part in right]
            for product in products:
                value = product if value is None else value + product
        total[:, low : low + width] = value


def early_kernel(depth, distances, second, *rest):
    blocks, (total, terms) = rest[:-2], rest[-2:]
    contract_second(depth, second, list(zip(distances, blocks)), total, None, terms)


def image_kernel(depth, steps, distance, second, depth_factor, waves, earlier, *rest):
    blocks, (image, terms, mixed, spread) = rest[:-4], rest[-4:]
    contract_second(depth, second, [(distance, *blocks)], mixed, earlier, terms)
    flat = mixed.shape[1]
    cells = image.shape[0]
    levels = depth_factor.shape[0]
    quads = LANES // depth
    groups = flat // LANES
    pad = spread.shape[0] // mixed.shape[0]
    for row in range(0, mixed.shape[0], 8):
        for group in range(groups):
            spread[pl.ds(row * pad + group, 8, stride=pad), :] = mixed[
                row : row + 8, group * LANES : (group + 1) * LANES
            ]
    square = jnp.concatenate([depth_factor[...].astype(F32)] * quads, axis=1)
    square = jnp.concatenate([square] * quads, axis=0)
    shape = square.shape
    same = lax.broadcasted_iota(jnp.int32, shape, 0) // levels == lax.broadcasted_iota(jnp.int32, shape, 1) // depth
    square = jnp.where(same, square, 0.0).astype(BF16)
    square = jnp.concatenate([square, square], axis=1)
    tiles = quads * levels // LANES
    contract = (((1,), (1,)), ((), ()))
    rest_x = cells // quads
    many = mixed.shape[0] // quads
    batch = 4 if many % 4 == 0 else 1
    for first in range(0, many, batch):
        stack = []
        for quad in range(first, first + batch):
            turned = [
                swap_groups(
                    [
                        spread[(quad * quads + j) * pad + top : (quad * quads + j) * pad + top + 8, :]
                        for j in range(quads)
                    ],
                    depth,
                )
                for top in range(0, pad, 8)
            ]
            stack += [piece[i] for i in range(quads) for piece in turned]
        high, rest_of = split(jnp.concatenate(stack, axis=0))
        source = lax.dot_general(
            jnp.concatenate([high, rest_of], axis=1), square, contract, preferred_element_type=F32
        )
        for quad in range(first, first + batch):
            base = (quad - first) * quads * pad
            for tile in range(tiles):
                at = quad * tiles + tile
                lanes = slice(tile * LANES, (tile + 1) * LANES)
                total = None
                for step in range(steps):
                    value = jnp.concatenate(
                        [
                            source[base + i * pad + step * rest_x : base + i * pad + (step + 1) * rest_x, lanes]
                            for i in range(quads)
                        ],
                        axis=0,
                    )
                    value = value * waves[at, step * cells : (step + 1) * cells, :]
                    total = value if total is None else total + value
                image[:, at * LANES : (at + 1) * LANES] = total


def lift_kernel(core, factor, core_near, factor_near):
    core_near[...] = core[...]
    factor_near[...] = factor[...]


def pack_kernel(pressure, previous, velocity, second, own, up, down, second_near):
    second_near[...] = second[...]
    cells, flat = pressure.shape
    span = up.shape[1] - LANES
    for row, part in ((0, pressure), (cells, previous)):
        codes, scale = encode(part[...])
        own[row : row + cells, :flat] = codes
        own[row : row + cells, flat:] = jnp.broadcast_to(scale, (cells, LANES)).astype(BF16)
    own[2 * cells :, :flat] = velocity[...]
    own[2 * cells :, flat:] = jnp.zeros((cells, LANES), BF16)
    up[:, :span] = own[:, flat - span : flat]
    down[:, :span] = own[:, :span]
    up[:, span:] = own[:, flat:]
    down[:, span:] = own[:, flat:]


def layout(cells, flat, near):
    widths = (flat, flat // 2, flat // 4, near, near // 2, LANES)
    starts = [sum(widths[:k]) for k in range(len(widths))]
    return [slice(start, start + width) for start, width in zip(starts, widths)]


def edge_kernel(own, low, high, ahead, behind):
    flat = own.shape[1] - LANES
    span = low.shape[1] - LANES
    near = span * 2 // 3
    cells = own.shape[0] // 3
    half, quarter = cells // 2, cells // 4
    places = layout(cells, flat, near)
    lane = lax.broadcasted_iota(jnp.int32, (cells, LANES), 1) // 16
    scales = jnp.zeros((cells, LANES), F32)
    for k, (part, row) in enumerate(((own, 0), (own, cells), (low, 0), (high, 0), (low, cells), (high, cells))):
        width = part.shape[1]
        scales = jnp.where(lane == k, part[row : row + cells, width - LANES :].astype(F32), scales)
    pressure = own[:cells, :flat].astype(F32)
    previous = own[cells : 2 * cells, :flat].astype(F32)
    speed = own[2 * cells :, :flat].astype(F32)
    below, above = low[:, span - near : span].astype(F32), high[:, :near].astype(F32)
    for ref, first, next_first in ((ahead, half, half - quarter), (behind, 0, half)):
        rows = slice(first, first + half)
        close = half if first > 0 else 0
        tight = slice(cells - quarter, cells) if first > 0 else slice(0, quarter)
        blocks = [
            [previous[rows], speed[rows]],
            [pressure[rows, : flat // 2], pressure[rows, flat // 2 :]],
            [pressure[next_first : next_first + quarter, k * (flat // 4) : (k + 1) * (flat // 4)] for k in range(4)],
            [below[close : close + half], above[close : close + half]],
            [
                below[cells + tight.start : cells + tight.stop, near // 2 :],
                above[cells + tight.start : cells + tight.stop, : near // 2],
                below[2 * cells + tight.start : 2 * cells + tight.stop, near // 2 :],
                above[2 * cells + tight.start : 2 * cells + tight.stop, : near // 2],
            ],
            [scales],
        ]
        for place, block in zip(places, blocks):
            ref[:, place] = jnp.concatenate(block, axis=0).astype(BF16)


def wave_kernel(levels, pressure, previous, velocity, left, right, low, high, waves, first, second, third, prior, speed):
    cells, flat = pressure.shape
    half = cells // 2
    span = low.shape[1] - LANES
    near = span * 2 // 3
    steps = waves.shape[1] // cells
    edge, inner, own_tiles = span // LANES, near // LANES, flat // LANES

    for tile in range(own_tiles):
        lane = tile * LANES
        first[edge + tile, cells : 2 * cells, :] = pressure[:, lane : lane + LANES]
        prior[inner + tile, half : half + cells, :] = previous[:, lane : lane + LANES]
        speed[inner + tile, half : half + cells, :] = velocity[:, lane : lane + LANES].astype(F32)
    for tile in range(2 * edge + own_tiles):
        if tile < edge or tile >= edge + own_tiles:
            first[tile, :cells, :] = jnp.zeros((cells, LANES), F32)
            first[tile, 2 * cells :, :] = jnp.zeros((cells, LANES), F32)
    for tile in range(2 * inner + own_tiles):
        if tile < inner or tile >= inner + own_tiles:
            for ref in (prior, speed):
                ref[tile, :half, :] = jnp.zeros((half, LANES), F32)
                ref[tile, half + cells :, :] = jnp.zeros((half, LANES), F32)
    quarter = cells // 4
    places = layout(cells, flat, near)
    for part, top, far, side, tight in (
        (left, cells - half, half - quarter, 0, half - quarter),
        (right, 2 * cells, 2 * cells + half, half + cells, half + cells),
    ):
        scales = part[:half, places[5]].astype(F32) * (1.0 / TOP)
        unit = [jnp.broadcast_to(scales[:, 16 * k : 16 * k + 1], (half, LANES)) for k in range(6)]

        def tile_of(place, tile):
            start = places[place].start + tile * LANES
            return part[:, start : start + LANES].astype(F32)

        for tile in range(own_tiles):
            both = tile_of(0, tile)
            prior[inner + tile, side : side + half, :] = decode(both[:half], unit[1])
            speed[inner + tile, side : side + half, :] = both[half:]
        for tile in range(own_tiles // 2):
            both = tile_of(1, tile)
            first[edge + tile, top : top + half, :] = decode(both[:half], unit[0])
            first[edge + own_tiles // 2 + tile, top : top + half, :] = decode(both[half:], unit[0])
        for tile in range(own_tiles // 4):
            both = decode(tile_of(2, tile), jnp.concatenate([unit[0]] * 2, axis=0))
            for k in range(4):
                into = edge + k * (own_tiles // 4) + tile
                first[into, far : far + quarter, :] = both[k * quarter : (k + 1) * quarter]
        for tile in range(inner):
            both = tile_of(3, tile)
            first[edge - inner + tile, top : top + half, :] = decode(both[:half], unit[2])
            first[edge + own_tiles + tile, top : top + half, :] = decode(both[half:], unit[3])
        for tile in range(inner // 2):
            both = tile_of(4, tile)
            ends = (inner // 2 + tile, inner + own_tiles + tile)
            values = decode(both[:half], jnp.concatenate([unit[4][:quarter], unit[5][:quarter]], axis=0))
            for k, end in enumerate(ends):
                rows = slice(k * quarter, (k + 1) * quarter)
                prior[end, tight : tight + quarter, :] = values[rows]
                speed[end, tight : tight + quarter, :] = both[half:][rows]
    for part, start, cut, begin in ((low, 0, edge - inner, 0), (high, edge + own_tiles, 0, inner + own_tiles)):
        unit = units(part, 0, 3 * cells, span)
        for tile in range(edge):
            lanes = slice(tile * LANES, (tile + 1) * LANES)
            first[start + tile, cells : 2 * cells, :] = decode(part[:cells, lanes], unit[:cells])
            if cut <= tile < cut + inner:
                prior[begin + tile - cut, half : half + cells, :] = decode(
                    part[cells : 2 * cells, lanes], unit[cells : 2 * cells]
                )
                speed[begin + tile - cut, half : half + cells, :] = part[2 * cells :, lanes].astype(F32)

    line = lax.broadcasted_iota(jnp.int32, (LANES, LANES), 0)
    column = lax.broadcasted_iota(jnp.int32, (LANES, LANES), 1)
    gap = jnp.abs(line - column)
    band = jnp.zeros((LANES, LANES), F32)
    for reach in range(5):
        band = jnp.where(gap == reach, STENCIL[reach] * (3.0 if reach == 0 else 1.0), band)
    band = jnp.where(line // levels == column // levels, band, 0.0)
    band_upper, band_lower = split(band)
    bands = jnp.concatenate([band_upper, band_upper, band_lower], axis=0)
    front = lax.broadcasted_iota(jnp.int32, (1, LANES), 1) < levels
    count = 4
    for tile in list(range(edge - inner)) + list(range(edge + own_tiles + inner, 2 * edge + own_tiles)):
        second[tile, :, :] = jnp.zeros((3 * cells, LANES), F32)

    def advance(now, before, shift, tile_shift, later, out_row, top, rows, tile):
        tiles = [now[tile + step, top : top + rows, :] for step in range(-2, count + 2)]
        rolled = [pltpu.roll(value, levels, 1) for value in tiles]
        tall = jnp.concatenate(tiles[2 : 2 + count], axis=0)
        upper, lower = split(tall)
        deep = dot(jnp.concatenate([upper, lower, upper], axis=1), bands)
        for step in range(count):
            at = step + 2
            total = deep[step * rows : (step + 1) * rows]
            sides = [
                jnp.where(front, rolled[at] + rolled[at - 1], rolled[at + 1] + rolled[at]),
                tiles[at + 1] + tiles[at - 1],
                jnp.where(front, rolled[at + 1] + rolled[at - 2], rolled[at + 2] + rolled[at - 1]),
                tiles[at + 2] + tiles[at - 2],
            ]
            for reach in range(1, 5):
                value = sides[reach - 1] + now[tile + step, top + reach : top + reach + rows, :]
                value = value + now[tile + step, top - reach : top - reach + rows, :]
                total = total + STENCIL[reach] * value
            rate = speed[tile + step - (edge - inner), top - half : top - half + rows, :]
            past = before[tile + step - tile_shift, top - shift : top - shift + rows, :]
            following = 2.0 * tiles[at] - past + rate * total
            if later is None:
                waves[tile + step - edge, out_row : out_row + rows, :] = following
            else:
                later[tile + step, top : top + rows, :] = following

    chain = [(first, prior, half, edge - inner, second), (second, first, 0, 0, third), (third, second, 0, 0, None)]
    for step in range(steps):
        now, before, shift, tile_shift, later = chain[step]
        top, rows = (cells - half, 2 * cells) if later is not None else (cells, cells)
        margin = (steps - 1 - step) * (edge // steps)

        for tile in range(edge - margin, edge + own_tiles + margin, count):
            advance(now, before, shift, tile_shift, later, step * cells, top, rows, tile)
        if later is not None:
            for tile in range(own_tiles):
                waves[tile, step * cells : (step + 1) * cells, :] = later[edge + tile, cells : 2 * cells, :]


def call(kernel, outs, scratch, flops, *args):
    moved = sum(arg.size * arg.dtype.itemsize for arg in args)
    moved += sum(out.size * jnp.dtype(out.dtype).itemsize for out in outs)
    return pl.pallas_call(
        kernel,
        out_shape=outs,
        scratch_shapes=scratch,
        cost_estimate=pl.CostEstimate(flops=flops, bytes_accessed=moved, transcendentals=0),
        compiler_params=pltpu.CompilerParams(vmem_limit_bytes=VMEM_BYTES),
    )(*args)


def shape_of(*shape, dtype=F32):
    return jax.ShapeDtypeStruct(shape, dtype)


def body(pressure, previous, velocity, tucker_core, first_factor, second_factor, depth_factor):
    cells, flat = pressure.shape
    levels, depth = depth_factor.shape
    steps, rank, core_flat = tucker_core.shape
    local_second = core_flat // depth
    lines = steps * cells
    count_x, count_y = lax.axis_size("gx"), lax.axis_size("gy")
    chips = count_x // 2
    span = 4 * steps * levels
    near = span * 2 // 3
    groups_pad = (core_flat // LANES + 7) // 8 * 8
    lines_pad = (lines * depth // LANES + 7) // 8 * 8

    across = [[(i, 2 * ((i // 2) ^ distance) + i % 2) for i in range(count_x)] for distance in range(1, chips)]
    factors = [lax.ppermute(first_factor, "gx", route) for route in across[::-1]]
    other = lax.ppermute(tucker_core, "gx", [(i, i + 1 - 2 * (i % 2)) for i in range(count_x)])
    core_near, factor_near = call(
        lift_kernel,
        [shape_of(*array.shape, dtype=BF16) for array in (tucker_core, first_factor)],
        [],
        1000,
        tucker_core,
        first_factor,
    )
    mine, *sends = call(
        functools.partial(project_kernel, chips),
        [shape_of(lines, core_flat)] + [message(lines, core_flat)] * (chips - 1),
        [pltpu.VMEM((chips - 1, lines, core_flat), F32)],
        4 * lines * chips * rank * core_flat,
        core_near,
        other,
        *factors,
        factor_near,
    )
    received = [lax.ppermute(send, "gx", route) for send, route in zip(sends, across)]
    pressure_later, _ = lax.optimization_barrier((pressure, mine))
    own, up, down, second_near = call(
        pack_kernel,
        [shape_of(3 * cells, flat + LANES, dtype=BF16)]
        + [shape_of(3 * cells, span + LANES, dtype=BF16)] * 2
        + [shape_of(*second_factor.shape, dtype=BF16)],
        [],
        10 * cells * flat,
        pressure_later,
        previous,
        velocity,
        second_factor,
    )
    low = lax.ppermute(up, "gy", [(i, i + 1) for i in range(count_y - 1)])
    high = lax.ppermute(down, "gy", [(i + 1, i) for i in range(count_y - 1)])

    ahead, behind = call(
        edge_kernel,
        [shape_of(cells, layout(cells, flat, near)[-1].stop, dtype=BF16)] * 2,
        [],
        1000,
        own,
        low,
        high,
    )

    mine, ahead, behind = lax.optimization_barrier((mine, ahead, behind))
    (codes,) = call(
        functools.partial(gather_kernel, depth, steps),
        [message(local_second, lines * depth)],
        [pltpu.VMEM((lines * groups_pad, LANES), F32), pltpu.VMEM((local_second, lines * depth), F32)],
        30 * chips * lines * core_flat,
        mine,
        *received,
    )
    codes, ahead, behind = lax.optimization_barrier((codes, ahead, behind))

    def far(distance):
        return lax.ppermute(codes, "gy", [(i, i ^ distance) for i in range(count_y)])

    if count_y == 4:
        distances = (0, 2, 1)
        blocks = [codes, far(2), far(1)]
        place = lax.axis_index("gy")
        passed = jnp.where((place == 1) | (place == 2), blocks[1], blocks[2])
        last = [lax.ppermute(passed, "gy", [(0, 2), (3, 1), (1, 0), (2, 3)])]
    else:
        distances = tuple(range(count_y - 1))
        blocks = [codes] + [far(distance) for distance in distances[1:]]
        last = [far(count_y - 1)]

    left = lax.ppermute(ahead, "gx", [(i, i + 1) for i in range(count_x - 1)])
    right = lax.ppermute(behind, "gx", [(i + 1, i) for i in range(count_x - 1)])
    (waves,) = call(
        functools.partial(wave_kernel, levels),
        [shape_of(flat // LANES, lines, LANES)],
        [pltpu.VMEM(((flat + 2 * span) // LANES, 3 * cells, LANES), F32)] * 3
        + [pltpu.VMEM(((flat + 2 * near) // LANES, 2 * cells, LANES), F32)] * 2,
        150 * lines * flat,
        pressure,
        previous,
        velocity,
        left,
        right,
        low,
        high,
    )
    cells_y = second_factor.shape[0]
    (mixed,) = call(
        functools.partial(early_kernel, depth, distances),
        [shape_of(cells_y, lines * depth)],
        [pltpu.VMEM((2 * (count_y - 1), local_second, lines * depth), BF16)],
        4 * cells_y * count_y * local_second * lines * depth,
        second_near,
        *blocks,
    )
    (image,) = call(
        functools.partial(image_kernel, depth, steps, count_y - 1),
        [shape_of(cells, flat)],
        [
            pltpu.VMEM((2, local_second, lines * depth), BF16),
            pltpu.VMEM((cells_y, lines * depth), F32),
            pltpu.VMEM((cells_y * lines_pad, LANES), F32),
        ],
        4 * cells_y * local_second * lines * depth,
        second_near,
        depth_factor,
        waves,
        mixed,
        *last,
    )
    return image


def solution(mesh):
    placed = (
        P("gx", "gy"),
        P("gx", "gy"),
        P("gx", "gy"),
        P(None, "gx", "gy"),
        P("gx", None),
        P("gy", None),
        P(),
    )
    return jax.shard_map(body, mesh=mesh, in_specs=placed, out_specs=P("gx", "gy"), check_vma=False)
```

```python
import functools

import jax
import jax.numpy as jnp
from jax import lax
from jax.experimental import pallas as pl
from jax.experimental.pallas import tpu as pltpu
from jax.sharding import PartitionSpec as P

STENCIL = (-205.0 / 72.0, 8.0 / 5.0, -1.0 / 5.0, 8.0 / 315.0, -1.0 / 560.0)
F32 = jnp.float32
BF16 = jnp.bfloat16
LANES = 128
TOP = 2.0**7.75
VMEM_BYTES = 48 * 1024 * 1024


def scale_of(peak):
    return (jnp.maximum(peak, 1e-30) * (1.0 + 2.0**-7)).astype(BF16).astype(F32)


def raise_power(ratio):
    power = ratio * ratio
    power = power * power
    power = power * power
    power = power * power
    return jnp.where(ratio < 0.0, -power, power).astype(BF16)


def encode(values):
    scale = scale_of(jnp.max(jnp.abs(values), axis=(0, 1), keepdims=True))
    return raise_power(values * (TOP / scale)), scale


def decode(codes, unit):
    codes = codes.astype(F32)
    size = jnp.maximum(jnp.abs(codes), 2.0**-126)
    for _ in range(4):
        size = lax.rsqrt(size)
    size = size * unit
    return jnp.where(codes < 0.0, -size, jnp.where(codes > 0.0, size, 0.0))


def stride_of(rows):
    return (rows + 15) // 16 * 16


def message(rows, flat):
    return shape_of(flat // LANES * stride_of(rows) + 16, LANES, dtype=BF16)


def put_message(ref, source):
    rows, flat = source.shape
    stride = stride_of(rows)
    peak = jnp.max(jnp.abs(source[...]), axis=0, keepdims=True)
    scale = scale_of(jnp.max(peak, axis=1, keepdims=True))
    factor = TOP / scale
    for tile in range(flat // LANES):
        for start, count in pieces(rows):
            into = tile * stride + start
            ref[into : into + count, :] = raise_power(
                source[start : start + count, tile * LANES : (tile + 1) * LANES] * factor
            )
    ref[flat // LANES * stride :, :] = jnp.broadcast_to(scale, (16, LANES)).astype(BF16)


def unit_of(ref):
    return ref[ref.shape[0] - 16 :, :].astype(F32)[:8] * (1.0 / TOP)


def units(ref, row, rows, lane):
    return ref[row : row + rows, lane : lane + LANES].astype(F32) * (1.0 / TOP)


def pieces(rows):
    return [(start, 16) for start in range(0, rows, 16)] if rows % 16 == 0 else [(0, rows)]


def split(values):
    upper = values.astype(BF16)
    return upper, (values - upper.astype(F32)).astype(BF16)


def dot(left, right):
    return jnp.dot(left, right, preferred_element_type=F32)


def swap_groups(tiles, depth):
    group = lax.broadcasted_iota(jnp.int32, (1, LANES), 1) // depth
    low_half, even = group < 2, group % 2 == 0

    def exchange(left, right, distance, keep):
        return (
            jnp.where(keep, left, pltpu.roll(right, distance, 1)),
            jnp.where(keep, pltpu.roll(left, LANES - distance, 1), right),
        )

    first, third = exchange(tiles[0], tiles[2], 2 * depth, low_half)
    second, fourth = exchange(tiles[1], tiles[3], 2 * depth, low_half)
    first, second = exchange(first, second, depth, even)
    third, fourth = exchange(third, fourth, depth, even)
    return first, second, third, fourth


def project_kernel(chips, core, other, *rest):
    factors, mine, sends, (partial,) = rest[:chips], rest[chips], rest[chips + 1 : -1], rest[-1:]
    steps, rank, flat = core.shape
    lines = mine.shape[0]
    cells = lines // steps
    place = lax.axis_index("gx")
    factor = jnp.concatenate([ref[...] for ref in factors[::-1]], axis=0)
    offset = lax.broadcasted_iota(jnp.int32, (factor.shape[1], rank), 0) - lax.broadcasted_iota(
        jnp.int32, (factor.shape[1], rank), 1
    )
    own_rows, other_rows = [
        dot(factor, jnp.where(offset == owner * rank, 1.0, 0.0).astype(BF16)).astype(BF16)
        for owner in (place, place + 1 - 2 * (place % 2))
    ]
    width = 512 if flat % 512 == 0 else 256
    for step in range(steps):
        for low in range(0, flat, width):
            lanes = slice(low, low + width)
            value = dot(own_rows, core[step, :, lanes]) + dot(other_rows, other[step, :, lanes])
            mine[step * cells : (step + 1) * cells, lanes] = value[:cells]
            for distance in range(1, chips):
                partial[distance - 1, step * cells : (step + 1) * cells, lanes] = value[
                    distance * cells : (distance + 1) * cells
                ]
    for distance in range(1, chips):
        put_message(sends[distance - 1], partial.at[distance - 1])


def presum_kernel(mine, part, total):
    lines, flat = mine.shape
    unit = unit_of(part)[:1]
    for group in range(flat // LANES):
        lanes = slice(group * LANES, (group + 1) * LANES)
        for start, count in pieces(lines):
            into = group * stride_of(lines) + start
            total[start : start + count, lanes] = mine[start : start + count, lanes] + decode(
                part[into : into + count, :], unit
            )


def gather_kernel(depth, steps, mine, *rest):
    received, (codes, spread, turned) = rest[:-3], rest[-3:]
    lines, flat = mine.shape
    cells = lines // steps
    quads = LANES // depth
    groups = flat // LANES
    pad = spread.shape[0] // lines
    scales = [unit_of(ref) for ref in received]
    for start, count in pieces(lines):
        for group in range(groups):
            lanes = slice(group * LANES, (group + 1) * LANES)
            value = mine[start : start + count, lanes]
            for ref, unit in zip(received, scales):
                into = group * stride_of(lines) + start
                value = value + decode(ref[into : into + count, :], unit[:1])
            for row in range(0, count, 8):
                spread[pl.ds((start + row) * pad + group, 8, stride=pad), :] = value[row : row + 8]
    rest_x = cells // quads
    for line in range(steps * rest_x):
        base = line // rest_x * cells + line % rest_x
        for top in range(0, groups, 8):
            count = min(8, groups - top)
            tiles = [
                spread[(base + i * rest_x) * pad + top : (base + i * rest_x) * pad + top + 8, :] for i in range(quads)
            ]
            for j, tile in enumerate(swap_groups(tiles, depth)):
                turned[j * groups + top : j * groups + top + count, line * LANES : (line + 1) * LANES] = tile[:count]
    put_message(codes, turned)


def contract_second(depth, second, blocks, total, earlier, terms):
    rows, flat = terms.shape[1], total.shape[1]
    quads = LANES // depth
    ranks = second.shape[1]
    place = lax.axis_index("gy")
    inner = (place == 1) | (place == 2)
    width = 512 if flat % 512 == 0 else 256
    columns = []
    inside = lax.broadcasted_iota(jnp.int32, (ranks, rows), 1)
    inside = inside % (rows // quads) * quads + inside // (rows // quads)
    offset = lax.broadcasted_iota(jnp.int32, (ranks, rows), 0) - inside
    for at, (distance, *options) in enumerate(blocks):
        owner = jnp.bitwise_xor(place, distance)
        chosen = jnp.where(offset == owner * rows, 1.0, 0.0).astype(BF16)
        columns.append(dot(second[...], chosen).astype(BF16))
        unit = unit_of(options[0])[:1]
        if len(options) > 1:
            unit = jnp.where(inner, unit, unit_of(options[1])[:1])
        for low in range(0, flat, LANES):
            for start, count in pieces(rows):
                into = low // LANES * stride_of(rows) + start
                codes = options[0][into : into + count, :].astype(F32)
                if len(options) > 1:
                    codes = jnp.where(inner, codes, options[1][into : into + count, :].astype(F32))
                high, rest_of = split(decode(codes, unit))
                terms[2 * at, start : start + count, low : low + LANES] = high
                terms[2 * at + 1, start : start + count, low : low + LANES] = rest_of
    together = len(blocks) if rows % 16 == 0 else 1
    for low in range(0, flat, width):
        value = None if earlier is None else earlier[:, low : low + width]
        for at in range(0, len(blocks), together):
            left = jnp.concatenate([columns[k // 2] for k in range(2 * at, 2 * (at + together))], axis=1)
            right = [terms[k, :, low : low + width] for k in range(2 * at, 2 * (at + together))]
            if rows % 16 == 0:
                products = [dot(left, jnp.concatenate(right, axis=0))]
            else:
                products = [dot(columns[at], part) for part in right]
            for product in products:
                value = product if value is None else value + product
        total[:, low : low + width] = value


def early_kernel(depth, distances, second, *rest):
    blocks, (total, terms) = rest[:-2], rest[-2:]
    contract_second(depth, second, list(zip(distances, blocks)), total, None, terms)


def image_kernel(depth, steps, distance, second, depth_factor, waves, earlier, *rest):
    blocks, (image, terms, mixed, spread) = rest[:-4], rest[-4:]
    contract_second(depth, second, [(distance, *blocks)], mixed, earlier, terms)
    flat = mixed.shape[1]
    cells = image.shape[0]
    levels = depth_factor.shape[0]
    quads = LANES // depth
    groups = flat // LANES
    pad = spread.shape[0] // mixed.shape[0]
    for row in range(0, mixed.shape[0], 8):
        for group in range(groups):
            spread[pl.ds(row * pad + group, 8, stride=pad), :] = mixed[
                row : row + 8, group * LANES : (group + 1) * LANES
            ]
    square = jnp.concatenate([depth_factor[...].astype(F32)] * quads, axis=1)
    square = jnp.concatenate([square] * quads, axis=0)
    shape = square.shape
    same = lax.broadcasted_iota(jnp.int32, shape, 0) // levels == lax.broadcasted_iota(jnp.int32, shape, 1) // depth
    square = jnp.where(same, square, 0.0).astype(BF16)
    square = jnp.concatenate([square, square], axis=1)
    tiles = quads * levels // LANES
    contract = (((1,), (1,)), ((), ()))
    rest_x = cells // quads
    many = mixed.shape[0] // quads
    batch = 4 if many % 4 == 0 else 1
    for first in range(0, many, batch):
        stack = []
        for quad in range(first, first + batch):
            turned = [
                swap_groups(
                    [
                        spread[(quad * quads + j) * pad + top : (quad * quads + j) * pad + top + 8, :]
                        for j in range(quads)
                    ],
                    depth,
                )
                for top in range(0, pad, 8)
            ]
            stack += [piece[i] for i in range(quads) for piece in turned]
        high, rest_of = split(jnp.concatenate(stack, axis=0))
        source = lax.dot_general(
            jnp.concatenate([high, rest_of], axis=1), square, contract, preferred_element_type=F32
        )
        for quad in range(first, first + batch):
            base = (quad - first) * quads * pad
            for tile in range(tiles):
                at = quad * tiles + tile
                lanes = slice(tile * LANES, (tile + 1) * LANES)
                total = None
                for step in range(steps):
                    value = jnp.concatenate(
                        [
                            source[base + i * pad + step * rest_x : base + i * pad + (step + 1) * rest_x, lanes]
                            for i in range(quads)
                        ],
                        axis=0,
                    )
                    value = value * waves[at, step * cells : (step + 1) * cells, :]
                    total = value if total is None else total + value
                image[:, at * LANES : (at + 1) * LANES] = total


def lift_kernel(core, factor, core_near, factor_near):
    core_near[...] = core[...]
    factor_near[...] = factor[...]


def pack_kernel(pressure, previous, velocity, second, own, up, down, second_near):
    second_near[...] = second[...]
    cells, flat = pressure.shape
    span = up.shape[1] - LANES
    for row, part in ((0, pressure), (cells, previous)):
        codes, scale = encode(part[...])
        own[row : row + cells, :flat] = codes
        own[row : row + cells, flat:] = jnp.broadcast_to(scale, (cells, LANES)).astype(BF16)
    own[2 * cells :, :flat] = velocity[...]
    own[2 * cells :, flat:] = jnp.zeros((cells, LANES), BF16)
    up[:, :span] = own[:, flat - span : flat]
    down[:, :span] = own[:, :span]
    up[:, span:] = own[:, flat:]
    down[:, span:] = own[:, flat:]


def layout(cells, flat, near):
    widths = (flat, flat // 2, flat // 4, near, near // 2, LANES)
    starts = [sum(widths[:k]) for k in range(len(widths))]
    return [slice(start, start + width) for start, width in zip(starts, widths)]


def edge_kernel(own, low, high, ahead, behind):
    flat = own.shape[1] - LANES
    span = low.shape[1] - LANES
    near = span * 2 // 3
    cells = own.shape[0] // 3
    half, quarter = cells // 2, cells // 4
    places = layout(cells, flat, near)
    lane = lax.broadcasted_iota(jnp.int32, (cells, LANES), 1) // 16
    scales = jnp.zeros((cells, LANES), F32)
    for k, (part, row) in enumerate(((own, 0), (own, cells), (low, 0), (high, 0), (low, cells), (high, cells))):
        width = part.shape[1]
        scales = jnp.where(lane == k, part[row : row + cells, width - LANES :].astype(F32), scales)
    pressure = own[:cells, :flat].astype(F32)
    previous = own[cells : 2 * cells, :flat].astype(F32)
    speed = own[2 * cells :, :flat].astype(F32)
    below, above = low[:, span - near : span].astype(F32), high[:, :near].astype(F32)
    for ref, first, next_first in ((ahead, half, half - quarter), (behind, 0, half)):
        rows = slice(first, first + half)
        close = half if first > 0 else 0
        tight = slice(cells - quarter, cells) if first > 0 else slice(0, quarter)
        blocks = [
            [previous[rows], speed[rows]],
            [pressure[rows, : flat // 2], pressure[rows, flat // 2 :]],
            [pressure[next_first : next_first + quarter, k * (flat // 4) : (k + 1) * (flat // 4)] for k in range(4)],
            [below[close : close + half], above[close : close + half]],
            [
                below[cells + tight.start : cells + tight.stop, near // 2 :],
                above[cells + tight.start : cells + tight.stop, : near // 2],
                below[2 * cells + tight.start : 2 * cells + tight.stop, near // 2 :],
                above[2 * cells + tight.start : 2 * cells + tight.stop, : near // 2],
            ],
            [scales],
        ]
        for place, block in zip(places, blocks):
            ref[:, place] = jnp.concatenate(block, axis=0).astype(BF16)


def wave_kernel(levels, pressure, previous, velocity, left, right, low, high, waves, first, second, third, prior, speed):
    cells, flat = pressure.shape
    half = cells // 2
    span = low.shape[1] - LANES
    near = span * 2 // 3
    steps = waves.shape[1] // cells
    edge, inner, own_tiles = span // LANES, near // LANES, flat // LANES

    for tile in range(own_tiles):
        lane = tile * LANES
        first[edge + tile, cells : 2 * cells, :] = pressure[:, lane : lane + LANES]
        prior[inner + tile, half : half + cells, :] = previous[:, lane : lane + LANES]
        speed[inner + tile, half : half + cells, :] = velocity[:, lane : lane + LANES].astype(F32)
    for tile in range(2 * edge + own_tiles):
        if tile < edge or tile >= edge + own_tiles:
            first[tile, :cells, :] = jnp.zeros((cells, LANES), F32)
            first[tile, 2 * cells :, :] = jnp.zeros((cells, LANES), F32)
    for tile in range(2 * inner + own_tiles):
        if tile < inner or tile >= inner + own_tiles:
            for ref in (prior, speed):
                ref[tile, :half, :] = jnp.zeros((half, LANES), F32)
                ref[tile, half + cells :, :] = jnp.zeros((half, LANES), F32)
    quarter = cells // 4
    places = layout(cells, flat, near)
    for part, top, far, side, tight in (
        (left, cells - half, half - quarter, 0, half - quarter),
        (right, 2 * cells, 2 * cells + half, half + cells, half + cells),
    ):
        scales = part[:half, places[5]].astype(F32) * (1.0 / TOP)
        unit = [jnp.broadcast_to(scales[:, 16 * k : 16 * k + 1], (half, LANES)) for k in range(6)]

        def tile_of(place, tile):
            start = places[place].start + tile * LANES
            return part[:, start : start + LANES].astype(F32)

        for tile in range(own_tiles):
            both = tile_of(0, tile)
            prior[inner + tile, side : side + half, :] = decode(both[:half], unit[1])
            speed[inner + tile, side : side + half, :] = both[half:]
        for tile in range(own_tiles // 2):
            both = tile_of(1, tile)
            first[edge + tile, top : top + half, :] = decode(both[:half], unit[0])
            first[edge + own_tiles // 2 + tile, top : top + half, :] = decode(both[half:], unit[0])
        for tile in range(own_tiles // 4):
            both = decode(tile_of(2, tile), jnp.concatenate([unit[0]] * 2, axis=0))
            for k in range(4):
                into = edge + k * (own_tiles // 4) + tile
                first[into, far : far + quarter, :] = both[k * quarter : (k + 1) * quarter]
        for tile in range(inner):
            both = tile_of(3, tile)
            first[edge - inner + tile, top : top + half, :] = decode(both[:half], unit[2])
            first[edge + own_tiles + tile, top : top + half, :] = decode(both[half:], unit[3])
        for tile in range(inner // 2):
            both = tile_of(4, tile)
            ends = (inner // 2 + tile, inner + own_tiles + tile)
            values = decode(both[:half], jnp.concatenate([unit[4][:quarter], unit[5][:quarter]], axis=0))
            for k, end in enumerate(ends):
                rows = slice(k * quarter, (k + 1) * quarter)
                prior[end, tight : tight + quarter, :] = values[rows]
                speed[end, tight : tight + quarter, :] = both[half:][rows]
    for part, start, cut, begin in ((low, 0, edge - inner, 0), (high, edge + own_tiles, 0, inner + own_tiles)):
        unit = units(part, 0, 3 * cells, span)
        for tile in range(edge):
            lanes = slice(tile * LANES, (tile + 1) * LANES)
            first[start + tile, cells : 2 * cells, :] = decode(part[:cells, lanes], unit[:cells])
            if cut <= tile < cut + inner:
                prior[begin + tile - cut, half : half + cells, :] = decode(
                    part[cells : 2 * cells, lanes], unit[cells : 2 * cells]
                )
                speed[begin + tile - cut, half : half + cells, :] = part[2 * cells :, lanes].astype(F32)

    line = lax.broadcasted_iota(jnp.int32, (LANES, LANES), 0)
    column = lax.broadcasted_iota(jnp.int32, (LANES, LANES), 1)
    gap = jnp.abs(line - column)
    band = jnp.zeros((LANES, LANES), F32)
    for reach in range(5):
        band = jnp.where(gap == reach, STENCIL[reach] * (3.0 if reach == 0 else 1.0), band)
    band = jnp.where(line // levels == column // levels, band, 0.0)
    band_upper, band_lower = split(band)
    bands = jnp.concatenate([band_upper, band_upper, band_lower], axis=0)
    front = lax.broadcasted_iota(jnp.int32, (1, LANES), 1) < levels
    count = 4
    for tile in list(range(edge - inner)) + list(range(edge + own_tiles + inner, 2 * edge + own_tiles)):
        second[tile, :, :] = jnp.zeros((3 * cells, LANES), F32)

    def advance(now, before, shift, tile_shift, later, out_row, top, rows, tile):
        tiles = [now[tile + step, top : top + rows, :] for step in range(-2, count + 2)]
        rolled = [pltpu.roll(value, levels, 1) for value in tiles]
        tall = jnp.concatenate(tiles[2 : 2 + count], axis=0)
        upper, lower = split(tall)
        deep = dot(jnp.concatenate([upper, lower, upper], axis=1), bands)
        for step in range(count):
            at = step + 2
            total = deep[step * rows : (step + 1) * rows]
            sides = [
                jnp.where(front, rolled[at] + rolled[at - 1], rolled[at + 1] + rolled[at]),
                tiles[at + 1] + tiles[at - 1],
                jnp.where(front, rolled[at + 1] + rolled[at - 2], rolled[at + 2] + rolled[at - 1]),
                tiles[at + 2] + tiles[at - 2],
            ]
            for reach in range(1, 5):
                value = sides[reach - 1] + now[tile + step, top + reach : top + reach + rows, :]
                value = value + now[tile + step, top - reach : top - reach + rows, :]
                total = total + STENCIL[reach] * value
            rate = speed[tile + step - (edge - inner), top - half : top - half + rows, :]
            past = before[tile + step - tile_shift, top - shift : top - shift + rows, :]
            following = 2.0 * tiles[at] - past + rate * total
            if later is None:
                waves[tile + step - edge, out_row : out_row + rows, :] = following
            else:
                later[tile + step, top : top + rows, :] = following

    chain = [(first, prior, half, edge - inner, second), (second, first, 0, 0, third), (third, second, 0, 0, None)]
    for step in range(steps):
        now, before, shift, tile_shift, later = chain[step]
        top, rows = (cells - half, 2 * cells) if later is not None else (cells, cells)
        margin = (steps - 1 - step) * (edge // steps)

        for tile in range(edge - margin, edge + own_tiles + margin, count):
            advance(now, before, shift, tile_shift, later, step * cells, top, rows, tile)
        if later is not None:
            for tile in range(own_tiles):
                waves[tile, step * cells : (step + 1) * cells, :] = later[edge + tile, cells : 2 * cells, :]


def call(kernel, outs, scratch, flops, *args):
    moved = sum(arg.size * arg.dtype.itemsize for arg in args)
    moved += sum(out.size * jnp.dtype(out.dtype).itemsize for out in outs)
    return pl.pallas_call(
        kernel,
        out_shape=outs,
        scratch_shapes=scratch,
        cost_estimate=pl.CostEstimate(flops=flops, bytes_accessed=moved, transcendentals=0),
        compiler_params=pltpu.CompilerParams(vmem_limit_bytes=VMEM_BYTES),
    )(*args)


def shape_of(*shape, dtype=F32):
    return jax.ShapeDtypeStruct(shape, dtype)


def body(pressure, previous, velocity, tucker_core, first_factor, second_factor, depth_factor):
    cells, flat = pressure.shape
    levels, depth = depth_factor.shape
    steps, rank, core_flat = tucker_core.shape
    local_second = core_flat // depth
    lines = steps * cells
    count_x, count_y = lax.axis_size("gx"), lax.axis_size("gy")
    chips = count_x // 2
    span = 4 * steps * levels
    near = span * 2 // 3
    groups_pad = (core_flat // LANES + 7) // 8 * 8
    lines_pad = (lines * depth // LANES + 7) // 8 * 8

    across = [[(i, 2 * ((i // 2) ^ distance) + i % 2) for i in range(count_x)] for distance in range(1, chips)]
    factors = [lax.ppermute(first_factor, "gx", route) for route in across[::-1]]
    other = lax.ppermute(tucker_core, "gx", [(i, i + 1 - 2 * (i % 2)) for i in range(count_x)])
    core_near, factor_near = call(
        lift_kernel,
        [shape_of(*array.shape, dtype=BF16) for array in (tucker_core, first_factor)],
        [],
        1000,
        tucker_core,
        first_factor,
    )
    mine, *sends = call(
        functools.partial(project_kernel, chips),
        [shape_of(lines, core_flat)] + [message(lines, core_flat)] * (chips - 1),
        [pltpu.VMEM((chips - 1, lines, core_flat), F32)],
        4 * lines * chips * rank * core_flat,
        core_near,
        other,
        *factors,
        factor_near,
    )
    received = [lax.ppermute(send, "gx", route) for send, route in zip(sends, across)]
    pressure_later, _ = lax.optimization_barrier((pressure, mine))
    own, up, down, second_near = call(
        pack_kernel,
        [shape_of(3 * cells, flat + LANES, dtype=BF16)]
        + [shape_of(3 * cells, span + LANES, dtype=BF16)] * 2
        + [shape_of(*second_factor.shape, dtype=BF16)],
        [],
        10 * cells * flat,
        pressure_later,
        previous,
        velocity,
        second_factor,
    )
    low = lax.ppermute(up, "gy", [(i, i + 1) for i in range(count_y - 1)])
    high = lax.ppermute(down, "gy", [(i + 1, i) for i in range(count_y - 1)])

    (mine,) = call(presum_kernel, [shape_of(lines, core_flat)], [], 1000, mine, received.pop(0))
    mine, low, high = lax.optimization_barrier((mine, low, high))
    ahead, behind = call(
        edge_kernel,
        [shape_of(cells, layout(cells, flat, near)[-1].stop, dtype=BF16)] * 2,
        [],
        1000,
        own,
        low,
        high,
    )

    mine, ahead, behind = lax.optimization_barrier((mine, ahead, behind))
    (codes,) = call(
        functools.partial(gather_kernel, depth, steps),
        [message(local_second, lines * depth)],
        [pltpu.VMEM((lines * groups_pad, LANES), F32), pltpu.VMEM((local_second, lines * depth), F32)],
        30 * chips * lines * core_flat,
        mine,
        *received,
    )
    codes, ahead, behind = lax.optimization_barrier((codes, ahead, behind))

    def far(distance):
        return lax.ppermute(codes, "gy", [(i, i ^ distance) for i in range(count_y)])

    if count_y == 4:
        distances = (0, 2, 1)
        blocks = [codes, far(2), far(1)]
        place = lax.axis_index("gy")
        passed = jnp.where((place == 1) | (place == 2), blocks[1], blocks[2])
        last = [lax.ppermute(passed, "gy", [(0, 2), (3, 1), (1, 0), (2, 3)])]
    else:
        distances = tuple(range(count_y - 1))
        blocks = [codes] + [far(distance) for distance in distances[1:]]
        last = [far(count_y - 1)]

    left = lax.ppermute(ahead, "gx", [(i, i + 1) for i in range(count_x - 1)])
    right = lax.ppermute(behind, "gx", [(i + 1, i) for i in range(count_x - 1)])
    (waves,) = call(
        functools.partial(wave_kernel, levels),
        [shape_of(flat // LANES, lines, LANES)],
        [pltpu.VMEM(((flat + 2 * span) // LANES, 3 * cells, LANES), F32)] * 3
        + [pltpu.VMEM(((flat + 2 * near) // LANES, 2 * cells, LANES), F32)] * 2,
        150 * lines * flat,
        pressure,
        previous,
        velocity,
        left,
        right,
        low,
        high,
    )
    cells_y = second_factor.shape[0]
    (mixed,) = call(
        functools.partial(early_kernel, depth, distances),
        [shape_of(cells_y, lines * depth)],
        [pltpu.VMEM((2 * (count_y - 1), local_second, lines * depth), BF16)],
        4 * cells_y * count_y * local_second * lines * depth,
        second_near,
        *blocks,
    )
    (image,) = call(
        functools.partial(image_kernel, depth, steps, count_y - 1),
        [shape_of(cells, flat)],
        [
            pltpu.VMEM((2, local_second, lines * depth), BF16),
            pltpu.VMEM((cells_y, lines * depth), F32),
            pltpu.VMEM((cells_y * lines_pad, LANES), F32),
        ],
        4 * cells_y * local_second * lines * depth,
        second_near,
        depth_factor,
        waves,
        mixed,
        *last,
    )
    return image


def solution(mesh):
    placed = (
        P("gx", "gy"),
        P("gx", "gy"),
        P("gx", "gy"),
        P(None, "gx", "gy"),
        P("gx", None),
        P("gy", None),
        P(),
    )
    return jax.shard_map(body, mesh=mesh, in_specs=placed, out_specs=P("gx", "gy"), check_vma=False)
```
